128 devices in a mesh: gx: 8 (over y, core), gy: 16 (over z, x).
Axes of the slice: x: 4, y: 4, z: 4, core: 2. Of those that a mesh axis runs over, the one named last changes fastest.
Arguments:
- velocity: float32 [3, 128, 128, 128], P(None, 'gx', 'gy'), may hold values from -6 to 6
- offsets: float32 [3, 16384, 128], P(None, ('gx', 'gy')), may hold values from -1.5 to 1.5
- forces: float32 [3, 16384, 128], P(None, ('gx', 'gy')), may hold values from -24 to 24
- owner: int32 [16384], P(('gx', 'gy')), may hold values from 0 to 127, as said below
- base: int32 [3, 16384], P(None, ('gx', 'gy')), may hold values from 0 to 123, as said below
- counts: int32 [128], P(('gx', 'gy')), may hold values from 64 to 128, as said below
Outputs:
- new_velocity: float32 [3, 128, 128, 128], P(None, 'gx', 'gy')
- pressure: float32 [128, 128, 128], P('gx', 'gy')
- marker_velocity: float32 [3, 16384, 128], P(None, ('gx', 'gy'))
The draws below stay inside these ranges and needn't reach their ends.
Inputs may be any that keep to these rules, and one draw needn't show every extreme that they name: Owners are device indices of gx+gy, gx major. Among one device's slots no owner appears more than 2 times, and 32 owners appear exactly 2 times among the live slots of every device. Rows 0 and 1: the base cell within the owner's block along x (below 16) and y (below 8); row 2: the cell along z, from 3 to 123. `counts`: slots below a device's count are live, the others are ignored.
All inputs are finite; a program needn't handle non-finite values.
Results may differ from the reference program's by a relative error of at most 0.0003.
Values sent between devices are 32-bit elements; how exact they have to be, the bound alone decides.
A program may use at most 64 MiB of HBM per device.

```python
import jax
import jax.numpy as jnp
from jax import lax

CX = 16
CY = 8
NZ = 128
PATCH_DEV = 128
MARK = 128
JAC = 4
CAP = 2
HOT = 32
PATCHES = 16384
NX = 128
NY = 128
N_GY = 16
DEVICES = 128


def routing_table(key):
    shuffled = jax.random.permutation(jax.random.fold_in(key, 101), DEVICES).astype(jnp.int32)
    busiest = jnp.repeat(shuffled[:HOT], CAP)
    quieter = jnp.repeat(shuffled[HOT:], CAP)
    entries = quieter.shape[0]
    sender_keys = jax.random.split(jax.random.fold_in(key, 102), DEVICES)

    def one_sender(sender_key):
        score_key, first_key, second_key = jax.random.split(sender_key, 3)
        scores = jax.random.randint(score_key, (entries,), 0, 2 ** 16) * entries + jnp.arange(entries, dtype=jnp.int32)
        picked_scores, picks = lax.top_k(scores, PATCH_DEV - PATCH_DEV // 2)
        chosen = quieter[picks]
        leading = jax.random.permutation(first_key, busiest)
        trailing = jax.random.permutation(second_key, chosen)
        return jnp.concatenate([leading, trailing])
    owners = jax.vmap(one_sender)(sender_keys).reshape(-1).astype(jnp.int32)
    tallies = jax.random.randint(jax.random.fold_in(key, 103), (DEVICES,), PATCH_DEV // 2, PATCH_DEV + 1)
    extremes = jax.random.permutation(jax.random.fold_in(key, 104), DEVICES)[:2]
    tallies = tallies.at[extremes[0]].set(PATCH_DEV).at[extremes[1]].set(PATCH_DEV // 2)
    return (owners, tallies.astype(jnp.int32))


def draw_owner(key, part):
    owners, tallies = routing_table(key)
    return owners


def draw_counts(key, part):
    owners, tallies = routing_table(key)
    return tallies


def draw_base(key, part):
    key = jax.random.fold_in(key, 7)
    across_key, upward_key, inward_key, spot_key = jax.random.split(key, 4)
    across = jax.random.randint(across_key, (PATCHES,), 0, CX)
    upward = jax.random.randint(upward_key, (PATCHES,), 0, CY)
    inward = jax.random.randint(inward_key, (PATCHES,), 3, NZ - 4)
    spots = jax.random.permutation(spot_key, PATCHES)[:4]
    across = across.at[spots[0]].set(CX - 1).at[spots[1]].set(0)
    upward = upward.at[spots[2]].set(CY - 1)
    inward = inward.at[spots[3]].set(NZ - 5)
    return jnp.stack([across, upward, inward]).astype(jnp.int32)


def steps_of(rng, dims, cuts, smallest, top_value):
    gain, own = 1.0, jax.random.fold_in(rng, 6)
    for dim, blocks in cuts:
        heights = jnp.exp(jax.random.uniform(jax.random.fold_in(own, dim), (blocks,), jnp.float32, smallest / len(cuts), top_value / len(cuts)))
        gain = gain * jnp.repeat(heights, dims[dim] // blocks).reshape([-1 if axis == dim else 1 for axis in range(len(dims))])
    return gain


def scatter_about(key, extent, scale, most, cuts=(), held_as=jnp.bfloat16):
    array = jax.random.normal(key, extent, jnp.float32) * scale
    if len(cuts) > 0:
        array = steps_of(key, extent, cuts, -0.22, 0.18) * array
    return jnp.clip(array, min=-most, max=most).astype(held_as)


def setup_inputs(seed: int = 0) -> dict:
    key_of = jax.random.split(jax.random.key(seed), 7)
    return {
        "velocity": scatter_about(key_of[0], (3, NX, NY, NZ), 1.0, 6.0, ((1, 8), (2, 16)), jnp.float32),
        "offsets": jnp.clip(jax.random.uniform(key_of[1], (3, PATCHES, MARK), jnp.float32, -1.5, 1.5) * steps_of(key_of[1], (3, PATCHES, MARK), ((1, 128),), -0.4, 0.0), -1.5, 1.5),
        "forces": scatter_about(key_of[2], (3, PATCHES, MARK), 4.0, 24.0, ((1, 128),), jnp.float32),
        "owner": draw_owner(jax.random.fold_in(key_of[6], 71), 0),
        "base": draw_base(jax.random.fold_in(key_of[6], 71), 0),
        "counts": draw_counts(jax.random.fold_in(key_of[6], 71), 0),
    }


time_step = 0.5
viscosity = 0.1
highest = lax.Precision.HIGHEST

def kernel(distance):
    magnitude = jnp.abs(distance)
    inner_part = (3.0 - 2.0 * magnitude + jnp.sqrt(1.0 + 4.0 * magnitude - 4.0 * magnitude * magnitude)) / 8.0
    outer_part = (5.0 - 2.0 * magnitude - jnp.sqrt(-7.0 + 12.0 * magnitude - 4.0 * magnitude * magnitude)) / 8.0
    return jnp.where(magnitude < 1.0, inner_part, jnp.where(magnitude < 2.0, outer_part, 0.0))

def kernel_table(offsets):
    shifts = jnp.arange(8).astype(jnp.float32) - 3.0
    return kernel(offsets[:, :, None, :] - shifts[None, None, :, None])

def planes_of(weights):
    joined = weights[0][:, :, None, :] * weights[1][:, None, :, :]
    return joined.reshape(joined.shape[0], 64, joined.shape[3])

def spread(offsets, forces):
    weights = kernel_table(offsets)
    loaded = forces[:, :, None, :] * planes_of(weights)[None]
    box_values = jnp.einsum('cspm,skm->cskp', loaded, weights[2], precision=highest)
    return box_values.reshape(3, box_values.shape[1], 512)

def interpolate(offsets, box_values):
    weights = kernel_table(offsets)
    cubes = box_values.reshape(3, box_values.shape[1], 8, 64)
    contracted = jnp.einsum('cskp,skm->cspm', cubes, weights[2], precision=highest)
    return lax.optimization_barrier(jnp.sum(contracted * planes_of(weights)[None], axis=2))

def by_blocks(function, arrays, block_rows):
    length = arrays[0].shape[1]

    def handle(start):
        pieces = [lax.dynamic_slice_in_dim(member, start, block_rows, 1) for member in arrays]
        return function(*pieces)
    starts = jnp.arange(length // block_rows, dtype=jnp.int32) * block_rows
    stacked = lax.map(handle, starts)
    moved = jnp.moveaxis(stacked, 0, 1)
    return moved.reshape((moved.shape[0], length) + moved.shape[3:])

def deposit(box_values, flat_index, cell_count):
    values = box_values.reshape(3, -1)
    clipped = jnp.clip(flat_index.reshape(-1), 0, cell_count - 1)
    return jax.vmap(lambda column: jax.ops.segment_sum(column, clipped, num_segments=cell_count))(values)

def neighbour_sum(padded):
    return padded[..., 2:, 1:-1, 1:-1] + padded[..., :-2, 1:-1, 1:-1] + padded[..., 1:-1, 2:, 1:-1] + padded[..., 1:-1, :-2, 1:-1] + padded[..., 1:-1, 1:-1, 2:] + padded[..., 1:-1, 1:-1, :-2]

def divergence(padded):
    return (0.5 * (padded[0, 2:, 1:-1, 1:-1] - padded[0, :-2, 1:-1, 1:-1] + (padded[1, 1:-1, 2:, 1:-1] - padded[1, 1:-1, :-2, 1:-1]) + (padded[2, 1:-1, 1:-1, 2:] - padded[2, 1:-1, 1:-1, :-2])))[None]

def gradient(padded):
    return 0.5 * jnp.stack([padded[0, 2:, 1:-1, 1:-1] - padded[0, :-2, 1:-1, 1:-1], padded[0, 1:-1, 2:, 1:-1] - padded[0, 1:-1, :-2, 1:-1], padded[0, 1:-1, 1:-1, 2:] - padded[0, 1:-1, 1:-1, :-2]])

def surround(grid_field):
    widened = jnp.pad(grid_field, ((0, 0), (1, 1), (1, 1), (0, 0)), mode='wrap')
    return jnp.pad(widened, ((0, 0), (0, 0), (0, 0), (1, 1)))

def global_index(whole_base):
    ladder = jnp.arange(512, dtype=jnp.int32)
    depth_step = ladder // 64
    row_step = ladder // 8 % 8
    column_step = ladder % 8
    across = (whole_base[0][:, None] - 3 + row_step[None, :]) % NX
    upward = (whole_base[1][:, None] - 3 + column_step[None, :]) % NY
    inward = whole_base[2][:, None] - 3 + depth_step[None, :]
    return ((across * NY + upward) * NZ + inward).astype(jnp.int32)

def reference(velocity, offsets, forces, owner, base, counts):
    slot_ids = jnp.arange(PATCHES, dtype=jnp.int32)
    living = slot_ids % PATCH_DEV < counts[slot_ids // PATCH_DEV]
    whole_base = jnp.stack([owner // N_GY * CX + base[0], owner % N_GY * CY + base[1], base[2]]).astype(jnp.int32)
    flat_index = global_index(whole_base)
    masked = jnp.where(living[None, :, None], forces, 0.0)
    box_values = by_blocks(spread, (offsets, masked), 1024)
    force_field = deposit(box_values, flat_index, NX * NY * NZ).reshape(3, NX, NY, NZ)
    laplace = neighbour_sum(surround(velocity)) - 6.0 * velocity
    provisional = velocity + time_step * (viscosity * laplace + force_field)
    source = divergence(surround(provisional)) / time_step
    pressure = -source / 6.0
    for sweep in range(JAC - 1):
        pressure = (neighbour_sum(surround(pressure)) - source) / 6.0
    new_velocity = provisional - time_step * gradient(surround(pressure))
    flat_velocity = new_velocity.reshape(3, -1)

    def at_markers(offset_rows, index_rows):
        gathered = jnp.take(flat_velocity, index_rows[0].reshape(-1), axis=1, mode='clip')
        return interpolate(offset_rows, gathered.reshape(3, index_rows.shape[1], 512))
    marker_velocity = by_blocks(at_markers, (offsets, flat_index[None]), 1024)
    marker_velocity = jnp.where(living[None, :, None], marker_velocity, 0.0)
    return (new_velocity, pressure[0], marker_velocity)
```

```python
import functools
import jax, jax.numpy as jnp
from jax import lax
from jax.experimental import pallas as pl
from jax.experimental.pallas import tpu as pltpu
from jax.sharding import PartitionSpec as P

JAC = 4
time_step = 0.5
viscosity = 0.1

F32 = jnp.float32
BF = jnp.bfloat16

def split(v):
    hi = v.astype(BF)
    lo = (v - hi.astype(F32)).astype(BF)
    return hi, lo

def fill_tables(r_ref, fl, a1, a2, q8, sources):
    def body(b, carry):
        t = r_ref[pl.ds(b * 8, 8), 0:8, :].reshape(64, 128)
        whole = jnp.floor(t)
        f = t - whole
        rows = pl.ds(pl.multiple_of(b * 64, 64), 64)
        fl[rows, :] = whole
        a1[rows, :] = (3.0 - 2.0 * f) * 0.125
        a2[rows, :] = (1.0 + 2.0 * f) * 0.125
        q8[rows, :] = jnp.sqrt(1.0 + 4.0 * f * (1.0 - f)) * 0.125
        return carry
    lax.fori_loop(0, sources // 8, body, 0)

def weight(cells, row, tabs):
    fl, a1, a2, q8 = [t[pl.ds(row, 1), :] for t in tabs]
    e = cells - fl
    s = jnp.where(e < 0.5, a1, a2)
    g = e * (e - 1.0)
    return jnp.where(g < 1.0, s + q8, jnp.where(g < 3.0, s - q8, 0.0))

def plane(base_s, p, row, tabs, wxs, iota8, iota16):
    wx = weight(iota8, row, tabs)
    y0 = base_s[p * 3 + 1].astype(F32)
    wy = weight(iota16 - y0, row + 1, tabs)
    wxs[...] = wx
    return jnp.concatenate([wxs[pl.ds(i, 1), :] * wy for i in range(8)], axis=0)

def spread_body(unroll, base_s, r_ref, out, fl, a1, a2, q8, acc, wxs, tot):
    sources = r_ref.shape[0]
    tabs = (fl, a1, a2, q8)
    def zero(x, carry):
        acc[x] = jnp.zeros((3, 128, 128), F32)
        return carry
    lax.fori_loop(0, 16, zero, 0)
    fill_tables(r_ref, *tabs, sources)
    iota8 = lax.broadcasted_iota(jnp.int32, (8, 128), 0).astype(F32) - 3.0
    iota16 = lax.broadcasted_iota(jnp.int32, (16, 128), 0).astype(F32) - 3.0
    def body(t, carry):
        res = []
        for u in range(unroll):
            s = t * unroll + u
            for r in range(2):
                p = s * 2 + r
                row = s * 8 + r * 3
                B = plane(base_s, p, row, tabs, wxs.at[u * 2 + r], iota8, iota16)
                wz = weight(iota8, row + 2, tabs)
                A = jnp.concatenate([r_ref[s, pl.ds(8 + r * 3 + c, 1), :] * wz for c in range(3)], axis=0)
                ah, al = split(A)
                bh, bl = split(B)
                o = lax.dot_general(jnp.concatenate([ah, al], 0), jnp.concatenate([bh, bl], 0), (((1,), (1,)), ((), ())), preferred_element_type=F32)
                res.append((p, o[:24, :128] + o[24:, :128] + o[:24, 128:]))
        for p, o in res:
            x0 = base_s[p * 3]
            z0 = jnp.maximum(base_s[p * 3 + 2] - 3, 0)
            for c in range(3):
                acc[x0, c, pl.ds(z0, 8), :] += o[c * 8:c * 8 + 8]
        return carry
    lax.fori_loop(0, sources // unroll, body, 0)
    lane = lax.broadcasted_iota(jnp.int32, (128, 128), 1)
    for c in range(3):
        tiles = [None] * 3
        for t in range(2):
            for r in range(8):
                a = acc[8 * t + r, c]
                if r == 0:
                    parts = [(t, a)]
                else:
                    a = pltpu.roll(a, 16 * r, 1)
                    parts = [(t, jnp.where(lane >= 16 * r, a, 0.0)), (t + 1, jnp.where(lane < 16 * r, a, 0.0))]
                for k, v in parts:
                    if tiles[k] is None:
                        tot[k] = v
                        tiles[k] = 1
                    else:
                        tot[k] += v
        for k in range(3):
            out[c, 8 * k:8 * k + 8] = tot[k].T.reshape(8, 16, 128)

def spread_call(base, R, unroll=2, vmem=48*2**20):
    n = R.shape[0]
    return pl.pallas_call(
        functools.partial(spread_body, unroll),
        out_shape=jax.ShapeDtypeStruct((3, 24, 16, 128), F32),
        in_specs=[pl.BlockSpec(memory_space=pltpu.SMEM), pl.BlockSpec(memory_space=pltpu.VMEM)],
        out_specs=pl.BlockSpec(memory_space=pltpu.VMEM),
        scratch_shapes=[pltpu.VMEM((n * 8, 128), F32)] * 4 + [pltpu.VMEM((16, 3, 128, 128), F32), pltpu.VMEM((2 * unroll, 8, 128), F32), pltpu.VMEM((3, 128, 128), F32)],
        compiler_params=pltpu.CompilerParams(vmem_limit_bytes=vmem),
        name="spread",
    )(base, R)

def interp_body(unroll, base_s, r_ref, v_ref, out, fl, a1, a2, q8, cop, wxs):
    sources = r_ref.shape[0]
    tabs = (fl, a1, a2, q8)
    fill_tables(r_ref, *tabs, sources)
    lane = lax.broadcasted_iota(jnp.int32, (128, 128), 1)
    for c in range(3):
        tiles = [v_ref[c, 8 * k:8 * k + 8].reshape(128, 128).T for k in range(3)]
        for r in range(8):
            if r == 0:
                cop[0, c], cop[8, c] = tiles[0], tiles[1]
            else:
                ro = [pltpu.roll(x, 128 - 16 * r, 1) for x in tiles]
                for t in range(2):
                    cop[8 * t + r, c] = jnp.where(lane < 128 - 16 * r, ro[t], ro[t + 1])
    iota8 = lax.broadcasted_iota(jnp.int32, (8, 128), 0).astype(F32) - 3.0
    iota16 = lax.broadcasted_iota(jnp.int32, (16, 128), 0).astype(F32) - 3.0
    def body(t, carry):
        for u in range(unroll):
            s = t * unroll + u
            for r in range(2):
                p = s * 2 + r
                row = s * 8 + r * 3
                B = plane(base_s, p, row, tabs, wxs.at[u * 2 + r], iota8, iota16)
                wz = weight(iota8, row + 2, tabs)
                x0 = base_s[p * 3]
                z0 = jnp.maximum(base_s[p * 3 + 2] - 3, 0)
                A = jnp.concatenate([cop[x0, c, pl.ds(z0, 8), :] for c in range(3)], axis=0)
                ah, al = split(A)
                bh, bl = split(B)
                o = jnp.dot(jnp.concatenate([ah, al], 0), jnp.concatenate([bh, bl], 1), preferred_element_type=F32)
                o = o[:24, :128] + o[24:, :128] + o[:24, 128:]
                for c in range(3):
                    out[s, pl.ds(r * 3 + c, 1), :] = jnp.sum(o[8 * c:8 * c + 8] * wz, axis=0, keepdims=True)
        return carry
    lax.fori_loop(0, sources // unroll, body, 0)

def interp_call(base, R, V, unroll=2, vmem=48*2**20):
    n = R.shape[0]
    return pl.pallas_call(
        functools.partial(interp_body, unroll),
        out_shape=jax.ShapeDtypeStruct((n, 8, 128), F32),
        in_specs=[pl.BlockSpec(memory_space=pltpu.SMEM), pl.BlockSpec(memory_space=pltpu.VMEM), pl.BlockSpec(memory_space=pltpu.VMEM)],
        out_specs=pl.BlockSpec(memory_space=pltpu.VMEM),
        scratch_shapes=[pltpu.VMEM((n * 8, 128), F32)] * 4 + [pltpu.VMEM((16, 3, 128, 128), F32), pltpu.VMEM((2 * unroll, 8, 128), F32)],
        compiler_params=pltpu.CompilerParams(vmem_limit_bytes=vmem),
        name="interp",
    )(base, R, V)


def split3(v):
    hi = v.astype(BF)
    rest = v - hi.astype(F32)
    mid = rest.astype(BF)
    return hi, mid, (rest - mid.astype(F32)).astype(BF)


def routes(owner_row, count):
    rows = lax.broadcasted_iota(jnp.int32, (128, 128), 0)
    slots = lax.broadcasted_iota(jnp.int32, (128, 128), 1)
    match = jnp.where((owner_row == rows) & (slots < count), 1.0, 0.0)
    before = jnp.where(rows < slots, 1.0, 0.0)
    rank = jnp.dot(match.astype(BF), before.astype(BF), preferred_element_type=F32)
    return jnp.where(rank < 0.5, match, 0.0), jnp.where(rank < 0.5, 0.0, match)


def spread_rows(stage, row, values):
    for d in range(0, 128, 8):
        stage[pl.ds(d * 16 + row, 8, stride=16), :] = values[d:d + 8]


def pack_rows(first, second, off_ref, frc_ref, base_ref, stage):
    both = jnp.concatenate([first, second], axis=0).astype(BF)
    for q in range(6):
        data = off_ref[q] if q < 3 else frc_ref[q - 3]
        parts = jnp.concatenate(split3(data), axis=1)
        got = jnp.dot(both, parts, preferred_element_type=F32)
        got = got[:, :128] + (got[:, 128:256] + got[:, 256:])
        for r in range(2):
            spread_rows(stage, (q // 3) * 8 + r * 3 + q % 3, got[r * 128:r * 128 + 128])
    rows = base_ref[...].astype(F32)
    none = jnp.zeros((122, 128), F32)
    blank = jnp.zeros((3, 128), F32)
    dims = (((1,), (1,)), ((), ()))
    one = jnp.concatenate([rows, blank, none], axis=0).astype(BF)
    two = jnp.concatenate([blank, rows, none], axis=0).astype(BF)
    corner = lax.dot_general(both[:128], one, dims, preferred_element_type=F32)
    corner += lax.dot_general(both[128:], two, dims, preferred_element_type=F32)
    spread_rows(stage, 6, corner)
    for row in (7, 14, 15):
        spread_rows(stage, row, jnp.zeros((128, 128), F32))


def pack_body(count_s, owner_ref, off_ref, frc_ref, base_ref, stage, back):
    first, second = routes(owner_ref[...], count_s[0])
    back[:, :128] = first.T
    back[:, 128:] = second.T
    pack_rows(first, second, off_ref, frc_ref, base_ref, stage)


def unpack_body(back, ret_ref, out):
    pick = back[...].astype(BF)
    for c in range(3):
        data = jnp.concatenate([ret_ref[pl.ds(r * 3 + c, 128, stride=8), :] for r in range(2)], axis=0)
        got = jnp.dot(pick, jnp.concatenate(split3(data), axis=1), preferred_element_type=F32)
        out[c] = got[:, :128] + (got[:, 128:256] + got[:, 256:])


VM = pl.BlockSpec(memory_space=pltpu.VMEM)
SM = pl.BlockSpec(memory_space=pltpu.SMEM)


def with_halo(block, sides, width):
    for axis, dim in sides:
        count = lax.axis_size(axis)
        forward = [(i, i + 1) for i in range(count - 1)]
        forward.append((count - 1, 0))
        backward = [(target, source) for source, target in forward]
        low = lax.ppermute(
            lax.slice_in_dim(block, block.shape[dim] - width, None, axis=dim), axis, forward
        )
        high = lax.ppermute(lax.slice_in_dim(block, 0, width, axis=dim), axis, backward)
        block = jnp.concatenate([low, block, high], axis=dim)
    return block


def neighbour_sum(padded):
    return (
        padded[..., 2:, 1:-1, 1:-1]
        + padded[..., :-2, 1:-1, 1:-1]
        + padded[..., 1:-1, 2:, 1:-1]
        + padded[..., 1:-1, :-2, 1:-1]
        + padded[..., 1:-1, 1:-1, 2:]
        + padded[..., 1:-1, 1:-1, :-2]
    )


def divergence(padded):
    return (
        0.5
        * (
            padded[0, 2:, 1:-1, 1:-1]
            - padded[0, :-2, 1:-1, 1:-1]
            + (padded[1, 1:-1, 2:, 1:-1] - padded[1, 1:-1, :-2, 1:-1])
            + (padded[2, 1:-1, 1:-1, 2:] - padded[2, 1:-1, 1:-1, :-2])
        )
    )[None]


def gradient(padded):
    return 0.5 * jnp.stack(
        [
            padded[0, 2:, 1:-1, 1:-1] - padded[0, :-2, 1:-1, 1:-1],
            padded[0, 1:-1, 2:, 1:-1] - padded[0, 1:-1, :-2, 1:-1],
            padded[0, 1:-1, 1:-1, 2:] - padded[0, 1:-1, 1:-1, :-2],
        ]
    )


def pad_depth(grid_field):
    return jnp.pad(grid_field, ((0, 0), (0, 0), (0, 0), (1, 1)))


def extend(grid_field):
    widened = with_halo(grid_field, (("gx", 1), ("gy", 2)), 1)
    return pad_depth(widened)


def grow_rims(grid_field):
    return with_halo(grid_field, (("gx", 1), ("gy", 2)), 3)


def fold_rims(widened, axis_dim, length):
    middle = lax.slice_in_dim(widened, 6, 6 + length, axis=axis_dim)
    lower_rim = lax.slice_in_dim(widened, 0, 3, axis=axis_dim)
    upper_rim = lax.slice_in_dim(widened, length + 9, length + 12, axis=axis_dim)
    low_pad = [(0, 0)] * widened.ndim
    low_pad[axis_dim] = (0, length - 3)
    high_pad = [(0, 0)] * widened.ndim
    high_pad[axis_dim] = (length - 3, 0)
    return middle + jnp.pad(lower_rim, low_pad) + jnp.pad(upper_rim, high_pad)


def shards(velocity, offsets, forces, owner, base, counts):
    width_x = velocity.shape[1]
    width_y = velocity.shape[2]
    axes = ("gx", "gy")
    stage, back = pl.pallas_call(
        pack_body,
        out_shape=(jax.ShapeDtypeStruct((2048, 128), F32), jax.ShapeDtypeStruct((128, 256), F32)),
        in_specs=[SM, VM, VM, VM, VM],
        out_specs=(VM, VM),
        compiler_params=pltpu.CompilerParams(vmem_limit_bytes=32 * 2**20),
        name="pack",
    )(counts, owner.reshape(1, 128), offsets, forces, base)
    arrived = lax.all_to_all(stage.reshape(128, 16, 128), axes, split_axis=0, concat_axis=0, tiled=True)
    corners = arrived[:, 6, :6].astype(jnp.int32).reshape(-1)
    spread_grid = spread_call(corners, arrived, 4)
    widened = grow_rims(spread_grid[:, : width_x + 6, : width_y + 6])
    force_field = fold_rims(fold_rims(widened, 1, width_x), 2, width_y)
    laplace = neighbour_sum(extend(velocity)) - 6.0 * velocity
    provisional = velocity + time_step * (viscosity * laplace + force_field)
    source = divergence(extend(provisional)) / time_step
    pressure = -source / 6.0
    for sweep in range(JAC - 1):
        pressure = (neighbour_sum(extend(pressure)) - source) / 6.0
    new_velocity = provisional - time_step * gradient(extend(pressure))
    sampled = jnp.pad(grow_rims(new_velocity), ((0, 0), (0, 2), (0, 2), (0, 0)))
    answers = interp_call(corners, arrived, sampled, 4)
    returned = lax.all_to_all(answers, axes, split_axis=0, concat_axis=0, tiled=True)
    marker_velocity = pl.pallas_call(
        unpack_body,
        out_shape=jax.ShapeDtypeStruct((3, 128, 128), F32),
        in_specs=[VM, VM],
        out_specs=VM,
        compiler_params=pltpu.CompilerParams(vmem_limit_bytes=32 * 2**20),
        name="unpack",
    )(back, returned.reshape(1024, 128))
    return (new_velocity, pressure[0], marker_velocity)


def solution(mesh):
    return jax.shard_map(
        shards,
        mesh=mesh,
        in_specs=(
            P(None, "gx", "gy", None),
            P(None, ("gx", "gy"), None),
            P(None, ("gx", "gy"), None),
            P(("gx", "gy")),
            P(None, ("gx", "gy")),
            P(("gx", "gy")),
        ),
        out_specs=(P(None, "gx", "gy", None), P("gx", "gy", None), P(None, ("gx", "gy"), None)),
        check_vma=False,
    )
```

```python
import functools
import jax, jax.numpy as jnp
from jax import lax
from jax.experimental import pallas as pl
from jax.experimental.pallas import tpu as pltpu
from jax.sharding import PartitionSpec as P

time_step = 0.5
viscosity = 0.1

F32 = jnp.float32
BF = jnp.bfloat16

def split(v):
    hi = v.astype(BF)
    lo = (v - hi.astype(F32)).astype(BF)
    return hi, lo

def fill_tables(r_ref, fl, a1, a2, q8, sources):
    def body(b, carry):
        t = r_ref[pl.ds(b * 8, 8), 0:8, :].reshape(64, 128)
        whole = jnp.floor(t)
        f = t - whole
        rows = pl.ds(pl.multiple_of(b * 64, 64), 64)
        fl[rows, :] = whole
        a1[rows, :] = (3.0 - 2.0 * f) * 0.125
        a2[rows, :] = (1.0 + 2.0 * f) * 0.125
        q8[rows, :] = jnp.sqrt(1.0 + 4.0 * f * (1.0 - f)) * 0.125
        return carry
    lax.fori_loop(0, sources // 8, body, 0)

def weight(cells, row, tabs):
    fl, a1, a2, q8 = [t[pl.ds(row, 1), :] for t in tabs]
    e = cells - fl
    s = jnp.where(e < 0.5, a1, a2)
    g = e * (e - 1.0)
    return jnp.where(g < 1.0, s + q8, jnp.where(g < 3.0, s - q8, 0.0))

def plane(base_s, p, row, tabs, wxs, iota8, iota16):
    wx = weight(iota8, row, tabs)
    y0 = base_s[p * 3 + 1].astype(F32)
    wy = weight(iota16 - y0, row + 1, tabs)
    wxs[...] = wx
    return jnp.concatenate([wxs[pl.ds(i, 1), :] * wy for i in range(8)], axis=0)

def spread_body(unroll, base_s, r_ref, out, fl, a1, a2, q8, acc, wxs, tot):
    sources = r_ref.shape[0]
    tabs = (fl, a1, a2, q8)
    def zero(x, carry):
        acc[x] = jnp.zeros((3, 128, 128), F32)
        return carry
    lax.fori_loop(0, 16, zero, 0)
    fill_tables(r_ref, *tabs, sources)
    iota8 = lax.broadcasted_iota(jnp.int32, (8, 128), 0).astype(F32) - 3.0
    iota16 = lax.broadcasted_iota(jnp.int32, (16, 128), 0).astype(F32) - 3.0
    def body(t, carry):
        res = []
        for u in range(unroll):
            s = t * unroll + u
            for r in range(2):
                p = s * 2 + r
                row = s * 8 + r * 3
                B = plane(base_s, p, row, tabs, wxs.at[u * 2 + r], iota8, iota16)
                wz = weight(iota8, row + 2, tabs)
                A = jnp.concatenate([r_ref[s, pl.ds(8 + r * 3 + c, 1), :] * wz for c in range(3)], axis=0)
                ah, al = split(A)
                bh, bl = split(B)
                o = lax.dot_general(jnp.concatenate([ah, al], 0), jnp.concatenate([bh, bl], 0), (((1,), (1,)), ((), ())), preferred_element_type=F32)
                res.append((p, o[:24, :128] + o[24:, :128] + o[:24, 128:]))
        for p, o in res:
            x0 = base_s[p * 3]
            z0 = jnp.maximum(base_s[p * 3 + 2] - 3, 0)
            for c in range(3):
                acc[x0, c, pl.ds(z0, 8), :] += o[c * 8:c * 8 + 8]
        return carry
    lax.fori_loop(0, sources // unroll, body, 0)
    lane = lax.broadcasted_iota(jnp.int32, (128, 128), 1)
    for c in range(3):
        tiles = [None] * 3
        for t in range(2):
            for r in range(8):
                a = acc[8 * t + r, c]
                if r == 0:
                    parts = [(t, a)]
                else:
                    a = pltpu.roll(a, 16 * r, 1)
                    parts = [(t, jnp.where(lane >= 16 * r, a, 0.0)), (t + 1, jnp.where(lane < 16 * r, a, 0.0))]
                for k, v in parts:
                    if tiles[k] is None:
                        tot[k] = v
                        tiles[k] = 1
                    else:
                        tot[k] += v
        for k in range(3):
            out[c, 8 * k:8 * k + 8] = tot[k].T.reshape(8, 16, 128)

def spread_call(base, R, unroll=2, vmem=48*2**20):
    n = R.shape[0]
    return pl.pallas_call(
        functools.partial(spread_body, unroll),
        out_shape=jax.ShapeDtypeStruct((3, 24, 16, 128), F32),
        in_specs=[pl.BlockSpec(memory_space=pltpu.SMEM), pl.BlockSpec(memory_space=pltpu.VMEM)],
        out_specs=pl.BlockSpec(memory_space=pltpu.VMEM),
        scratch_shapes=[pltpu.VMEM((n * 8, 128), F32)] * 4 + [pltpu.VMEM((16, 3, 128, 128), F32), pltpu.VMEM((2 * unroll, 8, 128), F32), pltpu.VMEM((3, 128, 128), F32)],
        compiler_params=pltpu.CompilerParams(vmem_limit_bytes=vmem),
        name="spread",
    )(base, R)

def interp_body(unroll, base_s, r_ref, v_ref, out, fl, a1, a2, q8, cop, wxs):
    sources = r_ref.shape[0]
    tabs = (fl, a1, a2, q8)
    fill_tables(r_ref, *tabs, sources)
    lane = lax.broadcasted_iota(jnp.int32, (128, 128), 1)
    for c in range(3):
        tiles = [v_ref[c, 8 * k:8 * k + 8].reshape(128, 128).T for k in range(3)]
        for r in range(8):
            if r == 0:
                cop[0, c], cop[8, c] = tiles[0], tiles[1]
            else:
                ro = [pltpu.roll(x, 128 - 16 * r, 1) for x in tiles]
                for t in range(2):
                    cop[8 * t + r, c] = jnp.where(lane < 128 - 16 * r, ro[t], ro[t + 1])
    iota8 = lax.broadcasted_iota(jnp.int32, (8, 128), 0).astype(F32) - 3.0
    iota16 = lax.broadcasted_iota(jnp.int32, (16, 128), 0).astype(F32) - 3.0
    def body(t, carry):
        for u in range(unroll):
            s = t * unroll + u
            for r in range(2):
                p = s * 2 + r
                row = s * 8 + r * 3
                B = plane(base_s, p, row, tabs, wxs.at[u * 2 + r], iota8, iota16)
                wz = weight(iota8, row + 2, tabs)
                x0 = base_s[p * 3]
                z0 = jnp.maximum(base_s[p * 3 + 2] - 3, 0)
                A = jnp.concatenate([cop[x0, c, pl.ds(z0, 8), :] for c in range(3)], axis=0)
                ah, al = split(A)
                bh, bl = split(B)
                o = jnp.dot(jnp.concatenate([ah, al], 0), jnp.concatenate([bh, bl], 1), preferred_element_type=F32)
                o = o[:24, :128] + o[24:, :128] + o[:24, 128:]
                for c in range(3):
                    out[s, pl.ds(r * 3 + c, 1), :] = jnp.sum(o[8 * c:8 * c + 8] * wz, axis=0, keepdims=True)
        return carry
    lax.fori_loop(0, sources // unroll, body, 0)

def interp_call(base, R, V, unroll=2, vmem=48*2**20):
    n = R.shape[0]
    return pl.pallas_call(
        functools.partial(interp_body, unroll),
        out_shape=jax.ShapeDtypeStruct((n, 8, 128), F32),
        in_specs=[pl.BlockSpec(memory_space=pltpu.SMEM), pl.BlockSpec(memory_space=pltpu.VMEM), pl.BlockSpec(memory_space=pltpu.VMEM)],
        out_specs=pl.BlockSpec(memory_space=pltpu.VMEM),
        scratch_shapes=[pltpu.VMEM((n * 8, 128), F32)] * 4 + [pltpu.VMEM((16, 3, 128, 128), F32), pltpu.VMEM((2 * unroll, 8, 128), F32)],
        compiler_params=pltpu.CompilerParams(vmem_limit_bytes=vmem),
        name="interp",
    )(base, R, V)


def split3(v):
    hi = v.astype(BF)
    rest = v - hi.astype(F32)
    mid = rest.astype(BF)
    return hi, mid, (rest - mid.astype(F32)).astype(BF)


def routes(owner_row, count):
    rows = lax.broadcasted_iota(jnp.int32, (128, 128), 0)
    slots = lax.broadcasted_iota(jnp.int32, (128, 128), 1)
    match = jnp.where((owner_row == rows) & (slots < count), 1.0, 0.0)
    before = jnp.where(rows < slots, 1.0, 0.0)
    rank = jnp.dot(match.astype(BF), before.astype(BF), preferred_element_type=F32)
    return jnp.where(rank < 0.5, match, 0.0), jnp.where(rank < 0.5, 0.0, match)


def spread_rows(stage, row, values):
    for d in range(0, 128, 8):
        stage[pl.ds(d * 16 + row, 8, stride=16), :] = values[d:d + 8]


def pack_rows(first, second, off_ref, frc_ref, base_ref, stage):
    both = jnp.concatenate([first, second], axis=0).astype(BF)
    for q in range(6):
        data = off_ref[q] if q < 3 else frc_ref[q - 3]
        parts = jnp.concatenate(split3(data), axis=1)
        got = jnp.dot(both, parts, preferred_element_type=F32)
        got = got[:, :128] + (got[:, 128:256] + got[:, 256:])
        for r in range(2):
            spread_rows(stage, (q // 3) * 8 + r * 3 + q % 3, got[r * 128:r * 128 + 128])
    rows = base_ref[...].astype(F32)
    none = jnp.zeros((122, 128), F32)
    blank = jnp.zeros((3, 128), F32)
    dims = (((1,), (1,)), ((), ()))
    one = jnp.concatenate([rows, blank, none], axis=0).astype(BF)
    two = jnp.concatenate([blank, rows, none], axis=0).astype(BF)
    corner = lax.dot_general(both[:128], one, dims, preferred_element_type=F32)
    corner += lax.dot_general(both[128:], two, dims, preferred_element_type=F32)
    spread_rows(stage, 6, corner)
    for row in (7, 14, 15):
        spread_rows(stage, row, jnp.zeros((128, 128), F32))


def pack_body(count_s, owner_ref, off_ref, frc_ref, base_ref, stage, back):
    first, second = routes(owner_ref[...], count_s[0])
    back[:, :128] = first.T
    back[:, 128:] = second.T
    pack_rows(first, second, off_ref, frc_ref, base_ref, stage)


def unpack_body(back, ret_ref, out):
    pick = back[...].astype(BF)
    for c in range(3):
        data = jnp.concatenate([ret_ref[pl.ds(r * 3 + c, 128, stride=8), :] for r in range(2)], axis=0)
        got = jnp.dot(pick, jnp.concatenate(split3(data), axis=1), preferred_element_type=F32)
        out[c] = got[:, :128] + (got[:, 128:256] + got[:, 256:])


VM = pl.BlockSpec(memory_space=pltpu.VMEM)
SM = pl.BlockSpec(memory_space=pltpu.SMEM)


MESH = pl.DeviceIdType.MESH
SIDES = ((1, 0), (-1, 0), (0, 1), (0, -1), (1, 1), (1, -1), (-1, 1), (-1, -1))


def neighbours():
    gx, gy = lax.axis_index("gx"), lax.axis_index("gy")
    nx, ny = lax.axis_size("gx"), lax.axis_size("gy")
    return [(lax.rem(gx + dx + nx, nx), lax.rem(gy + dy + ny, ny)) for dx, dy in SIDES]


def near(step, size, width):
    return (0, size) if step == 0 else ((size - width, width) if step > 0 else (0, width))


def there(step, size, width):
    return (0, size) if step == 0 else ((-width, width) if step > 0 else (size, width))


def inward(lane, v):
    above = jnp.where(lane == 127, 0.0, pltpu.roll(v, 127, 1))
    below = jnp.where(lane == 0, 0.0, pltpu.roll(v, 1, 1))
    return above, below


def fluid_body(w_ref, vel_ref, new_ref, prs_ref, v_ref, ve, pe, src, pa, pb, fold, send, recv):
    peers = neighbours()
    barrier = pltpu.get_barrier_semaphore()
    fold[...] = jnp.zeros(fold.shape, F32)
    for peer in peers:
        pl.semaphore_signal(barrier, inc=1, device_id=peer, device_id_type=MESH)
    ve[:, 1:17, 8:16, :] = vel_ref[...]
    pl.semaphore_wait(barrier, 8)
    started = []

    def push(source, target, k):
        n = len(started)
        copy = pltpu.make_async_remote_copy(source, target, send.at[n], recv.at[n], device_id=peers[k], device_id_type=MESH)
        copy.start()
        started.append(copy)
        return copy

    def box(ref, xs, ys, x_at, y_at):
        return ref.at[..., pl.ds(xs[0] + x_at, xs[1]), pl.ds(ys[0] + y_at, ys[1]), :]

    first = []
    for k, (dx, dy) in enumerate(SIDES):
        xs = (3, 16) if dx == 0 else ((19, 3) if dx > 0 else (0, 3))
        ys = (3, 8) if dy == 0 else ((11, 3) if dy > 0 else (0, 3))
        xd = (0, 16) if dx == 0 else ((0, 3) if dx > 0 else (13, 3))
        yd = (0, 8) if dy == 0 else ((0, 3) if dy > 0 else (5, 3))
        layer = 0 if dy == 0 else (1 if dx == 0 else 2)
        first.append(push(w_ref.at[:, pl.ds(xs[0], xs[1]), pl.ds(ys[0], ys[1]), :],
                          fold.at[layer, :, pl.ds(xd[0], xd[1]), pl.ds(yd[0], yd[1]), :], k))
        if k < 4:
            first.append(push(box(vel_ref, near(dx, 16, 1), near(dy, 8, 1), 0, 0),
                              box(ve, there(dx, 16, 1), there(dy, 8, 1), 1, 8), k))
    for copy in first:
        copy.wait_recv()
    lane = lax.broadcasted_iota(jnp.int32, (8, 128), 1)

    def provide(x, carry):
        for c in range(3):
            v = ve[c, x + 1, 8:16, :]
            above, below = inward(lane, v)
            lap = (ve[c, x + 2, 8:16, :] + ve[c, x, 8:16, :]) + (ve[c, x + 1, 9:17, :] + ve[c, x + 1, 7:15, :]) + (above + below) - 6.0 * v
            force = w_ref[c, x + 3, 3:11, :] + fold[0, c, x] + fold[1, c, x] + fold[2, c, x]
            pe[c, x + 8, 8:16, :] = v + time_step * (viscosity * lap + force)
        return carry

    lax.fori_loop(0, 16, provide, 0, unroll=4)

    second = [push(box(pe, near(dx, 16, 1), near(dy, 8, 1), 8, 8),
                   box(pe, there(dx, 16, 1), there(dy, 8, 1), 8, 8), k) for k, (dx, dy) in enumerate(SIDES[:4])]
    for copy in second:
        copy.wait_recv()

    def diverge(x, carry):
        above, below = inward(lane, pe[2, x + 8, 8:16, :])
        total = (pe[0, x + 9, 8:16, :] - pe[0, x + 7, 8:16, :]) + (pe[1, x + 8, 9:17, :] - pe[1, x + 8, 7:15, :]) + (above - below)
        src[x + 8, 8:16, :] = total * (0.5 / time_step)
        return carry

    lax.fori_loop(0, 16, diverge, 0, unroll=4)

    third = [push(box(src, near(dx, 16, 7), near(dy, 8, 7), 8, 8),
                  box(src, there(dx, 16, 7), there(dy, 8, 7), 8, 8), k) for k, (dx, dy) in enumerate(SIDES)]
    fourth = []
    for k, (dx, dy) in enumerate(SIDES):
        if k < 4:
            xs = (0, 16) if dx == 0 else ((13, 2) if dx > 0 else (1, 2))
            ys = (0, 8) if dy == 0 else ((5, 2) if dy > 0 else (1, 2))
            xd = (0, 16) if dx == 0 else ((-3, 2) if dx > 0 else (17, 2))
            yd = (0, 8) if dy == 0 else ((-3, 2) if dy > 0 else (9, 2))
        else:
            xs, ys, xd, yd = near(dx, 16, 3), near(dy, 8, 3), there(dx, 16, 3), there(dy, 8, 3)
        fourth.append(push(box(pe, xs, ys, 8, 8), box(pe, xd, yd, 8, 8), k))
    for copy in third:
        copy.wait_recv()

    def relax(old, new, reach, starts, first_sweep):
        scale = -1.0 / 6.0 if first_sweep else 1.0

        def step(x, carry):
            for s in starts:
                here = pl.ds(s, 8)
                v = old[x, here, :] * scale
                above, below = inward(lane, v)
                total = (old[x + 1, here, :] + old[x - 1, here, :]) + (old[x, s + 1:s + 9, :] + old[x, s - 1:s + 7, :])
                new[x, here, :] = (total * scale + (above + below) - src[x, here, :]) * (1.0 / 6.0)
            return carry

        lax.fori_loop(8 - reach, 24 + reach, step, 0, unroll=2)

    relax(src, pa, 6, (2, 8, 14), True)
    relax(pa, pb, 5, (3, 8, 13), False)
    relax(pb, pa, 4, (4, 12), False)
    for copy in fourth:
        copy.wait_recv()
    v_ref[:, :, 8:16, :] = jnp.zeros((3, 24, 8, 128), F32)
    v_ref[:, 22:24, 0:8, :] = jnp.zeros((3, 2, 8, 128), F32)

    def finish(x, carry):
        for s in (5, 11):
            here = pl.ds(s, 8)
            above, below = inward(lane, pa[x, here, :])
            grad = (pa[x + 1, here, :] - pa[x - 1, here, :], pa[x, s + 1:s + 9, :] - pa[x, s - 1:s + 7, :], above - below)
            for c in range(3):
                v_ref[c, x - 5, pl.ds(s - 5, 8), :] = pe[c, x, here, :] - (0.5 * time_step) * grad[c]
        return carry

    lax.fori_loop(5, 27, finish, 0, unroll=2)
    new_ref[...] = v_ref[:, 3:19, 3:11, :]
    prs_ref[...] = pa[8:24, 8:16, :]
    for copy in started:
        copy.wait_send()


def fluid_call(widened, velocity):
    return pl.pallas_call(
        fluid_body,
        out_shape=(jax.ShapeDtypeStruct((3, 16, 8, 128), F32), jax.ShapeDtypeStruct((16, 8, 128), F32), jax.ShapeDtypeStruct((3, 24, 16, 128), F32)),
        in_specs=[VM, VM],
        out_specs=(VM, VM, VM),
        scratch_shapes=[
            pltpu.VMEM((3, 18, 24, 128), F32),
            pltpu.VMEM((3, 32, 24, 128), F32),
            pltpu.VMEM((32, 24, 128), F32),
            pltpu.VMEM((32, 24, 128), F32),
            pltpu.VMEM((32, 24, 128), F32),
            pltpu.VMEM((3, 3, 16, 8, 128), F32),
            pltpu.SemaphoreType.DMA((32,)),
            pltpu.SemaphoreType.DMA((32,)),
        ],
        compiler_params=pltpu.CompilerParams(vmem_limit_bytes=32 * 2**20, collective_id=0, has_side_effects=True),
        name="fluid",
    )(widened, velocity)


def shards(velocity, offsets, forces, owner, base, counts):
    axes = ("gx", "gy")
    stage, back = pl.pallas_call(
        pack_body,
        out_shape=(jax.ShapeDtypeStruct((2048, 128), F32), jax.ShapeDtypeStruct((128, 256), F32)),
        in_specs=[SM, VM, VM, VM, VM],
        out_specs=(VM, VM),
        compiler_params=pltpu.CompilerParams(vmem_limit_bytes=32 * 2**20),
        name="pack",
    )(counts, owner.reshape(1, 128), offsets, forces, base)
    arrived = lax.all_to_all(stage.reshape(128, 16, 128), axes, split_axis=0, concat_axis=0, tiled=True)
    corners = arrived[:, 6, :6].astype(jnp.int32).reshape(-1)
    spread_grid = spread_call(corners, arrived, 4)
    new_velocity, pressure, sampled = fluid_call(spread_grid, velocity)
    answers = interp_call(corners, arrived, sampled, 4)
    returned = lax.all_to_all(answers, axes, split_axis=0, concat_axis=0, tiled=True)
    marker_velocity = pl.pallas_call(
        unpack_body,
        out_shape=jax.ShapeDtypeStruct((3, 128, 128), F32),
        in_specs=[VM, VM],
        out_specs=VM,
        compiler_params=pltpu.CompilerParams(vmem_limit_bytes=32 * 2**20),
        name="unpack",
    )(back, returned.reshape(1024, 128))
    return (new_velocity, pressure, marker_velocity)


def solution(mesh):
    return jax.shard_map(
        shards,
        mesh=mesh,
        in_specs=(
            P(None, "gx", "gy", None),
            P(None, ("gx", "gy"), None),
            P(None, ("gx", "gy"), None),
            P(("gx", "gy")),
            P(None, ("gx", "gy")),
            P(("gx", "gy")),
        ),
        out_specs=(P(None, "gx", "gy", None), P("gx", "gy", None), P(None, ("gx", "gy"), None)),
        check_vma=False,
    )
```

```python
import functools
import jax, jax.numpy as jnp
from jax import lax
from jax.experimental import pallas as pl
from jax.experimental.pallas import tpu as pltpu
from jax.sharding import PartitionSpec as P

time_step = 0.5
viscosity = 0.1

F32 = jnp.float32
BF = jnp.bfloat16

def split(v):
    hi = v.astype(BF)
    lo = (v - hi.astype(F32)).astype(BF)
    return hi, lo


def weight(cells, row, tabs):
    fl, a1, a2, q8 = [t[pl.ds(row, 1), :] for t in tabs]
    e = cells - fl
    s = jnp.where(e < 0.5, a1, a2)
    g = e * (e - 1.0)
    return jnp.where(g < 1.0, s + q8, jnp.where(g < 3.0, s - q8, 0.0))


def plane_of(y0, row, tabs, wxs, iota8, iota16):
    wxs[...] = weight(iota8, row, tabs)
    wy = weight(iota16 - y0, row + 1, tabs)
    return jnp.concatenate([wxs[pl.ds(i, 1), :] * wy for i in range(8)], axis=0)


def split3(v):
    hi = v.astype(BF)
    rest = v - hi.astype(F32)
    mid = rest.astype(BF)
    return hi, mid, (rest - mid.astype(F32)).astype(BF)


def routes(owner_row, count):
    rows = lax.broadcasted_iota(jnp.int32, (128, 128), 0)
    slots = lax.broadcasted_iota(jnp.int32, (128, 128), 1)
    match = jnp.where((owner_row == rows) & (slots < count), 1.0, 0.0)
    before = jnp.where(rows < slots, 1.0, 0.0)
    rank = jnp.dot(match.astype(BF), before.astype(BF), preferred_element_type=F32)
    return jnp.where(rank < 0.5, match, 0.0), jnp.where(rank < 0.5, 0.0, match)


def spread_rows(stage, row, values):
    for d in range(0, 128, 8):
        stage[pl.ds(d * 16 + row, 8, stride=16), :] = values[d:d + 8]


def pack_rows(first, second, off_ref, frc_ref, base_ref, stage):
    both = jnp.concatenate([first, second], axis=0).astype(BF)
    for q in range(6):
        data = off_ref[q] if q < 3 else frc_ref[q - 3]
        parts = jnp.concatenate(split3(data), axis=1)
        got = jnp.dot(both, parts, preferred_element_type=F32)
        got = got[:, :128] + (got[:, 128:256] + got[:, 256:])
        for r in range(2):
            spread_rows(stage, (q // 3) * 8 + r * 3 + q % 3, got[r * 128:r * 128 + 128])
    rows = base_ref[...].astype(F32)
    none = jnp.zeros((122, 128), F32)
    blank = jnp.zeros((3, 128), F32)
    dims = (((1,), (1,)), ((), ()))
    one = jnp.concatenate([rows, blank, none], axis=0).astype(BF)
    two = jnp.concatenate([blank, rows, none], axis=0).astype(BF)
    corner = lax.dot_general(both[:128], one, dims, preferred_element_type=F32)
    corner += lax.dot_general(both[128:], two, dims, preferred_element_type=F32)
    spread_rows(stage, 6, corner)
    for row in (7, 14, 15):
        spread_rows(stage, row, jnp.zeros((128, 128), F32))


VM = pl.BlockSpec(memory_space=pltpu.VMEM)
SM = pl.BlockSpec(memory_space=pltpu.SMEM)


MESH = pl.DeviceIdType.MESH
SIDES = ((1, 0), (-1, 0), (0, 1), (0, -1), (1, 1), (1, -1), (-1, 1), (-1, -1))


def neighbours():
    gx, gy = lax.axis_index("gx"), lax.axis_index("gy")
    nx, ny = lax.axis_size("gx"), lax.axis_size("gy")
    return [(lax.rem(gx + dx + nx, nx), lax.rem(gy + dy + ny, ny)) for dx, dy in SIDES]


def near(step, size, width):
    return (0, size) if step == 0 else ((size - width, width) if step > 0 else (0, width))


def there(step, size, width):
    return (0, size) if step == 0 else ((-width, width) if step > 0 else (size, width))


def inward(lane, v):
    above = jnp.where(lane == 127, 0.0, pltpu.roll(v, 127, 1))
    below = jnp.where(lane == 0, 0.0, pltpu.roll(v, 1, 1))
    return above, below


def fluid_body(w_ref, vel_ref, new_ref, prs_ref, v_ref, ve, pe, src, pa, pb, fold, send, recv):
    peers = neighbours()
    barrier = pltpu.get_barrier_semaphore()
    fold[...] = jnp.zeros(fold.shape, F32)
    for peer in peers:
        pl.semaphore_signal(barrier, inc=1, device_id=peer, device_id_type=MESH)
    ve[:, 1:17, 8:16, :] = vel_ref[...]
    pl.semaphore_wait(barrier, 8)
    started = []

    def push(source, target, k):
        n = len(started)
        copy = pltpu.make_async_remote_copy(source, target, send.at[n], recv.at[n], device_id=peers[k], device_id_type=MESH)
        copy.start()
        started.append(copy)
        return copy

    def box(ref, xs, ys, x_at, y_at):
        return ref.at[..., pl.ds(xs[0] + x_at, xs[1]), pl.ds(ys[0] + y_at, ys[1]), :]

    first = []
    for k, (dx, dy) in enumerate(SIDES):
        xs = (3, 16) if dx == 0 else ((19, 3) if dx > 0 else (0, 3))
        ys = (3, 8) if dy == 0 else ((11, 3) if dy > 0 else (0, 3))
        xd = (0, 16) if dx == 0 else ((0, 3) if dx > 0 else (13, 3))
        yd = (0, 8) if dy == 0 else ((0, 3) if dy > 0 else (5, 3))
        layer = 0 if dy == 0 else (1 if dx == 0 else 2)
        first.append(push(w_ref.at[:, pl.ds(xs[0], xs[1]), pl.ds(ys[0], ys[1]), :],
                          fold.at[layer, :, pl.ds(xd[0], xd[1]), pl.ds(yd[0], yd[1]), :], k))
        if k < 4:
            first.append(push(box(vel_ref, near(dx, 16, 1), near(dy, 8, 1), 0, 0),
                              box(ve, there(dx, 16, 1), there(dy, 8, 1), 1, 8), k))
    for copy in first:
        copy.wait_recv()
    lane = lax.broadcasted_iota(jnp.int32, (8, 128), 1)

    def provide(x, carry):
        for c in range(3):
            v = ve[c, x + 1, 8:16, :]
            above, below = inward(lane, v)
            lap = (ve[c, x + 2, 8:16, :] + ve[c, x, 8:16, :]) + (ve[c, x + 1, 9:17, :] + ve[c, x + 1, 7:15, :]) + (above + below) - 6.0 * v
            force = w_ref[c, x + 3, 3:11, :] + fold[0, c, x] + fold[1, c, x] + fold[2, c, x]
            pe[c, x + 8, 8:16, :] = v + time_step * (viscosity * lap + force)
        return carry

    lax.fori_loop(0, 16, provide, 0, unroll=4)

    second = [push(box(pe, near(dx, 16, 1), near(dy, 8, 1), 8, 8),
                   box(pe, there(dx, 16, 1), there(dy, 8, 1), 8, 8), k) for k, (dx, dy) in enumerate(SIDES[:4])]
    for copy in second:
        copy.wait_recv()

    def diverge(x, carry):
        above, below = inward(lane, pe[2, x + 8, 8:16, :])
        total = (pe[0, x + 9, 8:16, :] - pe[0, x + 7, 8:16, :]) + (pe[1, x + 8, 9:17, :] - pe[1, x + 8, 7:15, :]) + (above - below)
        src[x + 8, 8:16, :] = total * (0.5 / time_step)
        return carry

    lax.fori_loop(0, 16, diverge, 0, unroll=4)

    third = [push(box(src, near(dx, 16, 7), near(dy, 8, 7), 8, 8),
                  box(src, there(dx, 16, 7), there(dy, 8, 7), 8, 8), k) for k, (dx, dy) in enumerate(SIDES)]
    fourth = []
    for k, (dx, dy) in enumerate(SIDES):
        if k < 4:
            xs = (0, 16) if dx == 0 else ((13, 2) if dx > 0 else (1, 2))
            ys = (0, 8) if dy == 0 else ((5, 2) if dy > 0 else (1, 2))
            xd = (0, 16) if dx == 0 else ((-3, 2) if dx > 0 else (17, 2))
            yd = (0, 8) if dy == 0 else ((-3, 2) if dy > 0 else (9, 2))
        else:
            xs, ys, xd, yd = near(dx, 16, 3), near(dy, 8, 3), there(dx, 16, 3), there(dy, 8, 3)
        fourth.append(push(box(pe, xs, ys, 8, 8), box(pe, xd, yd, 8, 8), k))
    for copy in third:
        copy.wait_recv()

    def relax(old, new, reach, starts, first_sweep):
        scale = -1.0 / 6.0 if first_sweep else 1.0

        def step(x, carry):
            for s in starts:
                here = pl.ds(s, 8)
                v = old[x, here, :] * scale
                above, below = inward(lane, v)
                total = (old[x + 1, here, :] + old[x - 1, here, :]) + (old[x, s + 1:s + 9, :] + old[x, s - 1:s + 7, :])
                new[x, here, :] = (total * scale + (above + below) - src[x, here, :]) * (1.0 / 6.0)
            return carry

        lax.fori_loop(8 - reach, 24 + reach, step, 0, unroll=2)

    relax(src, pa, 6, (2, 8, 14), True)
    relax(pa, pb, 5, (3, 8, 13), False)
    relax(pb, pa, 4, (4, 12), False)
    for copy in fourth:
        copy.wait_recv()
    v_ref[:, :, 8:16, :] = jnp.zeros((3, 24, 8, 128), F32)
    v_ref[:, 22:24, 0:8, :] = jnp.zeros((3, 2, 8, 128), F32)

    def finish(x, carry):
        for s in (5, 11):
            here = pl.ds(s, 8)
            above, below = inward(lane, pa[x, here, :])
            grad = (pa[x + 1, here, :] - pa[x - 1, here, :], pa[x, s + 1:s + 9, :] - pa[x, s - 1:s + 7, :], above - below)
            for c in range(3):
                v_ref[c, x - 5, pl.ds(s - 5, 8), :] = pe[c, x, here, :] - (0.5 * time_step) * grad[c]
        return carry

    lax.fori_loop(5, 27, finish, 0, unroll=2)
    new_ref[...] = v_ref[:, 3:19, 3:11, :]
    prs_ref[...] = pa[8:24, 8:16, :]
    for copy in started:
        copy.wait_send()


def fluid_call(widened, velocity):
    return pl.pallas_call(
        fluid_body,
        out_shape=(jax.ShapeDtypeStruct((3, 16, 8, 128), F32), jax.ShapeDtypeStruct((16, 8, 128), F32), jax.ShapeDtypeStruct((3, 24, 16, 128), F32)),
        in_specs=[VM, VM],
        out_specs=(VM, VM, VM),
        scratch_shapes=[
            pltpu.VMEM((3, 18, 24, 128), F32),
            pltpu.VMEM((3, 32, 24, 128), F32),
            pltpu.VMEM((32, 24, 128), F32),
            pltpu.VMEM((32, 24, 128), F32),
            pltpu.VMEM((32, 24, 128), F32),
            pltpu.VMEM((3, 3, 16, 8, 128), F32),
            pltpu.SemaphoreType.DMA((32,)),
            pltpu.SemaphoreType.DMA((32,)),
        ],
        compiler_params=pltpu.CompilerParams(vmem_limit_bytes=32 * 2**20, collective_id=0, has_side_effects=True),
        name="fluid",
    )(widened, velocity)


def position():
    gx, gy = lax.axis_index("gx"), lax.axis_index("gy")
    return gx >> 1, gx & 1, gy >> 2, gy & 3


def shifted(k, here, sign):
    y, core, z, x = here
    kc, kx, ky, kz = k & 1, (k >> 1) & 3, (k >> 3) & 3, k >> 5
    if sign < 0:
        kx, ky, kz = 4 - kx, 4 - ky, 4 - kz
    return (((y + ky) & 3) * 2 + ((core + kc) & 1), ((z + kz) & 3) * 4 + ((x + kx) & 3))


def steps_to(owner, here):
    y, core, z, x = here
    row, column = owner >> 4, owner & 15
    kc, ky = ((row & 1) - core) & 1, ((row >> 1) - y) & 3
    kz, kx = ((column >> 2) - z) & 3, ((column & 3) - x) & 3
    return kc + 2 * kx + 8 * ky + 32 * kz


def greet_all(line_sem, between):
    gx, gy = lax.axis_index("gx"), lax.axis_index("gy")
    barrier = pltpu.get_barrier_semaphore()
    for i in range(1, 16):
        pl.semaphore_signal(barrier, inc=1, device_id=(gx, (gy + i) & 15), device_id_type=MESH)
    for i in range(1, 8):
        pl.semaphore_signal(barrier, inc=1, device_id=((gx + i) & 7, gy), device_id_type=MESH)
    between()
    pl.semaphore_wait(barrier, 22)
    for i in range(1, 8):
        pl.semaphore_signal(line_sem, inc=1, device_id=((gx + i) & 7, gy), device_id_type=MESH)
    pl.semaphore_wait(line_sem, 7)


def exchange_body(unroll, count_s, owner_ref, off_ref, frc_ref, base_ref, arrived, boxes, corners, back, stage, fl, a1, a2, q8, wxs, line_sem, send, recv):
    here = position()

    def prepare():
        first, second = routes(steps_to(owner_ref[...], here), count_s[0])
        back[:, :128] = first.T
        back[:, 128:] = second.T
        pack_rows(first, second, off_ref, frc_ref, base_ref, stage)

    greet_all(line_sem, prepare)

    def message(k):
        rows = pl.ds(pl.multiple_of(k * 16, 16), 14)
        return pltpu.make_async_remote_copy(stage.at[rows], arrived.at[rows], send.at[k], recv.at[k], device_id=shifted(k, here, 1), device_id_type=MESH)

    def begin(k, carry):
        message(k).start()
        return carry

    lax.fori_loop(1, 128, begin, 0)
    arrived[0:16] = stage[0:16]
    iota8 = lax.broadcasted_iota(jnp.int32, (8, 128), 0).astype(F32) - 3.0
    iota16 = lax.broadcasted_iota(jnp.int32, (16, 128), 0).astype(F32) - 3.0
    tabs = (fl, a1, a2, q8)

    def work(ks):
        for u, k in enumerate(ks):
            at = k * 16 if isinstance(k, int) else pl.multiple_of(k * 16, 16)
            t = arrived[pl.ds(at, 8), :]
            whole = jnp.floor(t)
            f = t - whole
            fl[u * 8:u * 8 + 8, :] = whole
            a1[u * 8:u * 8 + 8, :] = (3.0 - 2.0 * f) * 0.125
            a2[u * 8:u * 8 + 8, :] = (1.0 + 2.0 * f) * 0.125
            q8[u * 8:u * 8 + 8, :] = jnp.sqrt(1.0 + 4.0 * f * (1.0 - f)) * 0.125
        for u, k in enumerate(ks):
            for r in range(2):
                row = u * 8 + r * 3
                y0 = arrived[pl.ds(k * 16 + 6, 1), r * 3 + 1:r * 3 + 2]
                B = plane_of(y0, row, tabs, wxs.at[u * 2 + r], iota8, iota16)
                wz = weight(iota8, row + 2, tabs)
                A = jnp.concatenate([arrived[pl.ds(k * 16 + 8 + r * 3 + c, 1), :] * wz for c in range(3)], axis=0)
                ah, al = split(A)
                bh, bl = split(B)
                o = lax.dot_general(jnp.concatenate([ah, al], 0), jnp.concatenate([bh, bl], 0), (((1,), (1,)), ((), ())), preferred_element_type=F32)
                boxes[k * 2 + r] = o[:24, :128] + o[24:, :128] + o[:24, 128:]

    for k in range(1, unroll):
        message(k).wait_recv()
    work(list(range(unroll)))

    def turn(t, carry):
        ks = [t * unroll + u for u in range(unroll)]
        for k in ks:
            message(k).wait_recv()
        work(ks)
        return carry

    lax.fori_loop(1, 128 // unroll, turn, 0)
    gathered = jnp.concatenate([arrived[pl.ds(d * 16 + 6, 8, stride=16), :] for d in range(0, 128, 8)], axis=0)
    corners[...] = gathered.T[0:8].astype(jnp.int32)

    def end(k, carry):
        message(k).wait_send()
        return carry

    lax.fori_loop(1, 128, end, 0)


def exchange_call(counts, owner, offsets, forces, base, unroll=4):
    shapes = ((2048, 128), F32), ((256, 24, 128), F32), ((8, 128), jnp.int32), ((128, 256), F32)
    return pl.pallas_call(
        functools.partial(exchange_body, unroll),
        out_shape=tuple(jax.ShapeDtypeStruct(*s) for s in shapes),
        in_specs=[SM, VM, VM, VM, VM],
        out_specs=(VM,) * 4,
        scratch_shapes=[pltpu.VMEM((2048, 128), F32)] + [pltpu.VMEM((8 * unroll, 128), F32)] * 4 + [
            pltpu.VMEM((2 * unroll, 8, 128), F32),
            pltpu.SemaphoreType.REGULAR,
            pltpu.SemaphoreType.DMA((128,)),
            pltpu.SemaphoreType.DMA((128,)),
        ],
        compiler_params=pltpu.CompilerParams(vmem_limit_bytes=40 * 2**20, collective_id=1, has_side_effects=True),
        name="exchange",
    )(counts, owner.reshape(1, 128), offsets, forces, base)


def deposit_body(corners_s, boxes, out, acc, tot):
    def zero(x, carry):
        acc[x] = jnp.zeros((3, 128, 128), F32)
        return carry

    lax.fori_loop(0, 16, zero, 0)

    def add(k, carry):
        for r in range(2):
            x0 = corners_s[r * 3, k]
            z0 = jnp.maximum(corners_s[r * 3 + 2, k] - 3, 0)
            for c in range(3):
                acc[x0, c, pl.ds(z0, 8), :] += boxes[k * 2 + r, c * 8:c * 8 + 8]
        return carry

    lax.fori_loop(0, 128, add, 0, unroll=4)
    lane = lax.broadcasted_iota(jnp.int32, (128, 128), 1)
    for c in range(3):
        filled = [False] * 3
        for t in range(2):
            for r in range(8):
                a = acc[8 * t + r, c]
                if r == 0:
                    parts = [(t, a)]
                else:
                    a = pltpu.roll(a, 16 * r, 1)
                    parts = [(t, jnp.where(lane >= 16 * r, a, 0.0)), (t + 1, jnp.where(lane < 16 * r, a, 0.0))]
                for k, v in parts:
                    tot[k] = tot[k] + v if filled[k] else v
                    filled[k] = True
        for k in range(3):
            out[c, 8 * k:8 * k + 8] = tot[k].T.reshape(8, 16, 128)


def deposit_call(corners, boxes):
    return pl.pallas_call(
        deposit_body,
        out_shape=jax.ShapeDtypeStruct((3, 24, 16, 128), F32),
        in_specs=[SM, VM],
        out_specs=VM,
        scratch_shapes=[pltpu.VMEM((16, 3, 128, 128), F32), pltpu.VMEM((3, 128, 128), F32)],
        compiler_params=pltpu.CompilerParams(vmem_limit_bytes=40 * 2**20),
        name="deposit",
    )(corners, boxes)


def answer_body(unroll, corners_s, arrived, v_ref, back, out, ans, ret, fl, a1, a2, q8, cop, wxs, line_sem, send, recv):
    here = position()
    lane = lax.broadcasted_iota(jnp.int32, (128, 128), 1)
    tabs = (fl, a1, a2, q8)

    def prepare():
        for c in range(3):
            tiles = [v_ref[c, 8 * k:8 * k + 8].reshape(128, 128).T for k in range(3)]
            for r in range(8):
                if r == 0:
                    cop[0, c], cop[8, c] = tiles[0], tiles[1]
                else:
                    ro = [pltpu.roll(x, 128 - 16 * r, 1) for x in tiles]
                    for t in range(2):
                        cop[8 * t + r, c] = jnp.where(lane < 128 - 16 * r, ro[t], ro[t + 1])

        def body(b, carry):
            t = arrived[pl.ds(b * 8, 8), 0:8, :].reshape(64, 128)
            whole = jnp.floor(t)
            f = t - whole
            rows = pl.ds(pl.multiple_of(b * 64, 64), 64)
            fl[rows, :] = whole
            a1[rows, :] = (3.0 - 2.0 * f) * 0.125
            a2[rows, :] = (1.0 + 2.0 * f) * 0.125
            q8[rows, :] = jnp.sqrt(1.0 + 4.0 * f * (1.0 - f)) * 0.125
            return carry

        lax.fori_loop(0, 16, body, 0)

    greet_all(line_sem, prepare)
    iota8 = lax.broadcasted_iota(jnp.int32, (8, 128), 0).astype(F32) - 3.0
    iota16 = lax.broadcasted_iota(jnp.int32, (16, 128), 0).astype(F32) - 3.0

    def message(k):
        rows = pl.ds(pl.multiple_of(k * 8, 8), 6)
        return pltpu.make_async_remote_copy(ans.at[rows], ret.at[rows], send.at[k], recv.at[k], device_id=shifted(k, here, -1), device_id_type=MESH)

    def work(ks):
        for u, k in enumerate(ks):
            for r in range(2):
                row = k * 8 + r * 3
                B = plane_of(corners_s[r * 3 + 1, k].astype(F32), row, tabs, wxs.at[u * 2 + r], iota8, iota16)
                wz = weight(iota8, row + 2, tabs)
                x0 = corners_s[r * 3, k]
                z0 = jnp.maximum(corners_s[r * 3 + 2, k] - 3, 0)
                A = jnp.concatenate([cop[x0, c, pl.ds(z0, 8), :] for c in range(3)], axis=0)
                ah, al = split(A)
                bh, bl = split(B)
                o = jnp.dot(jnp.concatenate([ah, al], 0), jnp.concatenate([bh, bl], 1), preferred_element_type=F32)
                o = o[:24, :128] + o[24:, :128] + o[:24, 128:]
                for c in range(3):
                    ans[pl.ds(k * 8 + r * 3 + c, 1), :] = jnp.sum(o[8 * c:8 * c + 8] * wz, axis=0, keepdims=True)

    work(list(range(unroll)))
    for k in range(1, unroll):
        message(k).start()

    def turn(t, carry):
        ks = [t * unroll + u for u in range(unroll)]
        work(ks)
        for k in ks:
            message(k).start()
        return carry

    lax.fori_loop(1, 128 // unroll, turn, 0)
    ret[0:8] = ans[0:8]
    pick = back[...].astype(BF)

    def settle(k, carry):
        message(k).wait_recv()
        return carry

    lax.fori_loop(1, 128, settle, 0)
    for c in range(3):
        data = jnp.concatenate([ret[pl.ds(r * 3 + c, 128, stride=8), :] for r in range(2)], axis=0)
        got = jnp.dot(pick, jnp.concatenate(split3(data), axis=1), preferred_element_type=F32)
        out[c] = got[:, :128] + (got[:, 128:256] + got[:, 256:])

    def end(k, carry):
        message(k).wait_send()
        return carry

    lax.fori_loop(1, 128, end, 0)


def answer_call(corners, arrived, sampled, back, unroll=4):
    return pl.pallas_call(
        functools.partial(answer_body, unroll),
        out_shape=jax.ShapeDtypeStruct((3, 128, 128), F32),
        in_specs=[SM, VM, VM, VM],
        out_specs=VM,
        scratch_shapes=[pltpu.VMEM((1024, 128), F32)] * 2 + [pltpu.VMEM((1024, 128), F32)] * 4 + [
            pltpu.VMEM((16, 3, 128, 128), F32),
            pltpu.VMEM((2 * unroll, 8, 128), F32),
            pltpu.SemaphoreType.REGULAR,
            pltpu.SemaphoreType.DMA((128,)),
            pltpu.SemaphoreType.DMA((128,)),
        ],
        compiler_params=pltpu.CompilerParams(vmem_limit_bytes=40 * 2**20, collective_id=2, has_side_effects=True),
        name="answer",
    )(corners, arrived, sampled, back)


def shards(velocity, offsets, forces, owner, base, counts):
    arrived, boxes, corners, back = exchange_call(counts, owner, offsets, forces, base)
    new_velocity, pressure, sampled = fluid_call(deposit_call(corners, boxes), velocity)
    marker_velocity = answer_call(corners, arrived.reshape(128, 16, 128), sampled, back)
    return (new_velocity, pressure, marker_velocity)


def solution(mesh):
    return jax.shard_map(
        shards,
        mesh=mesh,
        in_specs=(
            P(None, "gx", "gy", None),
            P(None, ("gx", "gy"), None),
            P(None, ("gx", "gy"), None),
            P(("gx", "gy")),
            P(None, ("gx", "gy")),
            P(("gx", "gy")),
        ),
        out_specs=(P(None, "gx", "gy", None), P("gx", "gy", None), P(None, ("gx", "gy"), None)),
        check_vma=False,
    )
```

```python
import functools
import jax, jax.numpy as jnp
from jax import lax
from jax.experimental import pallas as pl
from jax.experimental.pallas import tpu as pltpu
from jax.sharding import PartitionSpec as P

time_step = 0.5
viscosity = 0.1

F32 = jnp.float32
BF = jnp.bfloat16

def split(v):
    hi = v.astype(BF)
    lo = (v - hi.astype(F32)).astype(BF)
    return hi, lo


def weight(cells, row, tabs):
    fl, a1, a2, q8 = [t[pl.ds(row, 1), :] for t in tabs]
    e = cells - fl
    s = jnp.where(e < 0.5, a1, a2)
    g = e * (e - 1.0)
    return jnp.where(g < 1.0, s + q8, jnp.where(g < 3.0, s - q8, 0.0))


def plane_of(y0, row, tabs, wxs, iota8, iota16):
    wxs[...] = weight(iota8, row, tabs)
    wy = weight(iota16 - y0, row + 1, tabs)
    return jnp.concatenate([wxs[pl.ds(i, 1), :] * wy for i in range(8)], axis=0)


def split3(v):
    hi = v.astype(BF)
    rest = v - hi.astype(F32)
    mid = rest.astype(BF)
    return hi, mid, (rest - mid.astype(F32)).astype(BF)


def routes(owner_row, count):
    rows = lax.broadcasted_iota(jnp.int32, (128, 128), 0)
    slots = lax.broadcasted_iota(jnp.int32, (128, 128), 1)
    match = jnp.where((owner_row == rows) & (slots < count), 1.0, 0.0)
    before = jnp.where(rows < slots, 1.0, 0.0)
    rank = jnp.dot(match.astype(BF), before.astype(BF), preferred_element_type=F32)
    return jnp.where(rank < 0.5, match, 0.0), jnp.where(rank < 0.5, 0.0, match)


def spread_rows(stage, row, values):
    for d in range(0, 128, 8):
        stage[pl.ds(d * 16 + row, 8, stride=16), :] = values[d:d + 8]


def pack_rows(first, second, off_ref, frc_ref, base_ref, stage):
    both = jnp.concatenate([first, second], axis=0).astype(BF)
    for q in range(6):
        data = off_ref[q] if q < 3 else frc_ref[q - 3]
        parts = jnp.concatenate(split3(data), axis=1)
        got = jnp.dot(both, parts, preferred_element_type=F32)
        got = got[:, :128] + (got[:, 128:256] + got[:, 256:])
        for r in range(2):
            spread_rows(stage, (q // 3) * 8 + r * 3 + q % 3, got[r * 128:r * 128 + 128])
    rows = base_ref[...].astype(F32)
    none = jnp.zeros((122, 128), F32)
    blank = jnp.zeros((3, 128), F32)
    dims = (((1,), (1,)), ((), ()))
    one = jnp.concatenate([rows, blank, none], axis=0).astype(BF)
    two = jnp.concatenate([blank, rows, none], axis=0).astype(BF)
    corner = lax.dot_general(both[:128], one, dims, preferred_element_type=F32)
    corner += lax.dot_general(both[128:], two, dims, preferred_element_type=F32)
    spread_rows(stage, 6, corner)
    for row in (7, 14, 15):
        spread_rows(stage, row, jnp.zeros((128, 128), F32))


VM = pl.BlockSpec(memory_space=pltpu.VMEM)
SM = pl.BlockSpec(memory_space=pltpu.SMEM)
ANY = pl.BlockSpec(memory_space=pltpu.HBM)


def position():
    gx, gy = lax.axis_index("gx"), lax.axis_index("gy")
    return gx >> 1, gx & 1, gy >> 2, gy & 3


def shifted(k, here, sign):
    y, core, z, x = here
    kc, kx, ky, kz = k & 1, (k >> 1) & 3, (k >> 3) & 3, k >> 5
    if sign < 0:
        kx, ky, kz = 4 - kx, 4 - ky, 4 - kz
    return (((y + ky) & 3) * 2 + ((core + kc) & 1), ((z + kz) & 3) * 4 + ((x + kx) & 3))


def steps_to(owner, here):
    y, core, z, x = here
    row, column = owner >> 4, owner & 15
    kc, ky = ((row & 1) - core) & 1, ((row >> 1) - y) & 3
    kz, kx = ((column >> 2) - z) & 3, ((column & 3) - x) & 3
    return kc + 2 * kx + 8 * ky + 32 * kz


def greet_all(line_sem, between):
    gx, gy = lax.axis_index("gx"), lax.axis_index("gy")
    barrier = pltpu.get_barrier_semaphore()
    for i in range(1, 16):
        pl.semaphore_signal(barrier, inc=1, device_id=(gx, (gy + i) & 15), device_id_type=MESH)
    for i in range(1, 8):
        pl.semaphore_signal(barrier, inc=1, device_id=((gx + i) & 7, gy), device_id_type=MESH)
    between()
    pl.semaphore_wait(barrier, 22)
    for i in range(1, 8):
        pl.semaphore_signal(line_sem, inc=1, device_id=((gx + i) & 7, gy), device_id_type=MESH)
    pl.semaphore_wait(line_sem, 7)


def exchange_body(unroll, count_s, owner_ref, off_hbm, frc_hbm, base_ref, arrived, boxes, corners, back, off_ref, frc_ref, load, stage, fl, a1, a2, q8, wxs, line_sem, send, recv):
    here = position()
    loads = [pltpu.make_async_copy(off_hbm, off_ref, load.at[0]), pltpu.make_async_copy(frc_hbm, frc_ref, load.at[1])]
    for copy in loads:
        copy.start()

    def prepare():
        first, second = routes(steps_to(owner_ref[...], here), count_s[0])
        back[:, :128] = first.T
        back[:, 128:] = second.T
        for copy in loads:
            copy.wait()
        pack_rows(first, second, off_ref, frc_ref, base_ref, stage)

    greet_all(line_sem, prepare)

    def message(k):
        rows = pl.ds(pl.multiple_of(k * 16, 16), 14)
        return pltpu.make_async_remote_copy(stage.at[rows], arrived.at[rows], send.at[k], recv.at[k], device_id=shifted(k, here, 1), device_id_type=MESH)

    def begin(k, carry):
        message(k).start()
        return carry

    lax.fori_loop(1, 128, begin, 0)
    arrived[0:16] = stage[0:16]
    iota8 = lax.broadcasted_iota(jnp.int32, (8, 128), 0).astype(F32) - 3.0
    iota16 = lax.broadcasted_iota(jnp.int32, (16, 128), 0).astype(F32) - 3.0
    tabs = (fl, a1, a2, q8)

    def work(ks):
        for u, k in enumerate(ks):
            at = k * 16 if isinstance(k, int) else pl.multiple_of(k * 16, 16)
            t = arrived[pl.ds(at, 8), :]
            whole = jnp.floor(t)
            f = t - whole
            fl[u * 8:u * 8 + 8, :] = whole
            a1[u * 8:u * 8 + 8, :] = (3.0 - 2.0 * f) * 0.125
            a2[u * 8:u * 8 + 8, :] = (1.0 + 2.0 * f) * 0.125
            q8[u * 8:u * 8 + 8, :] = jnp.sqrt(1.0 + 4.0 * f * (1.0 - f)) * 0.125
        for u, k in enumerate(ks):
            for r in range(2):
                row = u * 8 + r * 3
                y0 = arrived[pl.ds(k * 16 + 6, 1), r * 3 + 1:r * 3 + 2]
                B = plane_of(y0, row, tabs, wxs.at[u * 2 + r], iota8, iota16)
                wz = weight(iota8, row + 2, tabs)
                A = jnp.concatenate([arrived[pl.ds(k * 16 + 8 + r * 3 + c, 1), :] * wz for c in range(3)], axis=0)
                ah, al = split(A)
                bh, bl = split(B)
                o = lax.dot_general(jnp.concatenate([ah, al], 0), jnp.concatenate([bh, bl], 0), (((1,), (1,)), ((), ())), preferred_element_type=F32)
                boxes[k * 2 + r] = o[:24, :128] + o[24:, :128] + o[:24, 128:]

    for k in range(1, unroll):
        message(k).wait_recv()
    work(list(range(unroll)))

    def turn(t, carry):
        ks = [t * unroll + u for u in range(unroll)]
        for k in ks:
            message(k).wait_recv()
        work(ks)
        return carry

    lax.fori_loop(1, 128 // unroll, turn, 0)
    gathered = jnp.concatenate([arrived[pl.ds(d * 16 + 6, 8, stride=16), :] for d in range(0, 128, 8)], axis=0)
    corners[...] = gathered.T[0:8].astype(jnp.int32)

    def end(k, carry):
        message(k).wait_send()
        return carry

    lax.fori_loop(1, 128, end, 0)


def exchange_call(counts, owner, offsets, forces, base, unroll=8):
    shapes = ((2048, 128), F32), ((256, 24, 128), F32), ((8, 128), jnp.int32), ((128, 256), F32)
    return pl.pallas_call(
        functools.partial(exchange_body, unroll),
        out_shape=tuple(jax.ShapeDtypeStruct(*s) for s in shapes),
        in_specs=[SM, VM, ANY, ANY, VM],
        out_specs=(VM,) * 4,
        scratch_shapes=[pltpu.VMEM((3, 128, 128), F32), pltpu.VMEM((3, 128, 128), F32), pltpu.SemaphoreType.DMA((2,))] + [pltpu.VMEM((2048, 128), F32)] + [pltpu.VMEM((8 * unroll, 128), F32)] * 4 + [
            pltpu.VMEM((2 * unroll, 8, 128), F32),
            pltpu.SemaphoreType.REGULAR,
            pltpu.SemaphoreType.DMA((128,)),
            pltpu.SemaphoreType.DMA((128,)),
        ],
        compiler_params=pltpu.CompilerParams(vmem_limit_bytes=40 * 2**20, collective_id=1, has_side_effects=True),
        name="exchange",
    )(counts, owner.reshape(1, 128), offsets, forces, base)


def deposit_body(corners_s, boxes, out, acc, tot):
    def zero(x, carry):
        acc[x] = jnp.zeros((3, 128, 128), F32)
        return carry

    lax.fori_loop(0, 16, zero, 0)

    def add(k, carry):
        for r in range(2):
            x0 = corners_s[r * 3, k]
            z0 = jnp.maximum(corners_s[r * 3 + 2, k] - 3, 0)
            for c in range(3):
                acc[x0, c, pl.ds(z0, 8), :] += boxes[k * 2 + r, c * 8:c * 8 + 8]
        return carry

    lax.fori_loop(0, 128, add, 0, unroll=4)
    lane = lax.broadcasted_iota(jnp.int32, (128, 128), 1)
    for c in range(3):
        filled = [False] * 3
        for t in range(2):
            for r in range(8):
                a = acc[8 * t + r, c]
                if r == 0:
                    parts = [(t, a)]
                else:
                    a = pltpu.roll(a, 16 * r, 1)
                    parts = [(t, jnp.where(lane >= 16 * r, a, 0.0)), (t + 1, jnp.where(lane < 16 * r, a, 0.0))]
                for k, v in parts:
                    tot[k] = tot[k] + v if filled[k] else v
                    filled[k] = True
        for k in range(3):
            out[c, 8 * k:8 * k + 8] = tot[k].T.reshape(8, 16, 128)


def deposit_call(corners, boxes):
    return pl.pallas_call(
        deposit_body,
        out_shape=jax.ShapeDtypeStruct((3, 24, 16, 128), F32),
        in_specs=[SM, VM],
        out_specs=VM,
        scratch_shapes=[pltpu.VMEM((16, 3, 128, 128), F32), pltpu.VMEM((3, 128, 128), F32)],
        compiler_params=pltpu.CompilerParams(vmem_limit_bytes=40 * 2**20),
        name="deposit",
    )(corners, boxes)


MESH = pl.DeviceIdType.MESH
SIDES = ((1, 0), (-1, 0), (0, 1), (0, -1), (1, 1), (1, -1), (-1, 1), (-1, -1))


def neighbours():
    gx, gy = lax.axis_index("gx"), lax.axis_index("gy")
    nx, ny = lax.axis_size("gx"), lax.axis_size("gy")
    return [(lax.rem(gx + dx + nx, nx), lax.rem(gy + dy + ny, ny)) for dx, dy in SIDES]


def near(step, size, width):
    return (0, size) if step == 0 else ((size - width, width) if step > 0 else (0, width))


def there(step, size, width):
    return (0, size) if step == 0 else ((-width, width) if step > 0 else (size, width))


def inward(lane, v):
    above = jnp.where(lane == 127, 0.0, pltpu.roll(v, 127, 1))
    below = jnp.where(lane == 0, 0.0, pltpu.roll(v, 1, 1))
    return above, below


def project_body(unroll, chunks, corners_s, arrived, w_ref, vel_hbm, new_ref, prs_ref, ret, vel_ref, load, v_ref, ve, pe, src, pa, pb, fold, tables, wxs, planes, depths, cop, ans, line_sem, send, recv, out_sem, in_sem):
    here = position()
    peers = neighbours()
    gx, gy = lax.axis_index("gx"), lax.axis_index("gy")
    barrier = pltpu.get_barrier_semaphore()
    velocity_in = pltpu.make_async_copy(vel_hbm, vel_ref, load)
    velocity_in.start()
    fold[...] = jnp.zeros(fold.shape, F32)
    for i in range(1, 16):
        pl.semaphore_signal(barrier, inc=1, device_id=(gx, (gy + i) & 15), device_id_type=MESH)
    for i in range(1, 8):
        pl.semaphore_signal(barrier, inc=1, device_id=((gx + i) & 7, gy), device_id_type=MESH)
    velocity_in.wait()
    ve[:, 1:17, 8:16, :] = vel_ref[...]
    iota8 = lax.broadcasted_iota(jnp.int32, (8, 128), 0).astype(F32) - 3.0
    iota16 = lax.broadcasted_iota(jnp.int32, (16, 128), 0).astype(F32) - 3.0

    def weigh(begin, end):
        def turn(t, carry):
            for u in range(unroll):
                k = t * unroll + u
                rows = pl.ds(u * 8, 8)
                whole = jnp.floor(arrived[k, 0:8, :])
                f = arrived[k, 0:8, :] - whole
                for n, v in enumerate((whole, (3.0 - 2.0 * f) * 0.125, (1.0 + 2.0 * f) * 0.125, jnp.sqrt(1.0 + 4.0 * f * (1.0 - f)) * 0.125)):
                    tables[n, rows, :] = v
                for r in range(2):
                    row, p = u * 8 + r * 3, k * 2 + r
                    tabs = [tables.at[n] for n in range(4)]
                    bh, bl = split(plane_of(corners_s[r * 3 + 1, k].astype(F32), row, tabs, wxs.at[u * 2 + r], iota8, iota16))
                    planes[p, :, :128] = bh
                    planes[p, :, 128:] = bl
                    depths[p] = weight(iota8, row + 2, tabs)
            return carry

        lax.fori_loop(begin // unroll, end // unroll, turn, 0)

    weigh(chunks[0], chunks[1])
    pl.semaphore_wait(barrier, 22)
    for i in range(1, 8):
        pl.semaphore_signal(line_sem, inc=1, device_id=((gx + i) & 7, gy), device_id_type=MESH)
    started = []

    def push(source, target, k):
        n = len(started)
        copy = pltpu.make_async_remote_copy(source, target, send.at[n], recv.at[n], device_id=peers[k], device_id_type=MESH)
        copy.start()
        started.append(copy)
        return copy

    def box(ref, xs, ys, x_at, y_at):
        return ref.at[..., pl.ds(xs[0] + x_at, xs[1]), pl.ds(ys[0] + y_at, ys[1]), :]

    first = []
    for k, (dx, dy) in enumerate(SIDES):
        if k == 4:
            pl.semaphore_wait(line_sem, 7)
        xs = (3, 16) if dx == 0 else ((19, 3) if dx > 0 else (0, 3))
        ys = (3, 8) if dy == 0 else ((11, 3) if dy > 0 else (0, 3))
        xd = (0, 16) if dx == 0 else ((0, 3) if dx > 0 else (13, 3))
        yd = (0, 8) if dy == 0 else ((0, 3) if dy > 0 else (5, 3))
        layer = 0 if dy == 0 else (1 if dx == 0 else 2)
        first.append(push(w_ref.at[:, pl.ds(xs[0], xs[1]), pl.ds(ys[0], ys[1]), :],
                          fold.at[layer, :, pl.ds(xd[0], xd[1]), pl.ds(yd[0], yd[1]), :], k))
        if k < 4:
            first.append(push(box(vel_ref, near(dx, 16, 1), near(dy, 8, 1), 0, 0),
                              box(ve, there(dx, 16, 1), there(dy, 8, 1), 1, 8), k))
    weigh(chunks[1], chunks[2])
    for copy in first:
        copy.wait_recv()
    lane = lax.broadcasted_iota(jnp.int32, (8, 128), 1)

    def provide(x, carry):
        for c in range(3):
            v = ve[c, x + 1, 8:16, :]
            above, below = inward(lane, v)
            lap = (ve[c, x + 2, 8:16, :] + ve[c, x, 8:16, :]) + (ve[c, x + 1, 9:17, :] + ve[c, x + 1, 7:15, :]) + (above + below) - 6.0 * v
            force = w_ref[c, x + 3, 3:11, :] + fold[0, c, x] + fold[1, c, x] + fold[2, c, x]
            pe[c, x + 8, 8:16, :] = v + time_step * (viscosity * lap + force)
        return carry

    lax.fori_loop(0, 16, provide, 0, unroll=8)

    second = [push(box(pe, near(dx, 16, 1), near(dy, 8, 1), 8, 8),
                   box(pe, there(dx, 16, 1), there(dy, 8, 1), 8, 8), k) for k, (dx, dy) in enumerate(SIDES[:4])]
    weigh(chunks[2], chunks[3])
    for copy in second:
        copy.wait_recv()

    def diverge(x, carry):
        above, below = inward(lane, pe[2, x + 8, 8:16, :])
        total = (pe[0, x + 9, 8:16, :] - pe[0, x + 7, 8:16, :]) + (pe[1, x + 8, 9:17, :] - pe[1, x + 8, 7:15, :]) + (above - below)
        src[x + 8, 8:16, :] = total * (0.5 / time_step)
        return carry

    lax.fori_loop(0, 16, diverge, 0, unroll=16)

    third = [push(box(src, near(dx, 16, 7), near(dy, 8, 7), 8, 8),
                  box(src, there(dx, 16, 7), there(dy, 8, 7), 8, 8), k) for k, (dx, dy) in enumerate(SIDES)]
    fourth = []
    for k, (dx, dy) in enumerate(SIDES):
        if k < 4:
            xs = (0, 16) if dx == 0 else ((13, 2) if dx > 0 else (1, 2))
            ys = (0, 8) if dy == 0 else ((5, 2) if dy > 0 else (1, 2))
            xd = (0, 16) if dx == 0 else ((-3, 2) if dx > 0 else (17, 2))
            yd = (0, 8) if dy == 0 else ((-3, 2) if dy > 0 else (9, 2))
        else:
            xs, ys, xd, yd = near(dx, 16, 3), near(dy, 8, 3), there(dx, 16, 3), there(dy, 8, 3)
        fourth.append(push(box(pe, xs, ys, 8, 8), box(pe, xd, yd, 8, 8), k))
    weigh(chunks[3], chunks[4])
    for copy in third:
        copy.wait_recv()

    def relax(old, new, reach, starts, first_sweep):
        scale = -1.0 / 6.0 if first_sweep else 1.0

        def step(x, carry):
            for s in starts:
                here = pl.ds(s, 8)
                v = old[x, here, :] * scale
                above, below = inward(lane, v)
                total = (old[x + 1, here, :] + old[x - 1, here, :]) + (old[x, s + 1:s + 9, :] + old[x, s - 1:s + 7, :])
                new[x, here, :] = (total * scale + (above + below) - src[x, here, :]) * (1.0 / 6.0)
            return carry

        lax.fori_loop(8 - reach, 24 + reach, step, 0, unroll=(16 + 2 * reach) // 2)

    relax(src, pa, 6, (2, 8, 14), True)
    relax(pa, pb, 5, (3, 8, 13), False)
    relax(pb, pa, 4, (4, 12), False)
    for copy in fourth:
        copy.wait_recv()
    v_ref[:, :, 8:16, :] = jnp.zeros((3, 24, 8, 128), F32)
    v_ref[:, 22:24, 0:8, :] = jnp.zeros((3, 2, 8, 128), F32)

    def finish(x, carry):
        for s in (5, 11):
            here = pl.ds(s, 8)
            above, below = inward(lane, pa[x, here, :])
            grad = (pa[x + 1, here, :] - pa[x - 1, here, :], pa[x, s + 1:s + 9, :] - pa[x, s - 1:s + 7, :], above - below)
            for c in range(3):
                v_ref[c, x - 5, pl.ds(s - 5, 8), :] = pe[c, x, here, :] - (0.5 * time_step) * grad[c]
        return carry

    lax.fori_loop(5, 27, finish, 0, unroll=11)
    new_ref[...] = v_ref[:, 3:19, 3:11, :]
    prs_ref[...] = pa[8:24, 8:16, :]
    for copy in started:
        copy.wait_send()


    for c in range(3):
        tiles = [v_ref[c, 8 * k:8 * k + 8].reshape(128, 128).T for k in range(3)]
        wide = lax.broadcasted_iota(jnp.int32, (128, 128), 1)
        for r in range(8):
            if r == 0:
                cop[0, c], cop[8, c] = tiles[0], tiles[1]
            else:
                ro = [pltpu.roll(x, 128 - 16 * r, 1) for x in tiles]
                for t in range(2):
                    cop[8 * t + r, c] = jnp.where(wide < 128 - 16 * r, ro[t], ro[t + 1])

    def message(k):
        rows = pl.ds(pl.multiple_of(k * 8, 8), 6)
        return pltpu.make_async_remote_copy(ans.at[rows], ret.at[rows], out_sem.at[k], in_sem.at[k], device_id=shifted(k, here, -1), device_id_type=MESH)

    def work(ks):
        for k in ks:
            for r in range(2):
                p = k * 2 + r
                x0 = corners_s[r * 3, k]
                z0 = jnp.maximum(corners_s[r * 3 + 2, k] - 3, 0)
                ah, al = split(jnp.concatenate([cop[x0, c, pl.ds(z0, 8), :] for c in range(3)], axis=0))
                o = jnp.dot(jnp.concatenate([ah, al], 0), planes[p], preferred_element_type=F32)
                o = o[:24, :128] + o[24:, :128] + o[:24, 128:]
                wz = depths[p]
                for c in range(3):
                    ans[pl.ds(k * 8 + r * 3 + c, 1), :] = jnp.sum(o[8 * c:8 * c + 8] * wz, axis=0, keepdims=True)

    work(list(range(unroll)))
    for k in range(1, unroll):
        message(k).start()

    def turn(t, carry):
        ks = [t * unroll + u for u in range(unroll)]
        work(ks)
        for k in ks:
            message(k).start()
        return carry

    lax.fori_loop(1, 128 // unroll, turn, 0)
    ret[0:8] = ans[0:8]

    def settle(k, carry):
        message(k).wait_recv()
        return carry

    lax.fori_loop(1, 128, settle, 0)

    def end(k, carry):
        message(k).wait_send()
        return carry

    lax.fori_loop(1, 128, end, 0)


def project_call(corners, arrived, widened, velocity, unroll=4, chunks=(0, 16, 56, 88, 128)):
    shapes = (3, 16, 8, 128), (16, 8, 128), (1024, 128)
    return pl.pallas_call(
        functools.partial(project_body, unroll, chunks),
        out_shape=tuple(jax.ShapeDtypeStruct(s, F32) for s in shapes),
        in_specs=[SM, VM, VM, ANY],
        out_specs=(VM,) * 3,
        scratch_shapes=[
            pltpu.VMEM((3, 16, 8, 128), F32),
            pltpu.SemaphoreType.DMA,
            pltpu.VMEM((3, 24, 16, 128), F32),
            pltpu.VMEM((3, 18, 24, 128), F32),
            pltpu.VMEM((3, 32, 24, 128), F32),
            pltpu.VMEM((32, 24, 128), F32),
            pltpu.VMEM((32, 24, 128), F32),
            pltpu.VMEM((32, 24, 128), F32),
            pltpu.VMEM((3, 3, 16, 8, 128), F32),
            pltpu.VMEM((4, 8 * unroll, 128), F32),
            pltpu.VMEM((2 * unroll, 8, 128), F32),
            pltpu.VMEM((256, 128, 256), BF),
            pltpu.VMEM((256, 8, 128), F32),
            pltpu.VMEM((16, 3, 128, 128), F32),
            pltpu.VMEM((1024, 128), F32),
            pltpu.SemaphoreType.REGULAR,
            pltpu.SemaphoreType.DMA((32,)),
            pltpu.SemaphoreType.DMA((32,)),
            pltpu.SemaphoreType.DMA((128,)),
            pltpu.SemaphoreType.DMA((128,)),
        ],
        compiler_params=pltpu.CompilerParams(vmem_limit_bytes=40 * 2**20, collective_id=0, has_side_effects=True),
        name="project",
    )(corners, arrived, widened, velocity)


def finish_body(back, ret, new_ref, prs_ref, out_new, out_prs, out, sems):
    copies = [pltpu.make_async_copy(new_ref, out_new, sems.at[0]), pltpu.make_async_copy(prs_ref, out_prs, sems.at[1])]
    for copy in copies:
        copy.start()
    pick = back[...].astype(BF)
    for c in range(3):
        data = jnp.concatenate([ret[pl.ds(r * 3 + c, 128, stride=8), :] for r in range(2)], axis=0)
        got = jnp.dot(pick, jnp.concatenate(split3(data), axis=1), preferred_element_type=F32)
        out[c] = got[:, :128] + (got[:, 128:256] + got[:, 256:])
    for copy in copies:
        copy.wait()


def finish_call(back, ret, new, pressure):
    shapes = (3, 16, 8, 128), (16, 8, 128), (3, 128, 128)
    return pl.pallas_call(
        finish_body,
        out_shape=tuple(jax.ShapeDtypeStruct(s, F32) for s in shapes),
        in_specs=[VM, VM, VM, VM],
        out_specs=(ANY, ANY, VM),
        scratch_shapes=[pltpu.SemaphoreType.DMA((2,))],
        compiler_params=pltpu.CompilerParams(vmem_limit_bytes=32 * 2**20),
        name="finish",
    )(back, ret, new, pressure)


def shards(velocity, offsets, forces, owner, base, counts):
    arrived, boxes, corners, back = exchange_call(counts, owner, offsets, forces, base)
    widened = deposit_call(corners, boxes)
    new_velocity, pressure, returned = project_call(corners, arrived.reshape(128, 16, 128), widened, velocity)
    return finish_call(back, returned, new_velocity, pressure)


def solution(mesh):
    return jax.shard_map(
        shards,
        mesh=mesh,
        in_specs=(
            P(None, "gx", "gy", None),
            P(None, ("gx", "gy"), None),
            P(None, ("gx", "gy"), None),
            P(("gx", "gy")),
            P(None, ("gx", "gy")),
            P(("gx", "gy")),
        ),
        out_specs=(P(None, "gx", "gy", None), P("gx", "gy", None), P(None, ("gx", "gy"), None)),
        check_vma=False,
    )
```

```python
import functools
import jax, jax.numpy as jnp
from jax import lax
from jax.experimental import pallas as pl
from jax.experimental.pallas import tpu as pltpu
from jax.sharding import PartitionSpec as P

time_step = 0.5
viscosity = 0.1

F32 = jnp.float32
BF = jnp.bfloat16

def split(v):
    hi = v.astype(BF)
    lo = (v - hi.astype(F32)).astype(BF)
    return hi, lo


def weight(cells, row, tabs):
    fl, a1, a2, q8 = [t[pl.ds(row, 1), :] for t in tabs]
    e = cells - fl
    s = jnp.where(e < 0.5, a1, a2)
    g = e * (e - 1.0)
    return jnp.where(g < 1.0, s + q8, jnp.where(g < 3.0, s - q8, 0.0))


def plane_of(y0, row, tabs, wxs, iota8, iota16):
    wxs[...] = weight(iota8, row, tabs)
    wy = weight(iota16 - y0, row + 1, tabs)
    return jnp.concatenate([wxs[pl.ds(i, 1), :] * wy for i in range(8)], axis=0)


def split3(v):
    hi = v.astype(BF)
    rest = v - hi.astype(F32)
    mid = rest.astype(BF)
    return hi, mid, (rest - mid.astype(F32)).astype(BF)


def routes(owner_row, count):
    rows = lax.broadcasted_iota(jnp.int32, (128, 128), 0)
    slots = lax.broadcasted_iota(jnp.int32, (128, 128), 1)
    match = jnp.where((owner_row == rows) & (slots < count), 1.0, 0.0)
    before = jnp.where(rows < slots, 1.0, 0.0)
    rank = jnp.dot(match.astype(BF), before.astype(BF), preferred_element_type=F32)
    return jnp.where(rank < 0.5, match, 0.0), jnp.where(rank < 0.5, 0.0, match)


def spread_rows(stage, row, values):
    for d in range(0, 128, 8):
        stage[pl.ds(d % 64 * 32 + d // 64 * 13 + row, 8, stride=32), :] = values[d:d + 8]


def pack_rows(first, second, off_ref, frc_ref, base_ref, stage):
    both = jnp.concatenate([first, second], axis=0).astype(BF)
    for q in range(6):
        data = off_ref[q] if q < 3 else frc_ref[q - 3]
        parts = jnp.concatenate(split3(data), axis=1)
        got = jnp.dot(both, parts, preferred_element_type=F32)
        got = got[:, :128] + (got[:, 128:256] + got[:, 256:])
        for r in range(2):
            spread_rows(stage, (q // 3) * 7 + r * 3 + q % 3, got[r * 128:r * 128 + 128])
    rows = base_ref[...].astype(F32)
    none = jnp.zeros((122, 128), F32)
    blank = jnp.zeros((3, 128), F32)
    dims = (((1,), (1,)), ((), ()))
    one = jnp.concatenate([rows, blank, none], axis=0).astype(BF)
    two = jnp.concatenate([blank, rows, none], axis=0).astype(BF)
    corner = lax.dot_general(both[:128], one, dims, preferred_element_type=F32)
    corner += lax.dot_general(both[128:], two, dims, preferred_element_type=F32)
    spread_rows(stage, 6, corner)


VM = pl.BlockSpec(memory_space=pltpu.VMEM)
SM = pl.BlockSpec(memory_space=pltpu.SMEM)
ANY = pl.BlockSpec(memory_space=pltpu.HBM)


def position():
    gx, gy = lax.axis_index("gx"), lax.axis_index("gy")
    return gx >> 1, gx & 1, gy >> 2, gy & 3


def shifted(chip, here, sign):
    y, core, z, x = here
    kx, ky, kz = chip & 3, (chip >> 2) & 3, chip >> 4
    if sign < 0:
        kx, ky, kz = 4 - kx, 4 - ky, 4 - kz
    return (((y + ky) & 3) * 2 + core, ((z + kz) & 3) * 4 + ((x + kx) & 3))


def sibling(here):
    y, core, z, x = here
    return (y * 2 + 1 - core, z * 4 + x)


def steps_to(owner, here):
    y, core, z, x = here
    row, column = owner >> 4, owner & 15
    kc, ky = ((row & 1) - core) & 1, ((row >> 1) - y) & 3
    kz, kx = ((column >> 2) - z) & 3, ((column & 3) - x) & 3
    return kx + 4 * ky + 16 * kz + 64 * kc


def greet_all(line_sem, between):
    gx, gy = lax.axis_index("gx"), lax.axis_index("gy")
    barrier = pltpu.get_barrier_semaphore()
    for i in range(1, 16):
        pl.semaphore_signal(barrier, inc=1, device_id=(gx, (gy + i) & 15), device_id_type=MESH)
    for i in range(1, 8):
        pl.semaphore_signal(barrier, inc=1, device_id=((gx + i) & 7, gy), device_id_type=MESH)
    between()
    pl.semaphore_wait(barrier, 22)
    for i in range(1, 8):
        pl.semaphore_signal(line_sem, inc=1, device_id=((gx + i) & 7, gy), device_id_type=MESH)
    pl.semaphore_wait(line_sem, 7)


def exchange_body(count_s, owner_ref, off_hbm, frc_hbm, base_ref, inbox, relay, boxes, corners, back, off_ref, frc_ref, load, stage, tables, wxs, line_sem, send, recv, pass_sem, take_sem):
    here = position()
    loads = [pltpu.make_async_copy(off_hbm, off_ref, load.at[0]), pltpu.make_async_copy(frc_hbm, frc_ref, load.at[1])]
    for copy in loads:
        copy.start()

    def prepare():
        first, second = routes(steps_to(owner_ref[...], here), count_s[0])
        back[:, :128] = first.T
        back[:, 128:] = second.T
        for copy in loads:
            copy.wait()
        pack_rows(first, second, off_ref, frc_ref, base_ref, stage)

    greet_all(line_sem, prepare)

    def message(chip):
        rows = pl.ds(pl.multiple_of(chip * 32, 32), 26)
        return pltpu.make_async_remote_copy(stage.at[rows], inbox.at[rows], send.at[chip], recv.at[chip], device_id=shifted(chip, here, 1), device_id_type=MESH)

    def onward(group):
        return pltpu.make_async_remote_copy(
            inbox.reshape(64, 32, 128).at[pl.ds(group * 8, 8), pl.ds(13, 13)],
            relay.reshape(64, 16, 128).at[pl.ds(group * 8, 8), pl.ds(0, 13)],
            pass_sem.at[group], take_sem.at[group], device_id=sibling(here), device_id_type=MESH)

    def begin(chip, carry):
        message(chip).start()
        return carry

    lax.fori_loop(1, 64, begin, 0, unroll=7)
    inbox[0:32] = stage[0:32]
    iota8 = lax.broadcasted_iota(jnp.int32, (8, 128), 0).astype(F32) - 3.0
    iota16 = lax.broadcasted_iota(jnp.int32, (16, 128), 0).astype(F32) - 3.0
    tabs = [tables.at[n] for n in range(4)]

    def work(box, pitch, group, shift):
        for u in range(8):
            at = group * (8 * pitch) + u * pitch
            t = box[pl.ds(at, 8), :]
            whole = jnp.floor(t)
            f = t - whole
            for n, v in enumerate((whole, (3.0 - 2.0 * f) * 0.125, (1.0 + 2.0 * f) * 0.125, jnp.sqrt(1.0 + 4.0 * f * (1.0 - f)) * 0.125)):
                tables[n, u * 8:u * 8 + 8, :] = v
        for u in range(8):
            at = group * (8 * pitch) + u * pitch
            for r in range(2):
                row = u * 8 + r * 3
                y0 = box[pl.ds(at + 6, 1), r * 3 + 1:r * 3 + 2]
                B = plane_of(y0, row, tabs, wxs.at[u * 2 + r], iota8, iota16)
                wz = weight(iota8, row + 2, tabs)
                A = jnp.concatenate([box[pl.ds(at + 7 + r * 3 + c, 1), :] * wz for c in range(3)], axis=0)
                ah, al = split(A)
                bh, bl = split(B)
                both = jnp.concatenate([ah, al], 0)
                o = lax.dot_general(jnp.concatenate([both, both], 1), jnp.concatenate([bh, bl], 1), (((1,), (1,)), ((), ())), preferred_element_type=F32)
                boxes[(shift + group * 8 + u) * 2 + r] = o[:24] + o[24:]

    for chip in range(1, 8):
        message(chip).wait_recv()
    onward(0).start()
    work(inbox, 32, 0, 0)

    def turn(group, carry):
        for u in range(8):
            message(group * 8 + u).wait_recv()
        onward(group).start()
        work(inbox, 32, group, 0)
        onward(group - 1).wait_recv()
        work(relay, 16, group - 1, 64)
        return carry

    lax.fori_loop(1, 8, turn, 0)
    onward(7).wait_recv()
    work(relay, 16, 7, 64)
    gathered = jnp.concatenate([inbox[pl.ds(d * 32 + 6, 8, stride=32), :] for d in range(0, 64, 8)] + [relay[pl.ds(d * 16 + 6, 8, stride=16), :] for d in range(0, 64, 8)], axis=0)
    corners[...] = gathered.T[0:8].astype(jnp.int32)

    def end(chip, carry):
        message(chip).wait_send()
        return carry

    lax.fori_loop(1, 64, end, 0)
    for group in range(8):
        onward(group).wait_send()


def exchange_call(counts, owner, offsets, forces, base):
    shapes = ((2048, 128), F32), ((1024, 128), F32), ((256, 24, 128), F32), ((8, 128), jnp.int32), ((128, 256), F32)
    return pl.pallas_call(
        exchange_body,
        out_shape=tuple(jax.ShapeDtypeStruct(*s) for s in shapes),
        in_specs=[SM, VM, ANY, ANY, VM],
        out_specs=(VM,) * 5,
        scratch_shapes=[pltpu.VMEM((3, 128, 128), F32), pltpu.VMEM((3, 128, 128), F32), pltpu.SemaphoreType.DMA((2,))] + [
            pltpu.VMEM((2048, 128), F32),
            pltpu.VMEM((4, 64, 128), F32),
            pltpu.VMEM((16, 8, 128), F32),
            pltpu.SemaphoreType.REGULAR,
            pltpu.SemaphoreType.DMA((64,)),
            pltpu.SemaphoreType.DMA((64,)),
            pltpu.SemaphoreType.DMA((8,)),
            pltpu.SemaphoreType.DMA((8,)),
        ],
        compiler_params=pltpu.CompilerParams(vmem_limit_bytes=40 * 2**20, collective_id=1, has_side_effects=True),
        name="exchange",
    )(counts, owner.reshape(1, 128), offsets, forces, base)


def deposit_body(corners_s, boxes, out, acc, tot):
    def zero(x, carry):
        acc[x] = jnp.zeros((3, 128, 128), F32)
        return carry

    lax.fori_loop(0, 16, zero, 0)

    def add(k, carry):
        for r in range(2):
            x0 = corners_s[r * 3, k]
            z0 = jnp.maximum(corners_s[r * 3 + 2, k] - 3, 0)
            for c in range(3):
                acc[x0, c, pl.ds(z0, 8), :] += boxes[k * 2 + r, c * 8:c * 8 + 8]
        return carry

    lax.fori_loop(0, 128, add, 0, unroll=4)
    lane = lax.broadcasted_iota(jnp.int32, (128, 128), 1)
    for c in range(3):
        filled = [False] * 3
        for t in range(2):
            for r in range(8):
                a = acc[8 * t + r, c]
                if r == 0:
                    parts = [(t, a)]
                else:
                    a = pltpu.roll(a, 16 * r, 1)
                    parts = [(t, jnp.where(lane >= 16 * r, a, 0.0)), (t + 1, jnp.where(lane < 16 * r, a, 0.0))]
                for k, v in parts:
                    tot[k] = tot[k] + v if filled[k] else v
                    filled[k] = True
        for k in range(3):
            out[c, 8 * k:8 * k + 8] = tot[k].T.reshape(8, 16, 128)


def deposit_call(corners, boxes):
    return pl.pallas_call(
        deposit_body,
        out_shape=jax.ShapeDtypeStruct((3, 24, 16, 128), F32),
        in_specs=[SM, VM],
        out_specs=VM,
        scratch_shapes=[pltpu.VMEM((16, 3, 128, 128), F32), pltpu.VMEM((3, 128, 128), F32)],
        compiler_params=pltpu.CompilerParams(vmem_limit_bytes=40 * 2**20),
        name="deposit",
    )(corners, boxes)


MESH = pl.DeviceIdType.MESH
SIDES = ((1, 0), (-1, 0), (0, 1), (0, -1), (1, 1), (1, -1), (-1, 1), (-1, -1))


def neighbours():
    gx, gy = lax.axis_index("gx"), lax.axis_index("gy")
    nx, ny = lax.axis_size("gx"), lax.axis_size("gy")
    return [(lax.rem(gx + dx + nx, nx), lax.rem(gy + dy + ny, ny)) for dx, dy in SIDES]


def near(step, size, width):
    return (0, size) if step == 0 else ((size - width, width) if step > 0 else (0, width))


def there(step, size, width):
    return (0, size) if step == 0 else ((-width, width) if step > 0 else (size, width))


def inward(lane, v):
    above = jnp.where(lane == 127, 0.0, pltpu.roll(v, 127, 1))
    below = jnp.where(lane == 0, 0.0, pltpu.roll(v, 1, 1))
    return above, below


def project_body(unroll, chunks, corners_s, inbox, relay, w_ref, vel_hbm, new_ref, prs_ref, direct, passed, vel_ref, load, v_ref, ve, pe, src, pa, pb, fold, tables, wxs, planes, depths, cop, ans, line_sem, send, recv, out_sem, in_sem, pass_sem, take_sem):
    here = position()
    peers = neighbours()
    gx, gy = lax.axis_index("gx"), lax.axis_index("gy")
    barrier = pltpu.get_barrier_semaphore()
    velocity_in = pltpu.make_async_copy(vel_hbm, vel_ref, load)
    velocity_in.start()
    fold[...] = jnp.zeros(fold.shape, F32)
    for i in range(1, 16):
        pl.semaphore_signal(barrier, inc=1, device_id=(gx, (gy + i) & 15), device_id_type=MESH)
    for i in range(1, 8):
        pl.semaphore_signal(barrier, inc=1, device_id=((gx + i) & 7, gy), device_id_type=MESH)
    velocity_in.wait()
    ve[:, 1:17, 8:16, :] = vel_ref[...]
    iota8 = lax.broadcasted_iota(jnp.int32, (8, 128), 0).astype(F32) - 3.0
    iota16 = lax.broadcasted_iota(jnp.int32, (16, 128), 0).astype(F32) - 3.0

    def weigh(begin, end):
        box, pitch, shift = (inbox, 32, 0) if begin < 64 else (relay, 16, 64)

        def turn(t, carry):
            for u in range(unroll):
                k = t * unroll + u
                rows = pl.ds(u * 8, 8)
                v = box[pl.ds((k - shift) * pitch, 8), :]
                whole = jnp.floor(v)
                f = v - whole
                for n, v in enumerate((whole, (3.0 - 2.0 * f) * 0.125, (1.0 + 2.0 * f) * 0.125, jnp.sqrt(1.0 + 4.0 * f * (1.0 - f)) * 0.125)):
                    tables[n, rows, :] = v
                for r in range(2):
                    row, p = u * 8 + r * 3, k * 2 + r
                    tabs = [tables.at[n] for n in range(4)]
                    bh, bl = split(plane_of(corners_s[r * 3 + 1, k].astype(F32), row, tabs, wxs.at[u * 2 + r], iota8, iota16))
                    planes[p, :128] = bh
                    planes[p, 128:] = bl
                    depths[p] = weight(iota8, row + 2, tabs)
            return carry

        lax.fori_loop(begin // unroll, end // unroll, turn, 0)

    weigh(chunks[0], chunks[1])
    pl.semaphore_wait(barrier, 22)
    for i in range(1, 8):
        pl.semaphore_signal(line_sem, inc=1, device_id=((gx + i) & 7, gy), device_id_type=MESH)
    started = []

    def push(source, target, k):
        n = len(started)
        copy = pltpu.make_async_remote_copy(source, target, send.at[n], recv.at[n], device_id=peers[k], device_id_type=MESH)
        copy.start()
        started.append(copy)
        return copy

    def box(ref, xs, ys, x_at, y_at):
        return ref.at[..., pl.ds(xs[0] + x_at, xs[1]), pl.ds(ys[0] + y_at, ys[1]), :]

    first = []
    for k, (dx, dy) in enumerate(SIDES):
        if k == 4:
            pl.semaphore_wait(line_sem, 7)
        xs = (3, 16) if dx == 0 else ((19, 3) if dx > 0 else (0, 3))
        ys = (3, 8) if dy == 0 else ((11, 3) if dy > 0 else (0, 3))
        xd = (0, 16) if dx == 0 else ((0, 3) if dx > 0 else (13, 3))
        yd = (0, 8) if dy == 0 else ((0, 3) if dy > 0 else (5, 3))
        layer = 0 if dy == 0 else (1 if dx == 0 else 2)
        first.append(push(w_ref.at[:, pl.ds(xs[0], xs[1]), pl.ds(ys[0], ys[1]), :],
                          fold.at[layer, :, pl.ds(xd[0], xd[1]), pl.ds(yd[0], yd[1]), :], k))
        if k < 4:
            first.append(push(box(vel_ref, near(dx, 16, 1), near(dy, 8, 1), 0, 0),
                              box(ve, there(dx, 16, 1), there(dy, 8, 1), 1, 8), k))
    weigh(chunks[1], chunks[2])
    for copy in first:
        copy.wait_recv()
    lane = lax.broadcasted_iota(jnp.int32, (8, 128), 1)

    def provide(x, carry):
        for c in range(3):
            v = ve[c, x + 1, 8:16, :]
            above, below = inward(lane, v)
            lap = (ve[c, x + 2, 8:16, :] + ve[c, x, 8:16, :]) + (ve[c, x + 1, 9:17, :] + ve[c, x + 1, 7:15, :]) + (above + below) - 6.0 * v
            force = w_ref[c, x + 3, 3:11, :] + fold[0, c, x] + fold[1, c, x] + fold[2, c, x]
            pe[c, x + 8, 8:16, :] = v + time_step * (viscosity * lap + force)
        return carry

    lax.fori_loop(0, 16, provide, 0, unroll=8)

    second = [push(box(pe, near(dx, 16, 1), near(dy, 8, 1), 8, 8),
                   box(pe, there(dx, 16, 1), there(dy, 8, 1), 8, 8), k) for k, (dx, dy) in enumerate(SIDES[:4])]
    weigh(chunks[2], chunks[3])
    for copy in second:
        copy.wait_recv()

    def diverge(x, carry):
        above, below = inward(lane, pe[2, x + 8, 8:16, :])
        total = (pe[0, x + 9, 8:16, :] - pe[0, x + 7, 8:16, :]) + (pe[1, x + 8, 9:17, :] - pe[1, x + 8, 7:15, :]) + (above - below)
        src[x + 8, 8:16, :] = total * (0.5 / time_step)
        return carry

    lax.fori_loop(0, 16, diverge, 0, unroll=16)

    third = [push(box(src, near(dx, 16, 7), near(dy, 8, 7), 8, 8),
                  box(src, there(dx, 16, 7), there(dy, 8, 7), 8, 8), k) for k, (dx, dy) in enumerate(SIDES)]
    fourth = []
    for k, (dx, dy) in enumerate(SIDES):
        if k < 4:
            xs = (0, 16) if dx == 0 else ((13, 2) if dx > 0 else (1, 2))
            ys = (0, 8) if dy == 0 else ((5, 2) if dy > 0 else (1, 2))
            xd = (0, 16) if dx == 0 else ((-3, 2) if dx > 0 else (17, 2))
            yd = (0, 8) if dy == 0 else ((-3, 2) if dy > 0 else (9, 2))
        else:
            xs, ys, xd, yd = near(dx, 16, 3), near(dy, 8, 3), there(dx, 16, 3), there(dy, 8, 3)
        fourth.append(push(box(pe, xs, ys, 8, 8), box(pe, xd, yd, 8, 8), k))
    weigh(chunks[3], chunks[4])
    for copy in third:
        copy.wait_recv()

    def relax(old, new, reach, starts, first_sweep):
        scale = -1.0 / 6.0 if first_sweep else 1.0

        def step(x, carry):
            for s in starts:
                here = pl.ds(s, 8)
                v = old[x, here, :] * scale
                above, below = inward(lane, v)
                total = (old[x + 1, here, :] + old[x - 1, here, :]) + (old[x, s + 1:s + 9, :] + old[x, s - 1:s + 7, :])
                new[x, here, :] = (total * scale + (above + below) - src[x, here, :]) * (1.0 / 6.0)
            return carry

        lax.fori_loop(8 - reach, 24 + reach, step, 0, unroll=(16 + 2 * reach) // 2)

    relax(src, pa, 6, (2, 8, 14), True)
    relax(pa, pb, 5, (3, 8, 13), False)
    relax(pb, pa, 4, (4, 12), False)
    for copy in fourth:
        copy.wait_recv()
    v_ref[:, :, 8:16, :] = jnp.zeros((3, 24, 8, 128), F32)
    v_ref[:, 22:24, 0:8, :] = jnp.zeros((3, 2, 8, 128), F32)

    def finish(x, carry):
        for s in (5, 11):
            here = pl.ds(s, 8)
            above, below = inward(lane, pa[x, here, :])
            grad = (pa[x + 1, here, :] - pa[x - 1, here, :], pa[x, s + 1:s + 9, :] - pa[x, s - 1:s + 7, :], above - below)
            for c in range(3):
                v_ref[c, x - 5, pl.ds(s - 5, 8), :] = pe[c, x, here, :] - (0.5 * time_step) * grad[c]
        return carry

    lax.fori_loop(5, 27, finish, 0, unroll=11)
    new_ref[...] = v_ref[:, 3:19, 3:11, :]
    prs_ref[...] = pa[8:24, 8:16, :]


    for c in range(3):
        tiles = [v_ref[c, 8 * k:8 * k + 8].reshape(128, 128).T for k in range(3)]
        wide = lax.broadcasted_iota(jnp.int32, (128, 128), 1)
        for r in range(8):
            if r == 0:
                cop[0, c], cop[8, c] = tiles[0], tiles[1]
            else:
                ro = [pltpu.roll(x, 128 - 16 * r, 1) for x in tiles]
                for t in range(2):
                    cop[8 * t + r, c] = jnp.where(wide < 128 - 16 * r, ro[t], ro[t + 1])

    def message(chip):
        rows = pl.ds(pl.multiple_of(chip * 16, 16), 12)
        return pltpu.make_async_remote_copy(ans.at[rows], direct.at[rows], out_sem.at[chip], in_sem.at[chip], device_id=shifted(chip, here, -1), device_id_type=MESH)

    def onward(group):
        return pltpu.make_async_remote_copy(
            direct.reshape(64, 16, 128).at[pl.ds(group * 16, 16), pl.ds(6, 6)],
            passed.reshape(64, 8, 128).at[pl.ds(group * 16, 16), pl.ds(0, 6)],
            pass_sem.at[group], take_sem.at[group], device_id=sibling(here), device_id_type=MESH)

    def work(chips):
        for chip in chips:
            for kc in range(2):
                k = chip + 64 * kc
                for r in range(2):
                    p = k * 2 + r
                    x0 = corners_s[r * 3, k]
                    z0 = jnp.maximum(corners_s[r * 3 + 2, k] - 3, 0)
                    ah, al = split(jnp.concatenate([cop[x0, c, pl.ds(z0, 8), :] for c in range(3)], axis=0))
                    both = jnp.concatenate([ah, al], 0)
                    o = jnp.dot(jnp.concatenate([both, both], 1), planes[p], preferred_element_type=F32)
                    o = o[:24] + o[24:]
                    wz = depths[p]
                    for c in range(3):
                        ans[pl.ds(chip * 16 + kc * 6 + r * 3 + c, 1), :] = jnp.sum(o[8 * c:8 * c + 8] * wz, axis=0, keepdims=True)

    work(list(range(4)))
    for chip in range(1, 4):
        message(chip).start()

    def turn(t, carry):
        chips = [t * 4 + u for u in range(4)]
        work(chips)
        for chip in chips:
            message(chip).start()
        return carry

    lax.fori_loop(1, 16, turn, 0)
    direct[0:16] = ans[0:16]
    for group in range(4):
        for chip in range(max(group * 16, 1), group * 16 + 16):
            message(chip).wait_recv()
        onward(group).start()
    for group in range(4):
        onward(group).wait_recv()

    def end(chip, carry):
        message(chip).wait_send()
        return carry

    lax.fori_loop(1, 64, end, 0)
    for group in range(4):
        onward(group).wait_send()
    for copy in started:
        copy.wait_send()


def project_call(corners, inbox, relay, widened, velocity, unroll=4, chunks=(0, 24, 64, 96, 128)):
    shapes = (3, 16, 8, 128), (16, 8, 128), (1024, 128), (512, 128)
    return pl.pallas_call(
        functools.partial(project_body, unroll, chunks),
        out_shape=tuple(jax.ShapeDtypeStruct(s, F32) for s in shapes),
        in_specs=[SM, VM, VM, VM, ANY],
        out_specs=(VM,) * 4,
        scratch_shapes=[
            pltpu.VMEM((3, 16, 8, 128), F32),
            pltpu.SemaphoreType.DMA,
            pltpu.VMEM((3, 24, 16, 128), F32),
            pltpu.VMEM((3, 18, 24, 128), F32),
            pltpu.VMEM((3, 32, 24, 128), F32),
            pltpu.VMEM((32, 24, 128), F32),
            pltpu.VMEM((32, 24, 128), F32),
            pltpu.VMEM((32, 24, 128), F32),
            pltpu.VMEM((3, 3, 16, 8, 128), F32),
            pltpu.VMEM((4, 8 * unroll, 128), F32),
            pltpu.VMEM((2 * unroll, 8, 128), F32),
            pltpu.VMEM((256, 256, 128), BF),
            pltpu.VMEM((256, 8, 128), F32),
            pltpu.VMEM((16, 3, 128, 128), F32),
            pltpu.VMEM((1024, 128), F32),
            pltpu.SemaphoreType.REGULAR,
            pltpu.SemaphoreType.DMA((32,)),
            pltpu.SemaphoreType.DMA((32,)),
            pltpu.SemaphoreType.DMA((64,)),
            pltpu.SemaphoreType.DMA((64,)),
            pltpu.SemaphoreType.DMA((4,)),
            pltpu.SemaphoreType.DMA((4,)),
        ],
        compiler_params=pltpu.CompilerParams(vmem_limit_bytes=40 * 2**20, collective_id=0, has_side_effects=True),
        name="project",
    )(corners, inbox, relay, widened, velocity)


def finish_body(back, direct, passed, new_ref, prs_ref, out_new, out_prs, out, sems):
    copies = [pltpu.make_async_copy(new_ref, out_new, sems.at[0]), pltpu.make_async_copy(prs_ref, out_prs, sems.at[1])]
    for copy in copies:
        copy.start()
    pick = back[...].astype(BF)
    for c in range(3):
        data = jnp.concatenate([box[pl.ds(r * 3 + c, 64, stride=pitch), :] for r in range(2) for box, pitch in ((direct, 16), (passed, 8))], axis=0)
        got = jnp.dot(pick, jnp.concatenate(split3(data), axis=1), preferred_element_type=F32)
        out[c] = got[:, :128] + (got[:, 128:256] + got[:, 256:])
    for copy in copies:
        copy.wait()


def finish_call(back, direct, passed, new, pressure):
    shapes = (3, 16, 8, 128), (16, 8, 128), (3, 128, 128)
    return pl.pallas_call(
        finish_body,
        out_shape=tuple(jax.ShapeDtypeStruct(s, F32) for s in shapes),
        in_specs=[VM] * 5,
        out_specs=(ANY, ANY, VM),
        scratch_shapes=[pltpu.SemaphoreType.DMA((2,))],
        compiler_params=pltpu.CompilerParams(vmem_limit_bytes=32 * 2**20),
        name="finish",
    )(back, direct, passed, new, pressure)


def shards(velocity, offsets, forces, owner, base, counts):
    inbox, relay, boxes, corners, back = exchange_call(counts, owner, offsets, forces, base)
    widened = deposit_call(corners, boxes)
    new_velocity, pressure, direct, passed = project_call(corners, inbox, relay, widened, velocity)
    return finish_call(back, direct, passed, new_velocity, pressure)


def solution(mesh):
    return jax.shard_map(
        shards,
        mesh=mesh,
        in_specs=(
            P(None, "gx", "gy", None),
            P(None, ("gx", "gy"), None),
            P(None, ("gx", "gy"), None),
            P(("gx", "gy")),
            P(None, ("gx", "gy")),
            P(("gx", "gy")),
        ),
        out_specs=(P(None, "gx", "gy", None), P("gx", "gy", None), P(None, ("gx", "gy"), None)),
        check_vma=False,
    )
```

```python
import functools
import jax, jax.numpy as jnp
from jax import lax
from jax.experimental import pallas as pl
from jax.experimental.pallas import tpu as pltpu
from jax.sharding import PartitionSpec as P

time_step = 0.5
viscosity = 0.1

F32 = jnp.float32
BF = jnp.bfloat16

def split(v):
    hi = v.astype(BF)
    lo = (v - hi.astype(F32)).astype(BF)
    return hi, lo


def weight(cells, row, tabs):
    fl, a1, a2, q8 = [t[pl.ds(row, 1), :] for t in tabs]
    e = cells - fl
    s = jnp.where(e < 0.5, a1, a2)
    g = e * (e - 1.0)
    return jnp.where(g < 1.0, s + q8, jnp.where(g < 3.0, s - q8, 0.0))


def plane_of(y0, row, tabs, wxs, iota8, iota16):
    wxs[...] = weight(iota8, row, tabs)
    wy = weight(iota16 - y0, row + 1, tabs)
    return jnp.concatenate([wxs[pl.ds(i, 1), :] * wy for i in range(8)], axis=0)


def split3(v):
    hi = v.astype(BF)
    rest = v - hi.astype(F32)
    mid = rest.astype(BF)
    return hi, mid, (rest - mid.astype(F32)).astype(BF)


def routes(owner_row, count):
    rows = lax.broadcasted_iota(jnp.int32, (128, 128), 0)
    slots = lax.broadcasted_iota(jnp.int32, (128, 128), 1)
    match = jnp.where((owner_row == rows) & (slots < count), 1.0, 0.0)
    before = jnp.where(rows < slots, 1.0, 0.0)
    rank = jnp.dot(match.astype(BF), before.astype(BF), preferred_element_type=F32)
    return jnp.where(rank < 0.5, match, 0.0), jnp.where(rank < 0.5, 0.0, match)


def spread_rows(stage, row, values):
    for d in range(0, 128, 8):
        stage[pl.ds(d % 64 * 32 + d // 64 * 13 + row, 8, stride=32), :] = values[d:d + 8]


def pack_rows(first, second, off_ref, frc_ref, base_ref, stage):
    both = jnp.concatenate([first, second], axis=0).astype(BF)
    for q in range(6):
        data = off_ref[q] if q < 3 else frc_ref[q - 3]
        parts = jnp.concatenate(split3(data), axis=1)
        got = jnp.dot(both, parts, preferred_element_type=F32)
        got = got[:, :128] + (got[:, 128:256] + got[:, 256:])
        for r in range(2):
            spread_rows(stage, (q // 3) * 7 + r * 3 + q % 3, got[r * 128:r * 128 + 128])
    rows = base_ref[0:3].astype(F32)
    none = jnp.zeros((122, 128), F32)
    blank = jnp.zeros((3, 128), F32)
    dims = (((1,), (1,)), ((), ()))
    one = jnp.concatenate([rows, blank, none], axis=0).astype(BF)
    two = jnp.concatenate([blank, rows, none], axis=0).astype(BF)
    corner = lax.dot_general(both[:128], one, dims, preferred_element_type=F32)
    corner += lax.dot_general(both[128:], two, dims, preferred_element_type=F32)
    spread_rows(stage, 6, corner)


VM = pl.BlockSpec(memory_space=pltpu.VMEM)
SM = pl.BlockSpec(memory_space=pltpu.SMEM)
ANY = pl.BlockSpec(memory_space=pltpu.HBM)


def position():
    gx, gy = lax.axis_index("gx"), lax.axis_index("gy")
    return gx >> 1, gx & 1, gy >> 2, gy & 3


def shifted(chip, here, sign):
    y, core, z, x = here
    kx, ky, kz = chip & 3, (chip >> 2) & 3, chip >> 4
    if sign < 0:
        kx, ky, kz = 4 - kx, 4 - ky, 4 - kz
    return (((y + ky) & 3) * 2 + core, ((z + kz) & 3) * 4 + ((x + kx) & 3))


def sibling(here):
    y, core, z, x = here
    return (y * 2 + 1 - core, z * 4 + x)


def steps_to(owner, here):
    y, core, z, x = here
    row, column = owner >> 4, owner & 15
    kc, ky = ((row & 1) - core) & 1, ((row >> 1) - y) & 3
    kz, kx = ((column >> 2) - z) & 3, ((column & 3) - x) & 3
    return kx + 4 * ky + 16 * kz + 64 * kc


def greet_all(line_sem, between):
    gx, gy = lax.axis_index("gx"), lax.axis_index("gy")
    barrier = pltpu.get_barrier_semaphore()
    for i in range(1, 16):
        pl.semaphore_signal(barrier, inc=1, device_id=(gx, (gy + i) & 15), device_id_type=MESH)
    for i in range(1, 8):
        pl.semaphore_signal(barrier, inc=1, device_id=((gx + i) & 7, gy), device_id_type=MESH)
    between()
    pl.semaphore_wait(barrier, 22)
    for i in range(1, 8):
        pl.semaphore_signal(line_sem, inc=1, device_id=((gx + i) & 7, gy), device_id_type=MESH)
    pl.semaphore_wait(line_sem, 7)


def exchange_body(route_ref, all_hbm, inbox, relay, boxes, corners, back, ve, off_ref, frc_ref, load, stage, tables, wxs, line_sem, send, recv, pass_sem, take_sem, rim_send, rim_recv):
    here = position()
    peers = neighbours()
    velocity_in = pltpu.make_async_copy(all_hbm.at[2].reshape(3, 16, 8, 128), ve.at[:, pl.ds(2, 16), pl.ds(8, 8), :], load.at[2])
    velocity_in.start()
    loads = [pltpu.make_async_copy(all_hbm.at[0], off_ref, load.at[0]), pltpu.make_async_copy(all_hbm.at[1], frc_ref, load.at[1])]
    for copy in loads:
        copy.start()

    def prepare():
        first, second = routes(steps_to(route_ref[3:4], here), route_ref[4:5])
        back[:, :128] = first.T
        back[:, 128:] = second.T
        for copy in loads:
            copy.wait()
        pack_rows(first, second, off_ref, frc_ref, route_ref, stage)
        velocity_in.wait()

    greet_all(line_sem, prepare)

    def message(chip):
        rows = pl.ds(pl.multiple_of(chip * 32, 32), 26)
        return pltpu.make_async_remote_copy(stage.at[rows], inbox.at[rows], send.at[chip], recv.at[chip], device_id=shifted(chip, here, 1), device_id_type=MESH)

    def onward(group):
        return pltpu.make_async_remote_copy(
            inbox.reshape(64, 32, 128).at[pl.ds(group * 8, 8), pl.ds(13, 13)],
            relay.reshape(64, 16, 128).at[pl.ds(group * 8, 8), pl.ds(0, 13)],
            pass_sem.at[group], take_sem.at[group], device_id=sibling(here), device_id_type=MESH)

    def begin(chip, carry):
        message(chip).start()
        return carry

    lax.fori_loop(1, 64, begin, 0, unroll=7)
    rims = []
    for k, (dx, dy) in enumerate(SIDES):
        width = 2 if k < 4 else 1
        copy = pltpu.make_async_remote_copy(box(ve, near(dx, 16, width), near(dy, 8, width), 2, 8),
                                            box(ve, there(dx, 16, width), there(dy, 8, width), 2, 8),
                                            rim_send.at[k], rim_recv.at[k], device_id=peers[k], device_id_type=MESH)
        copy.start()
        rims.append(copy)
    inbox[0:32] = stage[0:32]
    iota8 = lax.broadcasted_iota(jnp.int32, (8, 128), 0).astype(F32) - 3.0
    iota16 = lax.broadcasted_iota(jnp.int32, (16, 128), 0).astype(F32) - 3.0
    tabs = [tables.at[n] for n in range(4)]

    def work(held, pitch, group, shift):
        for u in range(8):
            at = group * (8 * pitch) + u * pitch
            t = held[pl.ds(at, 8), :]
            whole = jnp.floor(t)
            f = t - whole
            for n, v in enumerate((whole, (3.0 - 2.0 * f) * 0.125, (1.0 + 2.0 * f) * 0.125, jnp.sqrt(1.0 + 4.0 * f * (1.0 - f)) * 0.125)):
                tables[n, u * 8:u * 8 + 8, :] = v
        for u in range(8):
            at = group * (8 * pitch) + u * pitch
            for r in range(2):
                row = u * 8 + r * 3
                y0 = held[pl.ds(at + 6, 1), r * 3 + 1:r * 3 + 2]
                B = plane_of(y0, row, tabs, wxs.at[u * 2 + r], iota8, iota16)
                wz = weight(iota8, row + 2, tabs)
                A = jnp.concatenate([held[pl.ds(at + 7 + r * 3 + c, 1), :] * wz for c in range(3)], axis=0)
                ah, al = split(A)
                bh, bl = split(B)
                both = jnp.concatenate([ah, al], 0)
                o = lax.dot_general(jnp.concatenate([both, both], 1), jnp.concatenate([bh, bl], 1), (((1,), (1,)), ((), ())), preferred_element_type=F32)
                boxes[(shift + group * 8 + u) * 2 + r] = o[:24] + o[24:]

    for chip in range(1, 8):
        message(chip).wait_recv()
    onward(0).start()
    work(inbox, 32, 0, 0)

    def turn(group, carry):
        for u in range(8):
            message(group * 8 + u).wait_recv()
        onward(group).start()
        work(inbox, 32, group, 0)
        onward(group - 1).wait_recv()
        work(relay, 16, group - 1, 64)
        return carry

    lax.fori_loop(1, 8, turn, 0)
    onward(7).wait_recv()
    work(relay, 16, 7, 64)
    gathered = jnp.concatenate([inbox[pl.ds(d * 32 + 6, 8, stride=32), :] for d in range(0, 64, 8)] + [relay[pl.ds(d * 16 + 6, 8, stride=16), :] for d in range(0, 64, 8)], axis=0)
    corners[...] = gathered.T[0:8].astype(jnp.int32)

    def end(chip, carry):
        message(chip).wait_send()
        return carry

    lax.fori_loop(1, 64, end, 0)
    for group in range(8):
        onward(group).wait_send()
    for copy in rims:
        copy.wait()


def exchange_call(counts, owner, offsets, forces, base, velocity):
    shapes = ((2048, 128), F32), ((1024, 128), F32), ((256, 24, 128), F32), ((8, 128), jnp.int32), ((128, 256), F32), ((3, 20, 24, 128), F32)
    return pl.pallas_call(
        exchange_body,
        out_shape=tuple(jax.ShapeDtypeStruct(*s) for s in shapes),
        in_specs=[VM, ANY],
        out_specs=(VM,) * 6,
        scratch_shapes=[pltpu.VMEM((3, 128, 128), F32), pltpu.VMEM((3, 128, 128), F32), pltpu.SemaphoreType.DMA((3,))] + [
            pltpu.VMEM((2048, 128), F32),
            pltpu.VMEM((4, 64, 128), F32),
            pltpu.VMEM((16, 8, 128), F32),
            pltpu.SemaphoreType.REGULAR,
            pltpu.SemaphoreType.DMA((64,)),
            pltpu.SemaphoreType.DMA((64,)),
            pltpu.SemaphoreType.DMA((8,)),
            pltpu.SemaphoreType.DMA((8,)),
            pltpu.SemaphoreType.DMA((8,)),
            pltpu.SemaphoreType.DMA((8,)),
        ],
        compiler_params=pltpu.CompilerParams(vmem_limit_bytes=40 * 2**20, collective_id=1, has_side_effects=True),
        name="exchange",
    )(jnp.concatenate([base, owner[None], jnp.broadcast_to(counts[:, None], (1, 128))], axis=0), jnp.stack([offsets, forces, velocity.reshape(3, 128, 128)]))


def deposit_body(corners_s, boxes, out, acc, tot):
    def zero(x, carry):
        acc[x] = jnp.zeros((3, 128, 128), F32)
        return carry

    lax.fori_loop(0, 16, zero, 0)

    def add(k, carry):
        for r in range(2):
            x0 = corners_s[r * 3, k]
            z0 = jnp.maximum(corners_s[r * 3 + 2, k] - 3, 0)
            for c in range(3):
                acc[x0, c, pl.ds(z0, 8), :] += boxes[k * 2 + r, c * 8:c * 8 + 8]
        return carry

    lax.fori_loop(0, 128, add, 0, unroll=4)
    lane = lax.broadcasted_iota(jnp.int32, (128, 128), 1)
    for c in range(3):
        filled = [False] * 3
        for t in range(2):
            for r in range(8):
                a = acc[8 * t + r, c]
                if r == 0:
                    parts = [(t, a)]
                else:
                    a = pltpu.roll(a, 16 * r, 1)
                    parts = [(t, jnp.where(lane >= 16 * r, a, 0.0)), (t + 1, jnp.where(lane < 16 * r, a, 0.0))]
                for k, v in parts:
                    tot[k] = tot[k] + v if filled[k] else v
                    filled[k] = True
        for k in range(3):
            out[c, 8 * k:8 * k + 8] = tot[k].T.reshape(8, 16, 128)


def deposit_call(corners, boxes):
    return pl.pallas_call(
        deposit_body,
        out_shape=jax.ShapeDtypeStruct((3, 24, 16, 128), F32),
        in_specs=[SM, VM],
        out_specs=VM,
        scratch_shapes=[pltpu.VMEM((16, 3, 128, 128), F32), pltpu.VMEM((3, 128, 128), F32)],
        compiler_params=pltpu.CompilerParams(vmem_limit_bytes=40 * 2**20),
        name="deposit",
    )(corners, boxes)


MESH = pl.DeviceIdType.MESH
SIDES = ((1, 0), (-1, 0), (0, 1), (0, -1), (1, 1), (1, -1), (-1, 1), (-1, -1))


def neighbours():
    gx, gy = lax.axis_index("gx"), lax.axis_index("gy")
    nx, ny = lax.axis_size("gx"), lax.axis_size("gy")
    return [(lax.rem(gx + dx + nx, nx), lax.rem(gy + dy + ny, ny)) for dx, dy in SIDES]


def near(step, size, width):
    return (0, size) if step == 0 else ((size - width, width) if step > 0 else (0, width))


def there(step, size, width):
    return (0, size) if step == 0 else ((-width, width) if step > 0 else (size, width))


def box(ref, xs, ys, x_at, y_at):
    return ref.at[..., pl.ds(xs[0] + x_at, xs[1]), pl.ds(ys[0] + y_at, ys[1]), :]


def inward(lane, v):
    above = jnp.where(lane == 127, 0.0, pltpu.roll(v, 127, 1))
    below = jnp.where(lane == 0, 0.0, pltpu.roll(v, 1, 1))
    return above, below


def project_body(unroll, chunks, corners_s, inbox, relay, w_ref, ve, new_ref, prs_ref, direct, passed, v_ref, pe, src, pa, pb, fold, tables, wxs, planes, depths, cop, ans, line_sem, send, recv, out_sem, in_sem, pass_sem, take_sem):
    here = position()
    peers = neighbours()
    gx, gy = lax.axis_index("gx"), lax.axis_index("gy")
    barrier = pltpu.get_barrier_semaphore()
    fold[...] = jnp.zeros(fold.shape, F32)
    for i in range(1, 16):
        pl.semaphore_signal(barrier, inc=1, device_id=(gx, (gy + i) & 15), device_id_type=MESH)
    for i in range(1, 8):
        pl.semaphore_signal(barrier, inc=1, device_id=((gx + i) & 7, gy), device_id_type=MESH)
    iota8 = lax.broadcasted_iota(jnp.int32, (8, 128), 0).astype(F32) - 3.0
    iota16 = lax.broadcasted_iota(jnp.int32, (16, 128), 0).astype(F32) - 3.0

    def weigh(begin, end):
        held, pitch, shift = (inbox, 32, 0) if begin < 64 else (relay, 16, 64)

        def turn(t, carry):
            for u in range(unroll):
                k = t * unroll + u
                rows = pl.ds(u * 8, 8)
                v = held[pl.ds((k - shift) * pitch, 8), :]
                whole = jnp.floor(v)
                f = v - whole
                for n, v in enumerate((whole, (3.0 - 2.0 * f) * 0.125, (1.0 + 2.0 * f) * 0.125, jnp.sqrt(1.0 + 4.0 * f * (1.0 - f)) * 0.125)):
                    tables[n, rows, :] = v
                for r in range(2):
                    row, p = u * 8 + r * 3, k * 2 + r
                    tabs = [tables.at[n] for n in range(4)]
                    bh, bl = split(plane_of(corners_s[r * 3 + 1, k].astype(F32), row, tabs, wxs.at[u * 2 + r], iota8, iota16))
                    planes[p, :128] = bh
                    planes[p, 128:] = bl
                    depths[p] = weight(iota8, row + 2, tabs)
            return carry

        lax.fori_loop(begin // unroll, end // unroll, turn, 0)

    weigh(chunks[0], chunks[1])
    pl.semaphore_wait(barrier, 22)
    for i in range(1, 8):
        pl.semaphore_signal(line_sem, inc=1, device_id=((gx + i) & 7, gy), device_id_type=MESH)
    started = []

    def push(source, target, k):
        n = len(started)
        copy = pltpu.make_async_remote_copy(source, target, send.at[n], recv.at[n], device_id=peers[k], device_id_type=MESH)
        copy.start()
        started.append(copy)
        return copy

    first = []
    for k, (dx, dy) in enumerate(SIDES):
        if k == 4:
            pl.semaphore_wait(line_sem, 7)
        xs = (2, 18) if dx == 0 else ((18, 4) if dx > 0 else (0, 4))
        ys = (2, 10) if dy == 0 else ((10, 4) if dy > 0 else (0, 4))
        xd = (0, 18) if dx == 0 else ((0, 4) if dx > 0 else (14, 4))
        yd = (2, 10) if dy == 0 else ((2, 4) if dy > 0 else (8, 4))
        layer = 0 if dy == 0 else (1 if dx == 0 else 2)
        first.append(push(w_ref.at[:, pl.ds(xs[0], xs[1]), pl.ds(ys[0], ys[1]), :],
                          fold.at[layer, :, pl.ds(xd[0], xd[1]), pl.ds(yd[0], yd[1]), :], k))
    weigh(chunks[1], chunks[2])
    for copy in first:
        copy.wait_recv()
    lane = lax.broadcasted_iota(jnp.int32, (8, 128), 1)

    def provide_rows(x, s):
        here_ = pl.ds(8 + s, 8)
        at = pl.ds(3 + s, 8)
        for c in range(3):
            v = ve[c, x + 2, here_, :]
            above, below = inward(lane, v)
            lap = (ve[c, x + 3, here_, :] + ve[c, x + 1, here_, :]) + (ve[c, x + 2, 9 + s:17 + s, :] + ve[c, x + 2, 7 + s:15 + s, :]) + (above + below) - 6.0 * v
            force = w_ref[c, x + 3, at, :] + fold[0, c, x + 1, at, :] + fold[1, c, x + 1, at, :] + fold[2, c, x + 1, at, :]
            pe[c, x + 8, here_, :] = v + time_step * (viscosity * lap + force)

    def provide(x, carry):
        provide_rows(x, -1)
        provide_rows(x, 1)
        return carry

    lax.fori_loop(0, 16, provide, 0, unroll=4)
    provide_rows(-1, 0)
    provide_rows(16, 0)

    def diverge(x, carry):
        above, below = inward(lane, pe[2, x + 8, 8:16, :])
        total = (pe[0, x + 9, 8:16, :] - pe[0, x + 7, 8:16, :]) + (pe[1, x + 8, 9:17, :] - pe[1, x + 8, 7:15, :]) + (above - below)
        src[x + 8, 8:16, :] = total * (0.5 / time_step)
        return carry

    lax.fori_loop(0, 16, diverge, 0, unroll=16)

    third = [push(box(src, near(dx, 16, 7), near(dy, 8, 7), 8, 8),
                  box(src, there(dx, 16, 7), there(dy, 8, 7), 8, 8), k) for k, (dx, dy) in enumerate(SIDES)]
    fourth = []
    for k, (dx, dy) in enumerate(SIDES):
        if k < 4:
            xs = (0, 16) if dx == 0 else ((13, 2) if dx > 0 else (1, 2))
            ys = (0, 8) if dy == 0 else ((5, 2) if dy > 0 else (1, 2))
            xd = (0, 16) if dx == 0 else ((-3, 2) if dx > 0 else (17, 2))
            yd = (0, 8) if dy == 0 else ((-3, 2) if dy > 0 else (9, 2))
        else:
            xs, ys, xd, yd = near(dx, 16, 3), near(dy, 8, 3), there(dx, 16, 3), there(dy, 8, 3)
        fourth.append(push(box(pe, xs, ys, 8, 8), box(pe, xd, yd, 8, 8), k))
    weigh(chunks[2], chunks[3])
    for copy in third:
        copy.wait_recv()

    def relax(old, new, reach, starts, first_sweep):
        scale = -1.0 / 6.0 if first_sweep else 1.0

        def step(x, carry):
            for s in starts:
                here = pl.ds(s, 8)
                v = old[x, here, :] * scale
                above, below = inward(lane, v)
                total = (old[x + 1, here, :] + old[x - 1, here, :]) + (old[x, s + 1:s + 9, :] + old[x, s - 1:s + 7, :])
                new[x, here, :] = (total * scale + (above + below) - src[x, here, :]) * (1.0 / 6.0)
            return carry

        lax.fori_loop(8 - reach, 24 + reach, step, 0, unroll=(16 + 2 * reach) // 2)

    relax(src, pa, 6, (2, 8, 14), True)
    relax(pa, pb, 5, (3, 8, 13), False)
    relax(pb, pa, 4, (4, 12), False)
    for copy in fourth:
        copy.wait_recv()
    v_ref[:, :, 8:16, :] = jnp.zeros((3, 24, 8, 128), F32)
    v_ref[:, 22:24, 0:8, :] = jnp.zeros((3, 2, 8, 128), F32)

    def finish(x, carry):
        for s in (5, 11):
            here = pl.ds(s, 8)
            above, below = inward(lane, pa[x, here, :])
            grad = (pa[x + 1, here, :] - pa[x - 1, here, :], pa[x, s + 1:s + 9, :] - pa[x, s - 1:s + 7, :], above - below)
            for c in range(3):
                v_ref[c, x - 5, pl.ds(s - 5, 8), :] = pe[c, x, here, :] - (0.5 * time_step) * grad[c]
        return carry

    lax.fori_loop(5, 27, finish, 0, unroll=11)
    new_ref[...] = v_ref[:, 3:19, 3:11, :]
    prs_ref[...] = pa[8:24, 8:16, :]


    for c in range(3):
        tiles = [v_ref[c, 8 * k:8 * k + 8].reshape(128, 128).T for k in range(3)]
        wide = lax.broadcasted_iota(jnp.int32, (128, 128), 1)
        for r in range(8):
            if r == 0:
                cop[0, c], cop[8, c] = tiles[0], tiles[1]
            else:
                ro = [pltpu.roll(x, 128 - 16 * r, 1) for x in tiles]
                for t in range(2):
                    cop[8 * t + r, c] = jnp.where(wide < 128 - 16 * r, ro[t], ro[t + 1])

    def message(chip):
        rows = pl.ds(pl.multiple_of(chip * 16, 16), 12)
        return pltpu.make_async_remote_copy(ans.at[rows], direct.at[rows], out_sem.at[chip], in_sem.at[chip], device_id=shifted(chip, here, -1), device_id_type=MESH)

    def onward(group):
        return pltpu.make_async_remote_copy(
            direct.reshape(64, 16, 128).at[pl.ds(group * 16, 16), pl.ds(6, 6)],
            passed.reshape(64, 8, 128).at[pl.ds(group * 16, 16), pl.ds(0, 6)],
            pass_sem.at[group], take_sem.at[group], device_id=sibling(here), device_id_type=MESH)

    def work(chips):
        for chip in chips:
            for kc in range(2):
                k = chip + 64 * kc
                for r in range(2):
                    p = k * 2 + r
                    x0 = corners_s[r * 3, k]
                    z0 = jnp.maximum(corners_s[r * 3 + 2, k] - 3, 0)
                    ah, al = split(jnp.concatenate([cop[x0, c, pl.ds(z0, 8), :] for c in range(3)], axis=0))
                    both = jnp.concatenate([ah, al], 0)
                    o = jnp.dot(jnp.concatenate([both, both], 1), planes[p], preferred_element_type=F32)
                    o = o[:24] + o[24:]
                    wz = depths[p]
                    for c in range(3):
                        ans[pl.ds(chip * 16 + kc * 6 + r * 3 + c, 1), :] = jnp.sum(o[8 * c:8 * c + 8] * wz, axis=0, keepdims=True)

    work(list(range(4)))
    for chip in range(1, 4):
        message(chip).start()

    def turn(t, carry):
        chips = [t * 4 + u for u in range(4)]
        work(chips)
        for chip in chips:
            message(chip).start()
        return carry

    lax.fori_loop(1, 16, turn, 0)
    direct[0:16] = ans[0:16]
    for group in range(4):
        for chip in range(max(group * 16, 1), group * 16 + 16):
            message(chip).wait_recv()
        onward(group).start()
    for group in range(4):
        onward(group).wait_recv()

    def end(chip, carry):
        message(chip).wait_send()
        return carry

    lax.fori_loop(1, 64, end, 0)
    for group in range(4):
        onward(group).wait_send()
    for copy in started:
        copy.wait_send()


def project_call(corners, inbox, relay, widened, moving, unroll=4, chunks=(0, 24, 64, 128)):
    shapes = (3, 16, 8, 128), (16, 8, 128), (1024, 128), (512, 128)
    return pl.pallas_call(
        functools.partial(project_body, unroll, chunks),
        out_shape=tuple(jax.ShapeDtypeStruct(s, F32) for s in shapes),
        in_specs=[SM, VM, VM, VM, VM],
        out_specs=(VM,) * 4,
        scratch_shapes=[
            pltpu.VMEM((3, 24, 16, 128), F32),
            pltpu.VMEM((3, 32, 24, 128), F32),
            pltpu.VMEM((32, 24, 128), F32),
            pltpu.VMEM((32, 24, 128), F32),
            pltpu.VMEM((32, 24, 128), F32),
            pltpu.VMEM((3, 3, 18, 16, 128), F32),
            pltpu.VMEM((4, 8 * unroll, 128), F32),
            pltpu.VMEM((2 * unroll, 8, 128), F32),
            pltpu.VMEM((256, 256, 128), BF),
            pltpu.VMEM((256, 8, 128), F32),
            pltpu.VMEM((16, 3, 128, 128), F32),
            pltpu.VMEM((1024, 128), F32),
            pltpu.SemaphoreType.REGULAR,
            pltpu.SemaphoreType.DMA((32,)),
            pltpu.SemaphoreType.DMA((32,)),
            pltpu.SemaphoreType.DMA((64,)),
            pltpu.SemaphoreType.DMA((64,)),
            pltpu.SemaphoreType.DMA((4,)),
            pltpu.SemaphoreType.DMA((4,)),
        ],
        compiler_params=pltpu.CompilerParams(vmem_limit_bytes=40 * 2**20, collective_id=0, has_side_effects=True),
        name="project",
    )(corners, inbox, relay, widened, moving)


def finish_body(back, direct, passed, new_ref, prs_ref, out_new, out_prs, out, sems):
    copies = [pltpu.make_async_copy(new_ref, out_new, sems.at[0]), pltpu.make_async_copy(prs_ref, out_prs, sems.at[1])]
    for copy in copies:
        copy.start()
    pick = back[...].astype(BF)
    for c in range(3):
        data = jnp.concatenate([box[pl.ds(r * 3 + c, 64, stride=pitch), :] for r in range(2) for box, pitch in ((direct, 16), (passed, 8))], axis=0)
        got = jnp.dot(pick, jnp.concatenate(split3(data), axis=1), preferred_element_type=F32)
        out[c] = got[:, :128] + (got[:, 128:256] + got[:, 256:])
    for copy in copies:
        copy.wait()


def finish_call(back, direct, passed, new, pressure):
    shapes = (3, 16, 8, 128), (16, 8, 128), (3, 128, 128)
    return pl.pallas_call(
        finish_body,
        out_shape=tuple(jax.ShapeDtypeStruct(s, F32) for s in shapes),
        in_specs=[VM] * 5,
        out_specs=(ANY, ANY, VM),
        scratch_shapes=[pltpu.SemaphoreType.DMA((2,))],
        compiler_params=pltpu.CompilerParams(vmem_limit_bytes=32 * 2**20),
        name="finish",
    )(back, direct, passed, new, pressure)


def shards(velocity, offsets, forces, owner, base, counts):
    inbox, relay, boxes, corners, back, moving = exchange_call(counts, owner, offsets, forces, base, velocity)
    widened = deposit_call(corners, boxes)
    new_velocity, pressure, direct, passed = project_call(corners, inbox, relay, widened, moving)
    return finish_call(back, direct, passed, new_velocity, pressure)


def solution(mesh):
    return jax.shard_map(
        shards,
        mesh=mesh,
        in_specs=(
            P(None, "gx", "gy", None),
            P(None, ("gx", "gy"), None),
            P(None, ("gx", "gy"), None),
            P(("gx", "gy")),
            P(None, ("gx", "gy")),
            P(("gx", "gy")),
        ),
        out_specs=(P(None, "gx", "gy", None), P("gx", "gy", None), P(None, ("gx", "gy"), None)),
        check_vma=False,
    )
```

```python
import functools
import jax, jax.numpy as jnp
from jax import lax
from jax.experimental import pallas as pl
from jax.experimental.pallas import tpu as pltpu
from jax.sharding import PartitionSpec as P

time_step = 0.5
viscosity = 0.1

F32 = jnp.float32
BF = jnp.bfloat16

def split(v):
    hi = v.astype(BF)
    lo = (v - hi.astype(F32)).astype(BF)
    return hi, lo


def weight(cells, row, tabs):
    fl, a1, a2, q8 = [t[pl.ds(row, 1), :] for t in tabs]
    e = cells - fl
    s = jnp.where(e < 0.5, a1, a2)
    g = e * (e - 1.0)
    return jnp.where(g < 1.0, s + q8, jnp.where(g < 3.0, s - q8, 0.0))


def plane_of(y0, row, tabs, wxs, iota8, iota16):
    wxs[...] = weight(iota8, row, tabs)
    wy = weight(iota16 - y0, row + 1, tabs)
    return jnp.concatenate([wxs[pl.ds(i, 1), :] * wy for i in range(8)], axis=0)


def split3(v):
    hi = v.astype(BF)
    rest = v - hi.astype(F32)
    mid = rest.astype(BF)
    return hi, mid, (rest - mid.astype(F32)).astype(BF)


def routes(owner_row, count):
    rows = lax.broadcasted_iota(jnp.int32, (128, 128), 0)
    slots = lax.broadcasted_iota(jnp.int32, (128, 128), 1)
    match = jnp.where((owner_row == rows) & (slots < count), 1.0, 0.0)
    before = jnp.where(rows < slots, 1.0, 0.0)
    rank = jnp.dot(match.astype(BF), before.astype(BF), preferred_element_type=F32)
    return jnp.where(rank < 0.5, match, 0.0), jnp.where(rank < 0.5, 0.0, match)


def spread_rows(stage, row, values):
    for d in range(0, 128, 8):
        stage[pl.ds(d % 64 * 32 + d // 64 * 13 + row, 8, stride=32), :] = values[d:d + 8]


def pack_rows(first, second, off_ref, frc_ref, base_ref, stage):
    both = jnp.concatenate([first, second], axis=0).astype(BF)
    for q in range(6):
        data = off_ref[q] if q < 3 else frc_ref[q - 3]
        parts = jnp.concatenate(split3(data), axis=1)
        got = jnp.dot(both, parts, preferred_element_type=F32)
        got = got[:, :128] + (got[:, 128:256] + got[:, 256:])
        for r in range(2):
            spread_rows(stage, (q // 3) * 7 + r * 3 + q % 3, got[r * 128:r * 128 + 128])
    rows = base_ref[0:3].astype(F32)
    none = jnp.zeros((122, 128), F32)
    blank = jnp.zeros((3, 128), F32)
    dims = (((1,), (1,)), ((), ()))
    one = jnp.concatenate([rows, blank, none], axis=0).astype(BF)
    two = jnp.concatenate([blank, rows, none], axis=0).astype(BF)
    corner = lax.dot_general(both[:128], one, dims, preferred_element_type=F32)
    corner += lax.dot_general(both[128:], two, dims, preferred_element_type=F32)
    spread_rows(stage, 6, corner)


VM = pl.BlockSpec(memory_space=pltpu.VMEM)
SM = pl.BlockSpec(memory_space=pltpu.SMEM)
ANY = pl.BlockSpec(memory_space=pltpu.HBM)


def position():
    gx, gy = lax.axis_index("gx"), lax.axis_index("gy")
    return gx >> 1, gx & 1, gy >> 2, gy & 3


def shifted(chip, here, sign):
    y, core, z, x = here
    kx, by, bz = chip & 3, (chip >> 2) & 3, chip >> 4
    ky, kz = (by + 3 * kx) & 3, (bz + by + kx) & 3
    if sign < 0:
        kx, ky, kz = 4 - kx, 4 - ky, 4 - kz
    return (((y + ky) & 3) * 2 + core, ((z + kz) & 3) * 4 + ((x + kx) & 3))


def sibling(here):
    y, core, z, x = here
    return (y * 2 + 1 - core, z * 4 + x)


def steps_to(owner, here):
    y, core, z, x = here
    row, column = owner >> 4, owner & 15
    kc, ky = ((row & 1) - core) & 1, ((row >> 1) - y) & 3
    kz, kx = ((column >> 2) - z) & 3, ((column & 3) - x) & 3
    by = (ky - 3 * kx) & 3
    return kx + 4 * by + 16 * ((kz - by - kx) & 3) + 64 * kc


def greet_all(line_sem, between):
    gx, gy = lax.axis_index("gx"), lax.axis_index("gy")
    barrier = pltpu.get_barrier_semaphore()
    for i in range(1, 16):
        pl.semaphore_signal(barrier, inc=1, device_id=(gx, (gy + i) & 15), device_id_type=MESH)
    for i in range(1, 8):
        pl.semaphore_signal(barrier, inc=1, device_id=((gx + i) & 7, gy), device_id_type=MESH)
    between()
    pl.semaphore_wait(barrier, 22)
    for i in range(1, 8):
        pl.semaphore_signal(line_sem, inc=1, device_id=((gx + i) & 7, gy), device_id_type=MESH)
    pl.semaphore_wait(line_sem, 7)


def exchange_body(route_ref, all_hbm, inbox, relay, boxes, corners, back, ve, off_ref, frc_ref, load, stage, tables, wxs, line_sem, send, recv, pass_sem, take_sem, rim_send, rim_recv):
    here = position()
    peers = neighbours()
    velocity_in = pltpu.make_async_copy(all_hbm.at[2].reshape(3, 16, 8, 128), ve.at[:, pl.ds(2, 16), pl.ds(8, 8), :], load.at[2])
    velocity_in.start()
    loads = [pltpu.make_async_copy(all_hbm.at[0], off_ref, load.at[0]), pltpu.make_async_copy(all_hbm.at[1], frc_ref, load.at[1])]
    for copy in loads:
        copy.start()

    def prepare():
        first, second = routes(steps_to(route_ref[3:4], here), route_ref[4:5])
        back[:, :128] = first.T
        back[:, 128:] = second.T
        for copy in loads:
            copy.wait()
        pack_rows(first, second, off_ref, frc_ref, route_ref, stage)
        velocity_in.wait()

    greet_all(line_sem, prepare)

    def message(chip):
        rows = pl.ds(pl.multiple_of(chip * 32, 32), 26)
        return pltpu.make_async_remote_copy(stage.at[rows], inbox.at[rows], send.at[chip], recv.at[chip], device_id=shifted(chip, here, 1), device_id_type=MESH)

    def onward(group):
        return pltpu.make_async_remote_copy(
            inbox.reshape(64, 32, 128).at[pl.ds(group * 8, 8), pl.ds(13, 13)],
            relay.reshape(64, 16, 128).at[pl.ds(group * 8, 8), pl.ds(0, 13)],
            pass_sem.at[group], take_sem.at[group], device_id=sibling(here), device_id_type=MESH)

    def begin(chip, carry):
        message(chip).start()
        return carry

    lax.fori_loop(1, 64, begin, 0, unroll=7)
    rims = []
    for k, (dx, dy) in enumerate(SIDES):
        width = 2 if k < 4 else 1
        copy = pltpu.make_async_remote_copy(box(ve, near(dx, 16, width), near(dy, 8, width), 2, 8),
                                            box(ve, there(dx, 16, width), there(dy, 8, width), 2, 8),
                                            rim_send.at[k], rim_recv.at[k], device_id=peers[k], device_id_type=MESH)
        copy.start()
        rims.append(copy)
    inbox[0:32] = stage[0:32]
    iota8 = lax.broadcasted_iota(jnp.int32, (8, 128), 0).astype(F32) - 3.0
    iota16 = lax.broadcasted_iota(jnp.int32, (16, 128), 0).astype(F32) - 3.0
    tabs = [tables.at[n] for n in range(4)]

    def work(held, pitch, group, shift):
        for u in range(8):
            at = group * (8 * pitch) + u * pitch
            t = held[pl.ds(at, 8), :]
            whole = jnp.floor(t)
            f = t - whole
            for n, v in enumerate((whole, (3.0 - 2.0 * f) * 0.125, (1.0 + 2.0 * f) * 0.125, jnp.sqrt(1.0 + 4.0 * f * (1.0 - f)) * 0.125)):
                tables[n, u * 8:u * 8 + 8, :] = v
        for u in range(8):
            at = group * (8 * pitch) + u * pitch
            for r in range(2):
                row = u * 8 + r * 3
                y0 = held[pl.ds(at + 6, 1), r * 3 + 1:r * 3 + 2]
                B = plane_of(y0, row, tabs, wxs.at[u * 2 + r], iota8, iota16)
                wz = weight(iota8, row + 2, tabs)
                A = jnp.concatenate([held[pl.ds(at + 7 + r * 3 + c, 1), :] * wz for c in range(3)], axis=0)
                ah, al = split(A)
                bh, bl = split(B)
                both = jnp.concatenate([ah, al], 0)
                o = lax.dot_general(jnp.concatenate([both, both], 1), jnp.concatenate([bh, bl], 1), (((1,), (1,)), ((), ())), preferred_element_type=F32)
                boxes[(shift + group * 8 + u) * 2 + r] = o[:24] + o[24:]

    for chip in range(1, 8):
        message(chip).wait_recv()
    onward(0).start()
    work(inbox, 32, 0, 0)

    def turn(group, carry):
        for u in range(8):
            message(group * 8 + u).wait_recv()
        onward(group).start()
        work(inbox, 32, group, 0)
        onward(group - 1).wait_recv()
        work(relay, 16, group - 1, 64)
        return carry

    lax.fori_loop(1, 8, turn, 0)
    onward(7).wait_recv()
    work(relay, 16, 7, 64)
    gathered = jnp.concatenate([inbox[pl.ds(d * 32 + 6, 8, stride=32), :] for d in range(0, 64, 8)] + [relay[pl.ds(d * 16 + 6, 8, stride=16), :] for d in range(0, 64, 8)], axis=0)
    corners[...] = gathered.T[0:8].astype(jnp.int32)

    def end(chip, carry):
        message(chip).wait_send()
        return carry

    lax.fori_loop(1, 64, end, 0)
    for group in range(8):
        onward(group).wait_send()
    for copy in rims:
        copy.wait()


def exchange_call(counts, owner, offsets, forces, base, velocity):
    shapes = ((2048, 128), F32), ((1024, 128), F32), ((256, 24, 128), F32), ((8, 128), jnp.int32), ((128, 256), F32), ((3, 20, 24, 128), F32)
    return pl.pallas_call(
        exchange_body,
        out_shape=tuple(jax.ShapeDtypeStruct(*s) for s in shapes),
        in_specs=[VM, ANY],
        out_specs=(VM,) * 6,
        scratch_shapes=[pltpu.VMEM((3, 128, 128), F32), pltpu.VMEM((3, 128, 128), F32), pltpu.SemaphoreType.DMA((3,))] + [
            pltpu.VMEM((2048, 128), F32),
            pltpu.VMEM((4, 64, 128), F32),
            pltpu.VMEM((16, 8, 128), F32),
            pltpu.SemaphoreType.REGULAR,
            pltpu.SemaphoreType.DMA((64,)),
            pltpu.SemaphoreType.DMA((64,)),
            pltpu.SemaphoreType.DMA((8,)),
            pltpu.SemaphoreType.DMA((8,)),
            pltpu.SemaphoreType.DMA((8,)),
            pltpu.SemaphoreType.DMA((8,)),
        ],
        compiler_params=pltpu.CompilerParams(vmem_limit_bytes=40 * 2**20, collective_id=1, has_side_effects=True),
        name="exchange",
    )(jnp.concatenate([base, owner[None], jnp.broadcast_to(counts[:, None], (1, 128))], axis=0), jnp.stack([offsets, forces, velocity.reshape(3, 128, 128)]))


def deposit_body(corners_s, boxes, acc):
    def zero(x, carry):
        acc[x] = jnp.zeros((3, 128, 128), F32)
        return carry

    lax.fori_loop(0, 16, zero, 0)

    def add(k, carry):
        for r in range(2):
            x0 = corners_s[r * 3, k]
            z0 = jnp.maximum(corners_s[r * 3 + 2, k] - 3, 0)
            for c in range(3):
                acc[x0, c, pl.ds(z0, 8), :] += boxes[k * 2 + r, c * 8:c * 8 + 8]
        return carry

    lax.fori_loop(0, 128, add, 0, unroll=4)


def deposit_call(corners, boxes):
    return pl.pallas_call(
        deposit_body,
        out_shape=jax.ShapeDtypeStruct((16, 3, 128, 128), F32),
        in_specs=[SM, VM],
        out_specs=VM,
        compiler_params=pltpu.CompilerParams(vmem_limit_bytes=40 * 2**20),
        name="deposit",
    )(corners, boxes)


MESH = pl.DeviceIdType.MESH
SIDES = ((1, 0), (-1, 0), (0, 1), (0, -1), (1, 1), (1, -1), (-1, 1), (-1, -1))


def neighbours():
    gx, gy = lax.axis_index("gx"), lax.axis_index("gy")
    nx, ny = lax.axis_size("gx"), lax.axis_size("gy")
    return [(lax.rem(gx + dx + nx, nx), lax.rem(gy + dy + ny, ny)) for dx, dy in SIDES]


def near(step, size, width):
    return (0, size) if step == 0 else ((size - width, width) if step > 0 else (0, width))


def there(step, size, width):
    return (0, size) if step == 0 else ((-width, width) if step > 0 else (size, width))


def box(ref, xs, ys, x_at, y_at):
    return ref.at[..., pl.ds(xs[0] + x_at, xs[1]), pl.ds(ys[0] + y_at, ys[1]), :]


def inward(lane, v):
    above = jnp.where(lane == 127, 0.0, pltpu.roll(v, 127, 1))
    below = jnp.where(lane == 0, 0.0, pltpu.roll(v, 1, 1))
    return above, below


def project_body(unroll, chunks, corners_s, inbox, relay, acc, ve, new_ref, prs_ref, direct, passed, w_ref, tot, v_ref, pe, src, pa, pb, fold, tables, wxs, planes, depths, cop, ans, line_sem, send, recv, out_sem, in_sem, pass_sem, take_sem):
    here = position()
    peers = neighbours()
    gx, gy = lax.axis_index("gx"), lax.axis_index("gy")
    barrier = pltpu.get_barrier_semaphore()
    fold[...] = jnp.zeros(fold.shape, F32)
    for i in range(1, 16):
        pl.semaphore_signal(barrier, inc=1, device_id=(gx, (gy + i) & 15), device_id_type=MESH)
    for i in range(1, 8):
        pl.semaphore_signal(barrier, inc=1, device_id=((gx + i) & 7, gy), device_id_type=MESH)
    iota8 = lax.broadcasted_iota(jnp.int32, (8, 128), 0).astype(F32) - 3.0
    iota16 = lax.broadcasted_iota(jnp.int32, (16, 128), 0).astype(F32) - 3.0

    def weigh(begin, end):
        held, pitch, shift = (inbox, 32, 0) if begin < 64 else (relay, 16, 64)

        def turn(t, carry):
            for u in range(unroll):
                k = t * unroll + u
                rows = pl.ds(u * 8, 8)
                v = held[pl.ds((k - shift) * pitch, 8), :]
                whole = jnp.floor(v)
                f = v - whole
                for n, v in enumerate((whole, (3.0 - 2.0 * f) * 0.125, (1.0 + 2.0 * f) * 0.125, jnp.sqrt(1.0 + 4.0 * f * (1.0 - f)) * 0.125)):
                    tables[n, rows, :] = v
                for r in range(2):
                    row, p = u * 8 + r * 3, k * 2 + r
                    tabs = [tables.at[n] for n in range(4)]
                    bh, bl = split(plane_of(corners_s[r * 3 + 1, k].astype(F32), row, tabs, wxs.at[u * 2 + r], iota8, iota16))
                    planes[p, :128] = bh
                    planes[p, 128:] = bl
                    depths[p] = weight(iota8, row + 2, tabs)
            return carry

        lax.fori_loop(begin // unroll, end // unroll, turn, 0)

    wide = lax.broadcasted_iota(jnp.int32, (128, 128), 1)
    for c in range(3):
        filled = [False] * 3
        for t in range(2):
            for r in range(8):
                a = acc[8 * t + r, c]
                if r == 0:
                    parts = [(t, a)]
                else:
                    a = pltpu.roll(a, 16 * r, 1)
                    parts = [(t, jnp.where(wide >= 16 * r, a, 0.0)), (t + 1, jnp.where(wide < 16 * r, a, 0.0))]
                for k, v in parts:
                    tot[k] = tot[k] + v if filled[k] else v
                    filled[k] = True
        for k in range(3):
            w_ref[c, 8 * k:8 * k + 8] = tot[k].T.reshape(8, 16, 128)
    weigh(chunks[0], chunks[1])
    pl.semaphore_wait(barrier, 22)
    for i in range(1, 8):
        pl.semaphore_signal(line_sem, inc=1, device_id=((gx + i) & 7, gy), device_id_type=MESH)
    started = []

    def push(source, target, k):
        n = len(started)
        copy = pltpu.make_async_remote_copy(source, target, send.at[n], recv.at[n], device_id=peers[k], device_id_type=MESH)
        copy.start()
        started.append(copy)
        return copy

    first = []
    for k, (dx, dy) in enumerate(SIDES):
        if k == 4:
            pl.semaphore_wait(line_sem, 7)
        xs = (2, 18) if dx == 0 else ((18, 4) if dx > 0 else (0, 4))
        ys = (2, 10) if dy == 0 else ((10, 4) if dy > 0 else (0, 4))
        xd = (0, 18) if dx == 0 else ((0, 4) if dx > 0 else (14, 4))
        yd = (2, 10) if dy == 0 else ((2, 4) if dy > 0 else (8, 4))
        layer = 0 if dy == 0 else (1 if dx == 0 else 2)
        first.append(push(w_ref.at[:, pl.ds(xs[0], xs[1]), pl.ds(ys[0], ys[1]), :],
                          fold.at[layer, :, pl.ds(xd[0], xd[1]), pl.ds(yd[0], yd[1]), :], k))
    weigh(chunks[1], chunks[2])
    for copy in first:
        copy.wait_recv()
    lane = lax.broadcasted_iota(jnp.int32, (8, 128), 1)

    def provide_rows(x, s):
        here_ = pl.ds(8 + s, 8)
        at = pl.ds(3 + s, 8)
        for c in range(3):
            v = ve[c, x + 2, here_, :]
            above, below = inward(lane, v)
            lap = (ve[c, x + 3, here_, :] + ve[c, x + 1, here_, :]) + (ve[c, x + 2, 9 + s:17 + s, :] + ve[c, x + 2, 7 + s:15 + s, :]) + (above + below) - 6.0 * v
            force = w_ref[c, x + 3, at, :] + fold[0, c, x + 1, at, :] + fold[1, c, x + 1, at, :] + fold[2, c, x + 1, at, :]
            pe[c, x + 8, here_, :] = v + time_step * (viscosity * lap + force)

    def provide(x, carry):
        provide_rows(x, -1)
        provide_rows(x, 1)
        return carry

    lax.fori_loop(0, 16, provide, 0, unroll=4)
    provide_rows(-1, 0)
    provide_rows(16, 0)

    def diverge(x, carry):
        above, below = inward(lane, pe[2, x + 8, 8:16, :])
        total = (pe[0, x + 9, 8:16, :] - pe[0, x + 7, 8:16, :]) + (pe[1, x + 8, 9:17, :] - pe[1, x + 8, 7:15, :]) + (above - below)
        src[x + 8, 8:16, :] = total * (0.5 / time_step)
        return carry

    lax.fori_loop(0, 16, diverge, 0, unroll=16)

    third = [push(box(src, near(dx, 16, 7), near(dy, 8, 7), 8, 8),
                  box(src, there(dx, 16, 7), there(dy, 8, 7), 8, 8), k) for k, (dx, dy) in enumerate(SIDES)]
    fourth = []
    for k, (dx, dy) in enumerate(SIDES):
        if k < 4:
            xs = (0, 16) if dx == 0 else ((13, 2) if dx > 0 else (1, 2))
            ys = (0, 8) if dy == 0 else ((5, 2) if dy > 0 else (1, 2))
            xd = (0, 16) if dx == 0 else ((-3, 2) if dx > 0 else (17, 2))
            yd = (0, 8) if dy == 0 else ((-3, 2) if dy > 0 else (9, 2))
        else:
            xs, ys, xd, yd = near(dx, 16, 3), near(dy, 8, 3), there(dx, 16, 3), there(dy, 8, 3)
        fourth.append(push(box(pe, xs, ys, 8, 8), box(pe, xd, yd, 8, 8), k))
    weigh(chunks[2], chunks[3])
    for copy in third:
        copy.wait_recv()

    def relax(old, new, reach, starts, first_sweep):
        scale = -1.0 / 6.0 if first_sweep else 1.0

        def step(x, carry):
            for s in starts:
                here = pl.ds(s, 8)
                v = old[x, here, :] * scale
                above, below = inward(lane, v)
                total = (old[x + 1, here, :] + old[x - 1, here, :]) + (old[x, s + 1:s + 9, :] + old[x, s - 1:s + 7, :])
                new[x, here, :] = (total * scale + (above + below) - src[x, here, :]) * (1.0 / 6.0)
            return carry

        lax.fori_loop(8 - reach, 24 + reach, step, 0, unroll=(16 + 2 * reach) // 2)

    relax(src, pa, 6, (2, 8, 14), True)
    relax(pa, pb, 5, (3, 8, 13), False)
    relax(pb, pa, 4, (4, 12), False)
    for copy in fourth:
        copy.wait_recv()
    v_ref[:, :, 8:16, :] = jnp.zeros((3, 24, 8, 128), F32)
    v_ref[:, 22:24, 0:8, :] = jnp.zeros((3, 2, 8, 128), F32)

    def finish(x, carry):
        for s in (5, 11):
            here = pl.ds(s, 8)
            above, below = inward(lane, pa[x, here, :])
            grad = (pa[x + 1, here, :] - pa[x - 1, here, :], pa[x, s + 1:s + 9, :] - pa[x, s - 1:s + 7, :], above - below)
            for c in range(3):
                v_ref[c, x - 5, pl.ds(s - 5, 8), :] = pe[c, x, here, :] - (0.5 * time_step) * grad[c]
        return carry

    lax.fori_loop(5, 27, finish, 0, unroll=11)
    new_ref[...] = v_ref[:, 3:19, 3:11, :]
    prs_ref[...] = pa[8:24, 8:16, :]


    for c in range(3):
        tiles = [v_ref[c, 8 * k:8 * k + 8].reshape(128, 128).T for k in range(3)]
        for r in range(8):
            if r == 0:
                cop[0, c], cop[8, c] = tiles[0], tiles[1]
            else:
                ro = [pltpu.roll(x, 128 - 16 * r, 1) for x in tiles]
                for t in range(2):
                    cop[8 * t + r, c] = jnp.where(wide < 128 - 16 * r, ro[t], ro[t + 1])

    def message(chip):
        rows = pl.ds(pl.multiple_of(chip * 16, 16), 12)
        return pltpu.make_async_remote_copy(ans.at[rows], direct.at[rows], out_sem.at[chip], in_sem.at[chip], device_id=shifted(chip, here, -1), device_id_type=MESH)

    def onward(group):
        return pltpu.make_async_remote_copy(
            direct.reshape(64, 16, 128).at[pl.ds(group * 16, 16), pl.ds(6, 6)],
            passed.reshape(64, 8, 128).at[pl.ds(group * 16, 16), pl.ds(0, 6)],
            pass_sem.at[group], take_sem.at[group], device_id=sibling(here), device_id_type=MESH)

    def work(chips):
        for chip in chips:
            for kc in range(2):
                k = chip + 64 * kc
                for r in range(2):
                    p = k * 2 + r
                    x0 = corners_s[r * 3, k]
                    z0 = jnp.maximum(corners_s[r * 3 + 2, k] - 3, 0)
                    ah, al = split(jnp.concatenate([cop[x0, c, pl.ds(z0, 8), :] for c in range(3)], axis=0))
                    both = jnp.concatenate([ah, al], 0)
                    o = jnp.dot(jnp.concatenate([both, both], 1), planes[p], preferred_element_type=F32)
                    o = o[:24] + o[24:]
                    wz = depths[p]
                    for c in range(3):
                        ans[pl.ds(chip * 16 + kc * 6 + r * 3 + c, 1), :] = jnp.sum(o[8 * c:8 * c + 8] * wz, axis=0, keepdims=True)

    work(list(range(8)))
    for chip in range(1, 8):
        message(chip).start()

    def turn(t, carry):
        chips = [t * 8 + u for u in range(8)]
        work(chips)
        for chip in chips:
            message(chip).start()
        return carry

    lax.fori_loop(1, 8, turn, 0)
    direct[0:16] = ans[0:16]
    for group in range(4):
        for chip in range(max(group * 16, 1), group * 16 + 16):
            message(chip).wait_recv()
        onward(group).start()
    for group in range(4):
        onward(group).wait_recv()

    def end(chip, carry):
        message(chip).wait_send()
        return carry

    lax.fori_loop(1, 64, end, 0)
    for group in range(4):
        onward(group).wait_send()
    for copy in started:
        copy.wait_send()


def project_call(corners, inbox, relay, spread, moving, unroll=4, chunks=(0, 0, 64, 128)):
    shapes = (3, 16, 8, 128), (16, 8, 128), (1024, 128), (512, 128)
    return pl.pallas_call(
        functools.partial(project_body, unroll, chunks),
        out_shape=tuple(jax.ShapeDtypeStruct(s, F32) for s in shapes),
        in_specs=[SM, VM, VM, VM, VM],
        out_specs=(VM,) * 4,
        scratch_shapes=[
            pltpu.VMEM((3, 24, 16, 128), F32),
            pltpu.VMEM((3, 128, 128), F32),
            pltpu.VMEM((3, 24, 16, 128), F32),
            pltpu.VMEM((3, 32, 24, 128), F32),
            pltpu.VMEM((32, 24, 128), F32),
            pltpu.VMEM((32, 24, 128), F32),
            pltpu.VMEM((32, 24, 128), F32),
            pltpu.VMEM((3, 3, 18, 16, 128), F32),
            pltpu.VMEM((4, 8 * unroll, 128), F32),
            pltpu.VMEM((2 * unroll, 8, 128), F32),
            pltpu.VMEM((256, 256, 128), BF),
            pltpu.VMEM((256, 8, 128), F32),
            pltpu.VMEM((16, 3, 128, 128), F32),
            pltpu.VMEM((1024, 128), F32),
            pltpu.SemaphoreType.REGULAR,
            pltpu.SemaphoreType.DMA((32,)),
            pltpu.SemaphoreType.DMA((32,)),
            pltpu.SemaphoreType.DMA((64,)),
            pltpu.SemaphoreType.DMA((64,)),
            pltpu.SemaphoreType.DMA((4,)),
            pltpu.SemaphoreType.DMA((4,)),
        ],
        compiler_params=pltpu.CompilerParams(vmem_limit_bytes=40 * 2**20, collective_id=0, has_side_effects=True),
        name="project",
    )(corners, inbox, relay, spread, moving)


def finish_body(back, direct, passed, new_ref, prs_ref, out_new, out_prs, out, sems):
    copies = [pltpu.make_async_copy(new_ref, out_new, sems.at[0]), pltpu.make_async_copy(prs_ref, out_prs, sems.at[1])]
    for copy in copies:
        copy.start()
    pick = back[...].astype(BF)
    for c in range(3):
        data = jnp.concatenate([box[pl.ds(r * 3 + c, 64, stride=pitch), :] for r in range(2) for box, pitch in ((direct, 16), (passed, 8))], axis=0)
        got = jnp.dot(pick, jnp.concatenate(split3(data), axis=1), preferred_element_type=F32)
        out[c] = got[:, :128] + (got[:, 128:256] + got[:, 256:])
    for copy in copies:
        copy.wait()


def finish_call(back, direct, passed, new, pressure):
    shapes = (3, 16, 8, 128), (16, 8, 128), (3, 128, 128)
    return pl.pallas_call(
        finish_body,
        out_shape=tuple(jax.ShapeDtypeStruct(s, F32) for s in shapes),
        in_specs=[VM] * 5,
        out_specs=(ANY, ANY, VM),
        scratch_shapes=[pltpu.SemaphoreType.DMA((2,))],
        compiler_params=pltpu.CompilerParams(vmem_limit_bytes=32 * 2**20),
        name="finish",
    )(back, direct, passed, new, pressure)


def shards(velocity, offsets, forces, owner, base, counts):
    inbox, relay, boxes, corners, back, moving = exchange_call(counts, owner, offsets, forces, base, velocity)
    spread = deposit_call(corners, boxes)
    new_velocity, pressure, direct, passed = project_call(corners, inbox, relay, spread, moving)
    return finish_call(back, direct, passed, new_velocity, pressure)


def solution(mesh):
    return jax.shard_map(
        shards,
        mesh=mesh,
        in_specs=(
            P(None, "gx", "gy", None),
            P(None, ("gx", "gy"), None),
            P(None, ("gx", "gy"), None),
            P(("gx", "gy")),
            P(None, ("gx", "gy")),
            P(("gx", "gy")),
        ),
        out_specs=(P(None, "gx", "gy", None), P("gx", "gy", None), P(None, ("gx", "gy"), None)),
        check_vma=False,
    )
```

```python
import functools
import jax, jax.numpy as jnp
from jax import lax
from jax.experimental import pallas as pl
from jax.experimental.pallas import tpu as pltpu
from jax.sharding import PartitionSpec as P

time_step = 0.5
viscosity = 0.1

F32 = jnp.float32
BF = jnp.bfloat16

def split(v):
    hi = v.astype(BF)
    lo = (v - hi.astype(F32)).astype(BF)
    return hi, lo


def weight(cells, row, tabs):
    fl, a1, a2, q8 = [t[pl.ds(row, 1), :] for t in tabs]
    e = cells - fl
    s = jnp.where(e < 0.5, a1, a2)
    g = e * (e - 1.0)
    return jnp.where(g < 1.0, s + q8, jnp.where(g < 3.0, s - q8, 0.0))


def plane_of(y0, row, tabs, wxs, iota8, iota16):
    wxs[...] = weight(iota8, row, tabs)
    wy = weight(iota16 - y0, row + 1, tabs)
    return jnp.concatenate([wxs[pl.ds(i, 1), :] * wy for i in range(8)], axis=0)


def split3(v):
    hi = v.astype(BF)
    rest = v - hi.astype(F32)
    mid = rest.astype(BF)
    return hi, mid, (rest - mid.astype(F32)).astype(BF)


def routes(owner_row, count):
    rows = lax.broadcasted_iota(jnp.int32, (128, 128), 0)
    slots = lax.broadcasted_iota(jnp.int32, (128, 128), 1)
    match = jnp.where((owner_row == rows) & (slots < count), 1.0, 0.0)
    before = jnp.where(rows < slots, 1.0, 0.0)
    rank = jnp.dot(match.astype(BF), before.astype(BF), preferred_element_type=F32)
    return jnp.where(rank < 0.5, match, 0.0), jnp.where(rank < 0.5, 0.0, match)


def spread_rows(stage, row, values):
    for d in range(0, 128, 8):
        stage[pl.ds(d % 64 * 32 + d // 64 * 13 + row, 8, stride=32), :] = values[d:d + 8]


def pack_rows(first, second, off_ref, frc_ref, base_ref, stage):
    both = jnp.concatenate([first, second], axis=0).astype(BF)
    for q in range(6):
        data = off_ref[q] if q < 3 else frc_ref[q - 3]
        parts = jnp.concatenate(split3(data), axis=1)
        got = jnp.dot(both, parts, preferred_element_type=F32)
        got = got[:, :128] + (got[:, 128:256] + got[:, 256:])
        for r in range(2):
            spread_rows(stage, (q // 3) * 7 + r * 3 + q % 3, got[r * 128:r * 128 + 128])
    rows = base_ref[0:3].astype(F32)
    none = jnp.zeros((122, 128), F32)
    blank = jnp.zeros((3, 128), F32)
    dims = (((1,), (1,)), ((), ()))
    one = jnp.concatenate([rows, blank, none], axis=0).astype(BF)
    two = jnp.concatenate([blank, rows, none], axis=0).astype(BF)
    corner = lax.dot_general(both[:128], one, dims, preferred_element_type=F32)
    corner += lax.dot_general(both[128:], two, dims, preferred_element_type=F32)
    spread_rows(stage, 6, corner)


VM = pl.BlockSpec(memory_space=pltpu.VMEM)
SM = pl.BlockSpec(memory_space=pltpu.SMEM)
ANY = pl.BlockSpec(memory_space=pltpu.HBM)


def position():
    gx, gy = lax.axis_index("gx"), lax.axis_index("gy")
    return gx >> 1, gx & 1, gy >> 2, gy & 3


def shifted(chip, here, sign):
    y, core, z, x = here
    kx, by, bz = chip & 3, (chip >> 2) & 3, chip >> 4
    ky, kz = (by + 3 * kx) & 3, (bz + by + kx) & 3
    if sign < 0:
        kx, ky, kz = 4 - kx, 4 - ky, 4 - kz
    return (((y + ky) & 3) * 2 + core, ((z + kz) & 3) * 4 + ((x + kx) & 3))


def sibling(here):
    y, core, z, x = here
    return (y * 2 + 1 - core, z * 4 + x)


def steps_to(owner, here):
    y, core, z, x = here
    row, column = owner >> 4, owner & 15
    kc, ky = ((row & 1) - core) & 1, ((row >> 1) - y) & 3
    kz, kx = ((column >> 2) - z) & 3, ((column & 3) - x) & 3
    by = (ky - 3 * kx) & 3
    return kx + 4 * by + 16 * ((kz - by - kx) & 3) + 64 * kc


def greet_all(line_sem, between):
    gx, gy = lax.axis_index("gx"), lax.axis_index("gy")
    barrier = pltpu.get_barrier_semaphore()
    for i in range(1, 16):
        pl.semaphore_signal(barrier, inc=1, device_id=(gx, (gy + i) & 15), device_id_type=MESH)
    for i in range(1, 8):
        pl.semaphore_signal(barrier, inc=1, device_id=((gx + i) & 7, gy), device_id_type=MESH)
    between()
    pl.semaphore_wait(barrier, 22)
    for i in range(1, 8):
        pl.semaphore_signal(line_sem, inc=1, device_id=((gx + i) & 7, gy), device_id_type=MESH)
    pl.semaphore_wait(line_sem, 7)


def exchange_body(route_ref, all_hbm, inbox, relay, boxes, corners, back, ve, off_ref, frc_ref, load, stage, tables, wxs, line_sem, send, recv, pass_sem, take_sem, rim_send, rim_recv):
    here = position()
    peers = neighbours()
    velocity_in = pltpu.make_async_copy(all_hbm.at[2].reshape(3, 16, 8, 128), ve.at[:, pl.ds(2, 16), pl.ds(8, 8), :], load.at[2])
    velocity_in.start()
    loads = [pltpu.make_async_copy(all_hbm.at[0], off_ref, load.at[0]), pltpu.make_async_copy(all_hbm.at[1], frc_ref, load.at[1])]
    for copy in loads:
        copy.start()

    def prepare():
        first, second = routes(steps_to(route_ref[3:4], here), route_ref[4:5])
        back[:, :128] = first.T
        back[:, 128:] = second.T
        for copy in loads:
            copy.wait()
        pack_rows(first, second, off_ref, frc_ref, route_ref, stage)
        velocity_in.wait()

    greet_all(line_sem, prepare)

    def message(chip):
        rows = pl.ds(pl.multiple_of(chip * 32, 32), 26)
        return pltpu.make_async_remote_copy(stage.at[rows], inbox.at[rows], send.at[chip], recv.at[chip], device_id=shifted(chip, here, 1), device_id_type=MESH)

    def onward(group):
        return pltpu.make_async_remote_copy(
            inbox.reshape(64, 32, 128).at[pl.ds(group * 8, 8), pl.ds(13, 13)],
            relay.reshape(64, 16, 128).at[pl.ds(group * 8, 8), pl.ds(0, 13)],
            pass_sem.at[group], take_sem.at[group], device_id=sibling(here), device_id_type=MESH)

    def begin(chip, carry):
        message(chip).start()
        return carry

    lax.fori_loop(1, 64, begin, 0, unroll=7)
    rims = []
    for k, (dx, dy) in enumerate(SIDES):
        width = 2 if k < 4 else 1
        copy = pltpu.make_async_remote_copy(box(ve, near(dx, 16, width), near(dy, 8, width), 2, 8),
                                            box(ve, there(dx, 16, width), there(dy, 8, width), 2, 8),
                                            rim_send.at[k], rim_recv.at[k], device_id=peers[k], device_id_type=MESH)
        copy.start()
        rims.append(copy)
    inbox[0:32] = stage[0:32]
    iota8 = lax.broadcasted_iota(jnp.int32, (8, 128), 0).astype(F32) - 3.0
    iota16 = lax.broadcasted_iota(jnp.int32, (16, 128), 0).astype(F32) - 3.0
    tabs = [tables.at[n] for n in range(4)]

    def work(held, pitch, group, shift):
        for u in range(8):
            at = group * (8 * pitch) + u * pitch
            t = held[pl.ds(at, 8), :]
            whole = jnp.floor(t)
            f = t - whole
            for n, v in enumerate((whole, (3.0 - 2.0 * f) * 0.125, (1.0 + 2.0 * f) * 0.125, jnp.sqrt(1.0 + 4.0 * f * (1.0 - f)) * 0.125)):
                tables[n, u * 8:u * 8 + 8, :] = v
        for u in range(8):
            at = group * (8 * pitch) + u * pitch
            for r in range(2):
                row = u * 8 + r * 3
                y0 = held[pl.ds(at + 6, 1), r * 3 + 1:r * 3 + 2]
                B = plane_of(y0, row, tabs, wxs.at[u * 2 + r], iota8, iota16)
                wz = weight(iota8, row + 2, tabs)
                A = jnp.concatenate([held[pl.ds(at + 7 + r * 3 + c, 1), :] * wz for c in range(3)], axis=0)
                ah, al = split(A)
                bh, bl = split(B)
                both = jnp.concatenate([ah, al], 0)
                o = lax.dot_general(jnp.concatenate([both, both], 1), jnp.concatenate([bh, bl], 1), (((1,), (1,)), ((), ())), preferred_element_type=F32)
                boxes[(shift + group * 8 + u) * 2 + r] = o[:24] + o[24:]

    for chip in range(1, 8):
        message(chip).wait_recv()
    onward(0).start()
    work(inbox, 32, 0, 0)

    def turn(group, carry):
        for u in range(8):
            message(group * 8 + u).wait_recv()
        onward(group).start()
        work(inbox, 32, group, 0)
        onward(group - 1).wait_recv()
        work(relay, 16, group - 1, 64)
        return carry

    lax.fori_loop(1, 8, turn, 0)
    onward(7).wait_recv()
    work(relay, 16, 7, 64)
    gathered = jnp.concatenate([inbox[pl.ds(d * 32 + 6, 8, stride=32), :] for d in range(0, 64, 8)] + [relay[pl.ds(d * 16 + 6, 8, stride=16), :] for d in range(0, 64, 8)], axis=0)
    corners[...] = gathered.T[0:8].astype(jnp.int32)

    def end(chip, carry):
        message(chip).wait_send()
        return carry

    lax.fori_loop(1, 64, end, 0)
    for group in range(8):
        onward(group).wait_send()
    for copy in rims:
        copy.wait()


def exchange_call(counts, owner, offsets, forces, base, velocity):
    shapes = ((2048, 128), F32), ((1024, 128), F32), ((256, 24, 128), F32), ((8, 128), jnp.int32), ((128, 256), F32), ((3, 20, 24, 128), F32)
    return pl.pallas_call(
        exchange_body,
        out_shape=tuple(jax.ShapeDtypeStruct(*s) for s in shapes),
        in_specs=[VM, ANY],
        out_specs=(VM,) * 6,
        scratch_shapes=[pltpu.VMEM((3, 128, 128), F32), pltpu.VMEM((3, 128, 128), F32), pltpu.SemaphoreType.DMA((3,))] + [
            pltpu.VMEM((2048, 128), F32),
            pltpu.VMEM((4, 64, 128), F32),
            pltpu.VMEM((16, 8, 128), F32),
            pltpu.SemaphoreType.REGULAR,
            pltpu.SemaphoreType.DMA((64,)),
            pltpu.SemaphoreType.DMA((64,)),
            pltpu.SemaphoreType.DMA((8,)),
            pltpu.SemaphoreType.DMA((8,)),
            pltpu.SemaphoreType.DMA((8,)),
            pltpu.SemaphoreType.DMA((8,)),
        ],
        compiler_params=pltpu.CompilerParams(vmem_limit_bytes=40 * 2**20, collective_id=1, has_side_effects=True),
        name="exchange",
    )(jnp.concatenate([base, owner[None], jnp.broadcast_to(counts[:, None], (1, 128))], axis=0), jnp.stack([offsets, forces, velocity.reshape(3, 128, 128)]))


def deposit_body(corners_s, boxes, acc):
    def zero(x, carry):
        acc[x] = jnp.zeros((3, 128, 128), F32)
        return carry

    lax.fori_loop(0, 16, zero, 0)

    def add(k, carry):
        for r in range(2):
            x0 = corners_s[r * 3, k]
            z0 = jnp.maximum(corners_s[r * 3 + 2, k] - 3, 0)
            for c in range(3):
                acc[x0, c, pl.ds(z0, 8), :] += boxes[k * 2 + r, c * 8:c * 8 + 8]
        return carry

    lax.fori_loop(0, 128, add, 0, unroll=16)


def deposit_call(corners, boxes):
    return pl.pallas_call(
        deposit_body,
        out_shape=jax.ShapeDtypeStruct((16, 3, 128, 128), F32),
        in_specs=[SM, VM],
        out_specs=VM,
        compiler_params=pltpu.CompilerParams(vmem_limit_bytes=40 * 2**20),
        name="deposit",
    )(corners, boxes)


MESH = pl.DeviceIdType.MESH
SIDES = ((1, 0), (-1, 0), (0, 1), (0, -1), (1, 1), (1, -1), (-1, 1), (-1, -1))


def neighbours():
    gx, gy = lax.axis_index("gx"), lax.axis_index("gy")
    nx, ny = lax.axis_size("gx"), lax.axis_size("gy")
    return [(lax.rem(gx + dx + nx, nx), lax.rem(gy + dy + ny, ny)) for dx, dy in SIDES]


def near(step, size, width):
    return (0, size) if step == 0 else ((size - width, width) if step > 0 else (0, width))


def there(step, size, width):
    return (0, size) if step == 0 else ((-width, width) if step > 0 else (size, width))


def box(ref, xs, ys, x_at, y_at):
    return ref.at[..., pl.ds(xs[0] + x_at, xs[1]), pl.ds(ys[0] + y_at, ys[1]), :]


def inward(lane, v):
    above = jnp.where(lane == 127, 0.0, pltpu.roll(v, 127, 1))
    below = jnp.where(lane == 0, 0.0, pltpu.roll(v, 1, 1))
    return above, below


def project_body(unroll, chunks, corners_s, inbox, relay, acc, ve, new_ref, prs_ref, direct, passed, w_ref, tot, v_ref, pe, src, pa, pb, fold, tables, wxs, planes, depths, cop, ans, line_sem, send, recv, out_sem, in_sem, pass_sem, take_sem):
    here = position()
    peers = neighbours()
    gx, gy = lax.axis_index("gx"), lax.axis_index("gy")
    barrier = pltpu.get_barrier_semaphore()
    fold[...] = jnp.zeros(fold.shape, F32)
    for i in range(1, 16):
        pl.semaphore_signal(barrier, inc=1, device_id=(gx, (gy + i) & 15), device_id_type=MESH)
    for i in range(1, 8):
        pl.semaphore_signal(barrier, inc=1, device_id=((gx + i) & 7, gy), device_id_type=MESH)
    iota8 = lax.broadcasted_iota(jnp.int32, (8, 128), 0).astype(F32) - 3.0
    iota16 = lax.broadcasted_iota(jnp.int32, (16, 128), 0).astype(F32) - 3.0

    def weigh(begin, end):
        held, pitch, shift = (inbox, 32, 0) if begin < 64 else (relay, 16, 64)

        def turn(t, carry):
            for u in range(unroll):
                k = t * unroll + u
                rows = pl.ds(u * 8, 8)
                v = held[pl.ds((k - shift) * pitch, 8), :]
                whole = jnp.floor(v)
                f = v - whole
                for n, v in enumerate((whole, (3.0 - 2.0 * f) * 0.125, (1.0 + 2.0 * f) * 0.125, jnp.sqrt(1.0 + 4.0 * f * (1.0 - f)) * 0.125)):
                    tables[n, rows, :] = v
                for r in range(2):
                    row, p = u * 8 + r * 3, k * 2 + r
                    tabs = [tables.at[n] for n in range(4)]
                    bh, bl = split(plane_of(corners_s[r * 3 + 1, k].astype(F32), row, tabs, wxs.at[u * 2 + r], iota8, iota16))
                    planes[p, :128] = bh
                    planes[p, 128:] = bl
                    depths[p] = weight(iota8, row + 2, tabs)
            return carry

        lax.fori_loop(begin // unroll, end // unroll, turn, 0)

    wide = lax.broadcasted_iota(jnp.int32, (128, 128), 1)
    for c in range(3):
        filled = [False] * 3
        for t in range(2):
            for r in range(8):
                a = acc[8 * t + r, c]
                if r == 0:
                    parts = [(t, a)]
                else:
                    a = pltpu.roll(a, 16 * r, 1)
                    parts = [(t, jnp.where(wide >= 16 * r, a, 0.0)), (t + 1, jnp.where(wide < 16 * r, a, 0.0))]
                for k, v in parts:
                    tot[k] = tot[k] + v if filled[k] else v
                    filled[k] = True
        for k in range(3):
            w_ref[c, 8 * k:8 * k + 8] = tot[k].T.reshape(8, 16, 128)
    weigh(chunks[0], chunks[1])
    pl.semaphore_wait(barrier, 22)
    for i in range(1, 8):
        pl.semaphore_signal(line_sem, inc=1, device_id=((gx + i) & 7, gy), device_id_type=MESH)
    started = []

    def push(source, target, k):
        n = len(started)
        copy = pltpu.make_async_remote_copy(source, target, send.at[n], recv.at[n], device_id=peers[k], device_id_type=MESH)
        copy.start()
        started.append(copy)
        return copy

    first = []
    for k, (dx, dy) in enumerate(SIDES):
        if k == 4:
            pl.semaphore_wait(line_sem, 7)
        xs = (2, 18) if dx == 0 else ((18, 4) if dx > 0 else (0, 4))
        ys = (2, 10) if dy == 0 else ((10, 4) if dy > 0 else (0, 4))
        xd = (0, 18) if dx == 0 else ((0, 4) if dx > 0 else (14, 4))
        yd = (2, 10) if dy == 0 else ((2, 4) if dy > 0 else (8, 4))
        layer = 0 if dy == 0 else (1 if dx == 0 else 2)
        first.append(push(w_ref.at[:, pl.ds(xs[0], xs[1]), pl.ds(ys[0], ys[1]), :],
                          fold.at[layer, :, pl.ds(xd[0], xd[1]), pl.ds(yd[0], yd[1]), :], k))
    weigh(chunks[1], chunks[2])
    for copy in first:
        copy.wait_recv()
    lane = lax.broadcasted_iota(jnp.int32, (8, 128), 1)

    def provide_rows(x, s):
        here_ = pl.ds(8 + s, 8)
        at = pl.ds(3 + s, 8)
        for c in range(3):
            v = ve[c, x + 2, here_, :]
            above, below = inward(lane, v)
            lap = (ve[c, x + 3, here_, :] + ve[c, x + 1, here_, :]) + (ve[c, x + 2, 9 + s:17 + s, :] + ve[c, x + 2, 7 + s:15 + s, :]) + (above + below) - 6.0 * v
            force = w_ref[c, x + 3, at, :] + fold[0, c, x + 1, at, :] + fold[1, c, x + 1, at, :] + fold[2, c, x + 1, at, :]
            pe[c, x + 8, here_, :] = v + time_step * (viscosity * lap + force)

    def provide(x, carry):
        provide_rows(x, -1)
        provide_rows(x, 1)
        return carry

    lax.fori_loop(0, 16, provide, 0, unroll=4)
    provide_rows(-1, 0)
    provide_rows(16, 0)

    def diverge(x, carry):
        above, below = inward(lane, pe[2, x + 8, 8:16, :])
        total = (pe[0, x + 9, 8:16, :] - pe[0, x + 7, 8:16, :]) + (pe[1, x + 8, 9:17, :] - pe[1, x + 8, 7:15, :]) + (above - below)
        src[x + 8, 8:16, :] = total * (0.5 / time_step)
        return carry

    lax.fori_loop(0, 16, diverge, 0, unroll=16)

    third = [push(box(src, near(dx, 16, 7), near(dy, 8, 7), 8, 8),
                  box(src, there(dx, 16, 7), there(dy, 8, 7), 8, 8), k) for k, (dx, dy) in enumerate(SIDES)]
    fourth = []
    for k, (dx, dy) in enumerate(SIDES):
        if k < 4:
            xs = (0, 16) if dx == 0 else ((13, 2) if dx > 0 else (1, 2))
            ys = (0, 8) if dy == 0 else ((5, 2) if dy > 0 else (1, 2))
            xd = (0, 16) if dx == 0 else ((-3, 2) if dx > 0 else (17, 2))
            yd = (0, 8) if dy == 0 else ((-3, 2) if dy > 0 else (9, 2))
        else:
            xs, ys, xd, yd = near(dx, 16, 3), near(dy, 8, 3), there(dx, 16, 3), there(dy, 8, 3)
        fourth.append(push(box(pe, xs, ys, 8, 8), box(pe, xd, yd, 8, 8), k))
    weigh(chunks[2], chunks[3])
    for copy in third:
        copy.wait_recv()

    def relax(old, new, reach, starts, first_sweep):
        scale = -1.0 / 6.0 if first_sweep else 1.0

        def step(x, carry):
            for s in starts:
                here = pl.ds(s, 8)
                v = old[x, here, :] * scale
                above, below = inward(lane, v)
                total = (old[x + 1, here, :] + old[x - 1, here, :]) + (old[x, s + 1:s + 9, :] + old[x, s - 1:s + 7, :])
                new[x, here, :] = (total * scale + (above + below) - src[x, here, :]) * (1.0 / 6.0)
            return carry

        lax.fori_loop(8 - reach, 24 + reach, step, 0, unroll=(16 + 2 * reach) // 2)

    relax(src, pa, 6, (2, 8, 14), True)
    relax(pa, pb, 5, (3, 8, 13), False)
    relax(pb, pa, 4, (4, 12), False)
    for copy in fourth:
        copy.wait_recv()
    v_ref[:, :, 8:16, :] = jnp.zeros((3, 24, 8, 128), F32)
    v_ref[:, 22:24, 0:8, :] = jnp.zeros((3, 2, 8, 128), F32)

    def finish(x, carry):
        for s in (5, 11):
            here = pl.ds(s, 8)
            above, below = inward(lane, pa[x, here, :])
            grad = (pa[x + 1, here, :] - pa[x - 1, here, :], pa[x, s + 1:s + 9, :] - pa[x, s - 1:s + 7, :], above - below)
            for c in range(3):
                v_ref[c, x - 5, pl.ds(s - 5, 8), :] = pe[c, x, here, :] - (0.5 * time_step) * grad[c]
        return carry

    lax.fori_loop(5, 27, finish, 0, unroll=11)
    new_ref[...] = v_ref[:, 3:19, 3:11, :]
    prs_ref[...] = pa[8:24, 8:16, :]


    for c in range(3):
        tiles = [v_ref[c, 8 * k:8 * k + 8].reshape(128, 128).T for k in range(3)]
        for r in range(8):
            if r == 0:
                cop[0, c], cop[8, c] = tiles[0], tiles[1]
            else:
                ro = [pltpu.roll(x, 128 - 16 * r, 1) for x in tiles]
                for t in range(2):
                    cop[8 * t + r, c] = jnp.where(wide < 128 - 16 * r, ro[t], ro[t + 1])

    def message(chip):
        rows = pl.ds(pl.multiple_of(chip * 16, 16), 12)
        return pltpu.make_async_remote_copy(ans.at[rows], direct.at[rows], out_sem.at[chip], in_sem.at[chip], device_id=shifted(chip, here, -1), device_id_type=MESH)

    def onward(group):
        return pltpu.make_async_remote_copy(
            direct.reshape(64, 16, 128).at[pl.ds(group * 16, 16), pl.ds(6, 6)],
            passed.reshape(64, 8, 128).at[pl.ds(group * 16, 16), pl.ds(0, 6)],
            pass_sem.at[group], take_sem.at[group], device_id=sibling(here), device_id_type=MESH)

    def work(chips):
        for chip in chips:
            for kc in range(2):
                k = chip + 64 * kc
                for r in range(2):
                    p = k * 2 + r
                    x0 = corners_s[r * 3, k]
                    z0 = jnp.maximum(corners_s[r * 3 + 2, k] - 3, 0)
                    ah, al = split(jnp.concatenate([cop[x0, c, pl.ds(z0, 8), :] for c in range(3)], axis=0))
                    both = jnp.concatenate([ah, al], 0)
                    o = jnp.dot(jnp.concatenate([both, both], 1), planes[p], preferred_element_type=F32)
                    o = o[:24] + o[24:]
                    wz = depths[p]
                    for c in range(3):
                        ans[pl.ds(chip * 16 + kc * 6 + r * 3 + c, 1), :] = jnp.sum(o[8 * c:8 * c + 8] * wz, axis=0, keepdims=True)

    work(list(range(8)))
    for chip in range(1, 8):
        message(chip).start()

    def turn(t, carry):
        chips = [t * 8 + u for u in range(8)]
        work(chips)
        for chip in chips:
            message(chip).start()
        return carry

    lax.fori_loop(1, 8, turn, 0)
    direct[0:16] = ans[0:16]
    for group in range(4):
        for chip in range(max(group * 16, 1), group * 16 + 16):
            message(chip).wait_recv()
        onward(group).start()
    for group in range(4):
        onward(group).wait_recv()

    def end(chip, carry):
        message(chip).wait_send()
        return carry

    lax.fori_loop(1, 64, end, 0)
    for group in range(4):
        onward(group).wait_send()
    for copy in started:
        copy.wait_send()


def project_call(corners, inbox, relay, spread, moving, unroll=8, chunks=(0, 0, 64, 128)):
    shapes = (3, 16, 8, 128), (16, 8, 128), (1024, 128), (512, 128)
    return pl.pallas_call(
        functools.partial(project_body, unroll, chunks),
        out_shape=tuple(jax.ShapeDtypeStruct(s, F32) for s in shapes),
        in_specs=[SM, VM, VM, VM, VM],
        out_specs=(VM,) * 4,
        scratch_shapes=[
            pltpu.VMEM((3, 24, 16, 128), F32),
            pltpu.VMEM((3, 128, 128), F32),
            pltpu.VMEM((3, 24, 16, 128), F32),
            pltpu.VMEM((3, 32, 24, 128), F32),
            pltpu.VMEM((32, 24, 128), F32),
            pltpu.VMEM((32, 24, 128), F32),
            pltpu.VMEM((32, 24, 128), F32),
            pltpu.VMEM((3, 3, 18, 16, 128), F32),
            pltpu.VMEM((4, 8 * unroll, 128), F32),
            pltpu.VMEM((2 * unroll, 8, 128), F32),
            pltpu.VMEM((256, 256, 128), BF),
            pltpu.VMEM((256, 8, 128), F32),
            pltpu.VMEM((16, 3, 128, 128), F32),
            pltpu.VMEM((1024, 128), F32),
            pltpu.SemaphoreType.REGULAR,
            pltpu.SemaphoreType.DMA((32,)),
            pltpu.SemaphoreType.DMA((32,)),
            pltpu.SemaphoreType.DMA((64,)),
            pltpu.SemaphoreType.DMA((64,)),
            pltpu.SemaphoreType.DMA((4,)),
            pltpu.SemaphoreType.DMA((4,)),
        ],
        compiler_params=pltpu.CompilerParams(vmem_limit_bytes=40 * 2**20, collective_id=0, has_side_effects=True),
        name="project",
    )(corners, inbox, relay, spread, moving)


def finish_body(back, direct, passed, new_ref, prs_ref, out_new, out_prs, out, sems):
    copies = [pltpu.make_async_copy(new_ref, out_new, sems.at[0]), pltpu.make_async_copy(prs_ref, out_prs, sems.at[1])]
    for copy in copies:
        copy.start()
    pick = back[...].astype(BF)
    for c in range(3):
        data = jnp.concatenate([box[pl.ds(r * 3 + c, 64, stride=pitch), :] for r in range(2) for box, pitch in ((direct, 16), (passed, 8))], axis=0)
        got = jnp.dot(pick, jnp.concatenate(split3(data), axis=1), preferred_element_type=F32)
        out[c] = got[:, :128] + (got[:, 128:256] + got[:, 256:])
    for copy in copies:
        copy.wait()


def finish_call(back, direct, passed, new, pressure):
    shapes = (3, 16, 8, 128), (16, 8, 128), (3, 128, 128)
    return pl.pallas_call(
        finish_body,
        out_shape=tuple(jax.ShapeDtypeStruct(s, F32) for s in shapes),
        in_specs=[VM] * 5,
        out_specs=(ANY, ANY, VM),
        scratch_shapes=[pltpu.SemaphoreType.DMA((2,))],
        compiler_params=pltpu.CompilerParams(vmem_limit_bytes=32 * 2**20),
        name="finish",
    )(back, direct, passed, new, pressure)


def shards(velocity, offsets, forces, owner, base, counts):
    inbox, relay, boxes, corners, back, moving = exchange_call(counts, owner, offsets, forces, base, velocity)
    spread = deposit_call(corners, boxes)
    new_velocity, pressure, direct, passed = project_call(corners, inbox, relay, spread, moving)
    return finish_call(back, direct, passed, new_velocity, pressure)


def solution(mesh):
    return jax.shard_map(
        shards,
        mesh=mesh,
        in_specs=(
            P(None, "gx", "gy", None),
            P(None, ("gx", "gy"), None),
            P(None, ("gx", "gy"), None),
            P(("gx", "gy")),
            P(None, ("gx", "gy")),
            P(("gx", "gy")),
        ),
        out_specs=(P(None, "gx", "gy", None), P("gx", "gy", None), P(None, ("gx", "gy"), None)),
        check_vma=False,
    )
```
